32 devices in a mesh: dp: 4 (over z), seq: 2 (over core), tensor: 4 (over y, x).
Axes of the slice: x: 2, y: 2, z: 4, core: 2. Of those that a mesh axis runs over, the one named last changes fastest.
Arguments:
- source: bfloat16 [16, 1024, 1024], P('dp', ('seq', 'tensor')), may hold values from -61 to 61
- target: bfloat16 [16, 1024, 1024], P('dp', ('seq', 'tensor')), may hold values from -61 to 61
- out_grad: bfloat16 [16, 1024, 1024], P('dp', ('seq', 'tensor')), may hold values from -6 to 6
- source_segments: int32 [16, 1024], P('dp'), may hold values from 0 to 8, as said below
- target_segments: int32 [16, 1024], P('dp'), may hold values from 0 to 8, as said below
- enc_gain: float32 [3, 1024], replicated, may hold values from 0.5 to 1.5
- enc_shift: float32 [3, 1024], replicated, may hold values from -1.2 to 1.2
- enc_qkv: bfloat16 [1024, 3, 1024], P(None, None, 'tensor'), may hold values from -0.1875 to 0.1875
- enc_proj: bfloat16 [1024, 1024], P('tensor'), may hold values from -0.5 to 0.5
- enc_up: bfloat16 [1024, 4096], P(None, 'tensor'), may hold values from -0.1875 to 0.1875
- enc_down: bfloat16 [4096, 1024], P('tensor'), may hold values from -0.09375 to 0.09375
- dec_gain: float32 [4, 1024], replicated, may hold values from 0.5 to 1.5
- dec_shift: float32 [4, 1024], replicated, may hold values from -1.2 to 1.2
- dec_self_qkv: bfloat16 [1024, 3, 1024], P(None, None, 'tensor'), may hold values from -0.1875 to 0.1875
- dec_self_proj: bfloat16 [1024, 1024], P('tensor'), may hold values from -0.5 to 0.5
- dec_cross_q: bfloat16 [1024, 1024], P(None, 'tensor'), may hold values from -0.1875 to 0.1875
- dec_cross_kv: bfloat16 [1024, 2, 1024], P(None, None, 'tensor'), may hold values from -0.1875 to 0.1875
- dec_cross_proj: bfloat16 [1024, 1024], P('tensor'), may hold values from -0.5 to 0.5
- dec_up: bfloat16 [1024, 4096], P(None, 'tensor'), may hold values from -0.1875 to 0.1875
- dec_down: bfloat16 [4096, 1024], P('tensor'), may hold values from -0.09375 to 0.09375
Outputs:
- decoded: bfloat16 [16, 1024, 1024], P('dp', ('seq', 'tensor'))
- source_grad: float32 [16, 1024, 1024], P('dp', ('seq', 'tensor'))
- target_grad: float32 [16, 1024, 1024], P('dp', ('seq', 'tensor'))
- enc_gain_grad: float32 [3, 1024], P(None, 'seq')
- enc_shift_grad: float32 [3, 1024], P(None, 'seq')
- enc_qkv_grad: float32 [1024, 3, 1024], P('seq', None, 'tensor')
- enc_proj_grad: float32 [1024, 1024], P('tensor', 'seq')
- enc_up_grad: float32 [1024, 4096], P('seq', 'tensor')
- enc_down_grad: float32 [4096, 1024], P('tensor', 'seq')
- dec_gain_grad: float32 [4, 1024], P(None, 'seq')
- dec_shift_grad: float32 [4, 1024], P(None, 'seq')
- dec_self_qkv_grad: float32 [1024, 3, 1024], P('seq', None, 'tensor')
- dec_self_proj_grad: float32 [1024, 1024], P('tensor', 'seq')
- dec_cross_q_grad: float32 [1024, 1024], P('seq', 'tensor')
- dec_cross_kv_grad: float32 [1024, 2, 1024], P('seq', None, 'tensor')
- dec_cross_proj_grad: float32 [1024, 1024], P('tensor', 'seq')
- dec_up_grad: float32 [1024, 4096], P('seq', 'tensor')
- dec_down_grad: float32 [4096, 1024], P('tensor', 'seq')
The draws below stay inside these ranges and needn't reach their ends.
Inputs may be any that keep to these rules, and one draw needn't show every extreme that they name: `source_segments`: 0 marks padding and k the k-th sentence pair of a slot; a slot holds either one pair (id 1) or eight pairs, pair k in rows (k - 1) * 128 to k * 128 - 1; every slot has a padding source row; of each 4 slots of one dp index, one holds a single pair whose source and target rows run past 7 / 8 of the slot and another holds eight pairs. `target_segments`: same slot layout as the source of the slot; every id in a slot's target occurs in its source.
All inputs are finite; a program needn't handle non-finite values.
Results may differ from the reference program's by a relative error of at most 0.038.
Values may be sent and summed in bfloat16 or wider, within the bound.
No kernel may reach another device: no remote copies, remote signals or barrier semaphores. Data moves between devices by JAX's collectives and lax.ppermute only.
A program may use at most 576 MiB of HBM per device.

```python
import jax
import jax.numpy as jnp
from jax import lax

D = 1024
HEADS = 16
FF = 4096
HEAD_DIM = 64
SLOT = 1024
SLOTS_DEV = 4
SLOTS = 16
TP_GROUPS = 4


def pair_segments(key):
    subkeys = jax.random.split(jax.random.fold_in(key, 7), 8)
    pair_rows = SLOT // 8
    groups = SLOTS // SLOTS_DEV
    slot_index = jnp.arange(SLOTS, dtype=jnp.int32) % SLOTS_DEV
    forced = jnp.repeat(jax.random.randint(subkeys[0], (groups,), 0, SLOTS_DEV), SLOTS_DEV)
    spanning = slot_index == forced
    packing = slot_index == (forced + 1) % SLOTS_DEV
    chosen = jax.random.randint(subkeys[1], (SLOTS,), 0, 2) == 1
    packed = packing | chosen & jnp.logical_not(spanning)
    long_source = jax.random.randint(subkeys[2], (SLOTS,), SLOT - pair_rows + 1, SLOT)
    long_target = jax.random.randint(subkeys[3], (SLOTS,), SLOT - pair_rows + 1, SLOT + 1)
    free_source = jax.random.randint(subkeys[4], (SLOTS,), SLOT // 4, SLOT)
    free_target = jax.random.randint(subkeys[5], (SLOTS,), SLOT // 4, SLOT + 1)
    single_source = jnp.where(spanning, long_source, free_source)
    single_target = jnp.where(spanning, long_target, free_target)
    pair_source = jax.random.randint(subkeys[6], (SLOTS, 8), 1, pair_rows)
    pair_target = jax.random.randint(subkeys[7], (SLOTS, 8), 1, pair_rows + 1)
    positions = jnp.arange(SLOT, dtype=jnp.int32)
    pair_of = positions // pair_rows
    within = positions % pair_rows

    def segment_ids(single, pair_lengths):
        packed_ids = jnp.where(within[None, :] < pair_lengths[:, pair_of], pair_of[None, :] + 1, 0)
        single_ids = jnp.where(positions[None, :] < single[:, None], 1, 0)
        return jnp.where(packed[:, None], packed_ids, single_ids).astype(jnp.int32)
    return (segment_ids(single_source, pair_source), segment_ids(single_target, pair_target))


def draw_source_segments(key, part):
    return pair_segments(key)[0]


def draw_target_segments(key, part):
    return pair_segments(key)[1]


def draw_activity(key, spread):
    subkeys = jax.random.split(key, 3)
    base_draw = jax.random.truncated_normal(subkeys[0], -4.0, 4.0, (SLOTS, SLOT, D), jnp.float32)
    column = jnp.exp(jax.random.uniform(subkeys[1], (D,), jnp.float32, -spread, spread))
    row_scale = jnp.exp(jax.random.uniform(subkeys[2], (SLOTS, SLOT, 1), jnp.float32, -spread, spread))
    return base_draw * column * row_scale


def draw_source(key, part):
    key = jax.random.fold_in(key, 1)
    return draw_activity(key, 1.15).astype(jnp.bfloat16)


def draw_target(key, part):
    key = jax.random.fold_in(key, 2)
    return draw_activity(key, 1.15).astype(jnp.bfloat16)


def block_scale(rng, extent, cuts, least, high):
    factor_of, own = 1.0, jax.random.fold_in(rng, 6)
    for dim, shards_of in cuts:
        steps = jnp.exp(jax.random.uniform(jax.random.fold_in(own, dim), (shards_of,), jnp.float32, least / len(cuts), high / len(cuts)))
        factor_of = factor_of * jnp.repeat(steps, extent[dim] // shards_of).reshape([-1 if axis == dim else 1 for axis in range(len(extent))])
    return factor_of


def normal_values(key, shape, scale, limit, cuts=(), held_as=jnp.bfloat16):
    level = block_scale(key, shape, cuts, -0.22, 0.18) if cuts else 1.0
    array = jax.random.normal(key, shape, jnp.float32) * scale * level
    return jnp.minimum(jnp.maximum(array, -limit), limit).astype(held_as)


def setup_inputs(seed: int = 0) -> dict:
    key_list = jax.random.split(jax.random.key(seed), 21)
    source = draw_source(jax.random.fold_in(key_list[20], 71), 0)
    target = draw_target(jax.random.fold_in(key_list[20], 71), 0)
    out_grad = normal_values(key_list[2], (SLOTS, SLOT, D), 1.0, 6.0, ((0, 4), (1, 8)))
    source_segments = draw_source_segments(jax.random.fold_in(key_list[20], 71), 0)
    target_segments = draw_target_segments(jax.random.fold_in(key_list[20], 71), 0)
    enc_gain = jnp.clip(1.0 + 0.1 * jax.random.normal(key_list[5], (3, D), jnp.float32), 0.5, 1.5)
    enc_shift = normal_values(key_list[6], (3, D), 0.2, 1.2, (), jnp.float32)
    enc_qkv = normal_values(key_list[7], (D, 3, D), D ** -0.5, 0.1875, ((2, 4),))
    enc_proj = normal_values(key_list[8], (D, D), (D // 8) ** -0.5, 0.5, ((0, 4),))
    enc_up = normal_values(key_list[9], (D, FF), D ** -0.5, 0.1875, ((1, 4),))
    enc_down = normal_values(key_list[10], (FF, D), FF ** -0.5, 0.09375, ((0, 4),))
    dec_gain = jnp.clip(1.0 + 0.1 * jax.random.normal(key_list[11], (4, D), jnp.float32), 0.5, 1.5)
    dec_shift = normal_values(key_list[12], (4, D), 0.2, 1.2, (), jnp.float32)
    dec_self_qkv = normal_values(key_list[13], (D, 3, D), D ** -0.5, 0.1875, ((2, 4),))
    dec_self_proj = normal_values(key_list[14], (D, D), (D // 8) ** -0.5, 0.5, ((0, 4),))
    dec_cross_q = normal_values(key_list[15], (D, D), D ** -0.5, 0.1875, ((1, 4),))
    dec_cross_kv = normal_values(key_list[16], (D, 2, D), D ** -0.5, 0.1875, ((2, 4),))
    dec_cross_proj = normal_values(key_list[17], (D, D), (D // 8) ** -0.5, 0.5, ((0, 4),))
    dec_up = normal_values(key_list[18], (D, FF), D ** -0.5, 0.1875, ((1, 4),))
    dec_down = normal_values(key_list[19], (FF, D), FF ** -0.5, 0.09375, ((0, 4),))
    return {"source": source, "target": target, "out_grad": out_grad, "source_segments": source_segments, "target_segments": target_segments, "enc_gain": enc_gain, "enc_shift": enc_shift, "enc_qkv": enc_qkv, "enc_proj": enc_proj, "enc_up": enc_up, "enc_down": enc_down, "dec_gain": dec_gain, "dec_shift": dec_shift, "dec_self_qkv": dec_self_qkv, "dec_self_proj": dec_self_proj, "dec_cross_q": dec_cross_q, "dec_cross_kv": dec_cross_kv, "dec_cross_proj": dec_cross_proj, "dec_up": dec_up, "dec_down": dec_down}


EPS = 1e-05
NEG = -1e+30
PRECISE = lax.Precision.HIGHEST

@jax.custom_vjp
def low(v):
    return lax.optimization_barrier(v.astype(jnp.bfloat16)).astype(jnp.float32)

@jax.custom_vjp
def low_back(v):
    return v

def low_keep(v):
    return (low(v), None)

def low_pass(kept, grad):
    return (grad,)

def back_keep(v):
    return (v, None)

def back_low(kept, grad):
    return (low(grad),)
low.defvjp(low_keep, low_pass)
low_back.defvjp(back_keep, back_low)

def layer_norm(inputs, norm_gain, norm_shift):
    row_mean = lax.optimization_barrier(jnp.mean(inputs, -1, keepdims=True))
    centred = inputs - row_mean
    spread = lax.optimization_barrier(jnp.mean(centred * centred, -1, keepdims=True))
    return centred * lax.rsqrt(spread + EPS) * norm_gain + norm_shift

def grouped_out(row_block, weight):
    inner_width = weight.shape[0] // TP_GROUPS
    parts = row_block.reshape(row_block.shape[0], row_block.shape[1], TP_GROUPS, inner_width)
    grouped_weight = weight.reshape(TP_GROUPS, inner_width, weight.shape[1])
    partial_sums = jnp.einsum('srga,gab->srgb', parts, grouped_weight, precision=PRECISE)
    return lax.optimization_barrier(jnp.sum(low(partial_sums), 2))

def grouped_in(normed, weight):
    blocks = weight.shape[1]
    inner_width = weight.shape[2] // TP_GROUPS
    copies = low_back(jnp.broadcast_to(normed[:, :, None, :], (normed.shape[0], normed.shape[1], TP_GROUPS, normed.shape[2])))
    grouped_weight = weight.reshape(weight.shape[0], blocks, TP_GROUPS, inner_width)
    result = jnp.einsum('srga,amgb->srmgb', copies, grouped_weight, precision=PRECISE)
    return result.reshape(normed.shape[0], normed.shape[1], blocks * weight.shape[2])

def attend_slot(queries, key_rows, value_rows, allowed):
    query_heads = queries.reshape(queries.shape[0], HEADS, HEAD_DIM)
    key_heads = key_rows.reshape(key_rows.shape[0], HEADS, HEAD_DIM)
    value_heads = value_rows.reshape(value_rows.shape[0], HEADS, HEAD_DIM)
    raw_scores = low_back(jnp.einsum('qhd,khd->hqk', query_heads, key_heads, precision=PRECISE) * HEAD_DIM ** (-0.5))
    raw_scores = jnp.where(allowed[None], raw_scores, NEG)
    row_max = lax.optimization_barrier(jnp.max(raw_scores, -1, keepdims=True))
    weights = jnp.exp(raw_scores - row_max)
    probs_low = low(weights / lax.optimization_barrier(jnp.sum(weights, -1, keepdims=True)))
    mixed_rows = jnp.einsum('hqk,khd->qhd', probs_low, value_heads, precision=PRECISE)
    return mixed_rows.reshape(queries.shape[0], D)

def attention(queries, key_rows, value_rows, allowed):
    slot_step = jax.checkpoint(attend_slot)
    mixed_rows = lax.map(lambda operands: slot_step(operands[0], operands[1], operands[2], operands[3]), (queries, key_rows, value_rows, allowed))
    return low(low_back(mixed_rows))

def self_attention(normed, weight_qkv, allowed):
    qkv_rows = low(low_back(grouped_in(normed, weight_qkv)))
    return attention(qkv_rows[:, :, :D], qkv_rows[:, :, D:2 * D], qkv_rows[:, :, 2 * D:], allowed)

def feed_forward(normed, weight_up, weight_down):
    inner = low_back(grouped_in(normed, weight_up.reshape(D, 1, FF)))
    return low_back(grouped_out(low(jax.nn.gelu(inner, approximate=False)), weight_down))

def forward(source, target, enc_gain, enc_shift, enc_qkv, enc_proj, enc_up, enc_down, dec_gain, dec_shift, dec_self_qkv, dec_self_proj, dec_cross_q, dec_cross_kv, dec_cross_proj, dec_up, dec_down, mask_set):
    enc_mask, self_mask, cross_mask = mask_set
    normed = low(layer_norm(source, enc_gain[0], enc_shift[0]))
    hidden = source + low_back(grouped_out(self_attention(normed, enc_qkv, enc_mask), enc_proj))
    normed = low(layer_norm(hidden, enc_gain[1], enc_shift[1]))
    encoded = hidden + feed_forward(normed, enc_up, enc_down)
    memory = low(layer_norm(encoded, enc_gain[2], enc_shift[2]))
    memory_pairs = low(low_back(grouped_in(memory, dec_cross_kv)))
    normed = low(layer_norm(target, dec_gain[0], dec_shift[0]))
    after_self = target + low_back(grouped_out(self_attention(normed, dec_self_qkv, self_mask), dec_self_proj))
    normed = low(layer_norm(after_self, dec_gain[1], dec_shift[1]))
    cross_query = low(low_back(grouped_in(normed, dec_cross_q.reshape(D, 1, D))))
    mixed_cross = attention(cross_query, memory_pairs[:, :, :D], memory_pairs[:, :, D:], cross_mask)
    after_cross = after_self + low_back(grouped_out(mixed_cross, dec_cross_proj))
    normed = low(layer_norm(after_cross, dec_gain[2], dec_shift[2]))
    final_rows = after_cross + feed_forward(normed, dec_up, dec_down)
    return layer_norm(final_rows, dec_gain[3], dec_shift[3])

def reference(source, target, out_grad, source_segments, target_segments, enc_gain, enc_shift, enc_qkv, enc_proj, enc_up, enc_down, dec_gain, dec_shift, dec_self_qkv, dec_self_proj, dec_cross_q, dec_cross_kv, dec_cross_proj, dec_up, dec_down):
    positions = jnp.arange(SLOT, dtype=jnp.int32)
    enc_mask = source_segments[:, :, None] == source_segments[:, None, :]
    self_mask = (target_segments[:, :, None] == target_segments[:, None, :]) & (positions[None, None, :] <= positions[None, :, None])
    cross_mask = target_segments[:, :, None] == source_segments[:, None, :]
    initials = (source, target, enc_gain, enc_shift, enc_qkv, enc_proj, enc_up, enc_down, dec_gain, dec_shift, dec_self_qkv, dec_self_proj, dec_cross_q, dec_cross_kv, dec_cross_proj, dec_up, dec_down)
    floats = tuple((argument.astype(jnp.float32) for argument in initials))
    batch = 4
    count = SLOTS // batch

    def block_step(operands, weights):
        return forward(operands[0], operands[1], *weights, (operands[2], operands[3], operands[4]))
    checked = jax.checkpoint(block_step)

    def wrapped(source_rows, target_rows, *weights):
        stacked = (source_rows.reshape(count, batch, SLOT, D), target_rows.reshape(count, batch, SLOT, D), enc_mask.reshape(count, batch, SLOT, SLOT), self_mask.reshape(count, batch, SLOT, SLOT), cross_mask.reshape(count, batch, SLOT, SLOT))
        results = lax.map(lambda operands: checked(operands, weights), stacked)
        return results.reshape(SLOTS, SLOT, D)
    decoded, pullback = jax.vjp(wrapped, *floats)
    gradients = pullback(out_grad.astype(jnp.float32))
    return (decoded.astype(jnp.bfloat16), gradients[0], gradients[1], gradients[2], gradients[3], gradients[4], gradients[5], gradients[6], gradients[7], gradients[8], gradients[9], gradients[10], gradients[11], gradients[12], gradients[13], gradients[14], gradients[15], gradients[16])
```

```python
import functools

import jax
import jax.numpy as jnp
from jax import lax
from jax.experimental import pallas as pl
from jax.experimental.pallas import tpu as pltpu
from jax.sharding import PartitionSpec as P

HEAD_DIM = 64
LANES = 128
IDS = 9
EPS = 1e-05
NEG = -1e30
SCALE = HEAD_DIM ** (-0.5)
F32 = jnp.float32
BF16 = jnp.bfloat16
NT = (((1,), (1,)), ((), ()))
NN = (((1,), (0,)), ((), ()))
TN = (((0,), (0,)), ((), ()))


def mxu(left, right, dims):
    return lax.dot_general(left, right, dims, preferred_element_type=F32)


def layer_norm(inputs, norm_gain, norm_shift):
    row_mean = jnp.mean(inputs, -1, keepdims=True)
    centred = inputs - row_mean
    spread = jnp.mean(centred * centred, -1, keepdims=True)
    return centred * lax.rsqrt(spread + EPS) * norm_gain + norm_shift


def exact_gelu(inputs):
    return jax.nn.gelu(inputs, approximate=False)


def norm_back(inputs, norm_gain, norm_shift, cotangent):
    _, pullback = jax.vjp(layer_norm, inputs, norm_gain, norm_shift)
    return pullback(cotangent)


def project(rows, weight):
    return mxu(rows, weight, NN)


def back_project(grad, weight):
    return mxu(grad, weight, NT)


def weight_grad(rows, grad):
    return mxu(rows, grad, TN).astype(BF16)


def attend_kernel(causal, first_ref, q_ref, k_ref, v_ref, qa_ref, ka_ref, o_ref, lse_ref):
    rows = q_ref.shape[0]
    keys = k_ref.shape[0]
    block = min(rows, 256)
    low_half = lax.broadcasted_iota(jnp.int32, (1, LANES), 1) < HEAD_DIM
    key_block = k_ref[...]
    key_mark = ka_ref[...]
    values = v_ref[...]
    for start in range(0, rows, block):
        query = q_ref[pl.ds(start, block), :] * BF16(SCALE)
        query_mark = qa_ref[pl.ds(start, block), :]
        halves = []
        lses = []
        for head in range(2):
            keep = low_half if head == 0 else jnp.logical_not(low_half)
            scores = mxu(
                jnp.where(keep, query, query_mark), jnp.where(keep, key_block, key_mark), NT
            )
            if causal:
                place = (
                    first_ref[0] + start + lax.broadcasted_iota(jnp.int32, (block, keys), 0)
                )
                scores = jnp.where(
                    lax.broadcasted_iota(jnp.int32, (block, keys), 1) <= place, scores, NEG
                )
            top = jnp.max(scores, -1, keepdims=True)
            weights = jnp.exp(scores - top)
            total = jnp.sum(weights, -1, keepdims=True)
            mixed = mxu(weights.astype(BF16), values, NN)
            halves.append(mixed / total)
            lses.append(top + jnp.log(total))
        o_ref[pl.ds(start, block), :] = jnp.where(low_half, halves[0], halves[1]).astype(BF16)
        both = jnp.where(low_half, lses[0], lses[1])
        turned = both.T
        lse_ref[0, 0:1, pl.ds(start, block)] = turned[0:1]
        lse_ref[0, 1:2, pl.ds(start, block)] = turned[HEAD_DIM : HEAD_DIM + 1]


def attend(queries, keys, values, query_mark, key_mark, first_row, causal):
    rows, width = queries.shape
    key_rows = keys.shape[0]
    pairs = width // LANES
    return pl.pallas_call(
        functools.partial(attend_kernel, causal),
        grid_spec=pltpu.PrefetchScalarGridSpec(
            num_scalar_prefetch=1,
            grid=(pairs,),
            in_specs=[
                pl.BlockSpec((rows, LANES), lambda p, first: (0, p)),
                pl.BlockSpec((key_rows, LANES), lambda p, first: (0, p)),
                pl.BlockSpec((key_rows, LANES), lambda p, first: (0, p)),
                pl.BlockSpec((rows, LANES), lambda p, first: (0, 0)),
                pl.BlockSpec((key_rows, LANES), lambda p, first: (0, 0)),
            ],
            out_specs=[
                pl.BlockSpec((rows, LANES), lambda p, first: (0, p)),
                pl.BlockSpec((1, 2, rows), lambda p, first: (p, 0, 0)),
            ],
        ),
        out_shape=[
            jax.ShapeDtypeStruct((rows, width), BF16),
            jax.ShapeDtypeStruct((pairs, 2, rows), F32),
        ],
        compiler_params=pltpu.CompilerParams(vmem_limit_bytes=40 << 20),
        cost_estimate=pl.CostEstimate(
            flops=4 * rows * key_rows * width * 2,
            bytes_accessed=4 * rows * width + 4 * key_rows * width,
            transcendentals=rows * key_rows * width // HEAD_DIM,
        ),
        name="attend",
    )(first_row, queries, keys, values, query_mark, key_mark)


def attend_back_kernel(
    causal,
    first_ref,
    q_ref,
    k_ref,
    v_ref,
    qa_ref,
    ka_ref,
    lse_ref,
    o_ref,
    do_ref,
    dq_ref,
    dk_ref,
    dv_ref,
    dk_acc,
    dv_acc,
):
    rows = q_ref.shape[0]
    keys = k_ref.shape[0]
    block = min(rows, 256)
    low_half = lax.broadcasted_iota(jnp.int32, (1, LANES), 1) < HEAD_DIM
    key_block = k_ref[...]
    key_mark = ka_ref[...]
    values = v_ref[...]
    zero = jnp.zeros((), BF16)
    dk_acc[...] = jnp.zeros_like(dk_acc)
    dv_acc[...] = jnp.zeros_like(dv_acc)
    for start in range(0, rows, block):
        span = pl.ds(start, block)
        query = q_ref[span, :] * BF16(SCALE)
        query_mark = qa_ref[span, :]
        d_out = do_ref[span, :]
        inner = (d_out.astype(F32) * o_ref[span, :].astype(F32)).T
        d_query = None
        for head in range(2):
            keep = low_half if head == 0 else jnp.logical_not(low_half)
            delta = jnp.sum(
                inner[head * HEAD_DIM : (head + 1) * HEAD_DIM], axis=0, keepdims=True
            )
            scores = mxu(
                jnp.where(keep, key_block, key_mark), jnp.where(keep, query, query_mark), NT
            )
            if causal:
                place = (
                    first_ref[0] + start + lax.broadcasted_iota(jnp.int32, (keys, block), 1)
                )
                scores = jnp.where(
                    lax.broadcasted_iota(jnp.int32, (keys, block), 0) <= place, scores, NEG
                )
            probs = jnp.exp(scores - lse_ref[0, head : head + 1, span])
            own_out = jnp.where(keep, d_out, zero)
            d_probs = mxu(values, own_out, NT)
            d_scores = (probs * (d_probs - delta)).astype(BF16)
            dv_acc[...] += mxu(probs.astype(BF16), own_out, NN)
            dk_acc[...] += mxu(d_scores, jnp.where(keep, query, zero), NN)
            term = mxu(jnp.where(keep, key_block, zero), d_scores, TN)
            d_query = term if d_query is None else d_query + term
        dq_ref[span, :] = (d_query * SCALE).T.astype(BF16)
    dk_ref[...] = dk_acc[...].astype(BF16)
    dv_ref[...] = dv_acc[...].astype(BF16)


def attend_back(
    queries, keys, values, query_mark, key_mark, first_row, causal, log_total, mixed, d_mixed
):
    rows, width = queries.shape
    key_rows = keys.shape[0]
    pairs = width // LANES
    row_spec = pl.BlockSpec((rows, LANES), lambda p, first: (0, p))
    key_spec = pl.BlockSpec((key_rows, LANES), lambda p, first: (0, p))
    return pl.pallas_call(
        functools.partial(attend_back_kernel, causal),
        grid_spec=pltpu.PrefetchScalarGridSpec(
            num_scalar_prefetch=1,
            grid=(pairs,),
            in_specs=[
                row_spec,
                key_spec,
                key_spec,
                pl.BlockSpec((rows, LANES), lambda p, first: (0, 0)),
                pl.BlockSpec((key_rows, LANES), lambda p, first: (0, 0)),
                pl.BlockSpec((1, 2, rows), lambda p, first: (p, 0, 0)),
                row_spec,
                row_spec,
            ],
            out_specs=[row_spec, key_spec, key_spec],
            scratch_shapes=[
                pltpu.VMEM((key_rows, LANES), F32),
                pltpu.VMEM((key_rows, LANES), F32),
            ],
        ),
        out_shape=[
            jax.ShapeDtypeStruct((rows, width), BF16),
            jax.ShapeDtypeStruct((key_rows, width), BF16),
            jax.ShapeDtypeStruct((key_rows, width), BF16),
        ],
        compiler_params=pltpu.CompilerParams(vmem_limit_bytes=40 << 20),
        cost_estimate=pl.CostEstimate(
            flops=10 * rows * key_rows * width * 2,
            bytes_accessed=8 * rows * width + 8 * key_rows * width,
            transcendentals=rows * key_rows * width // HEAD_DIM,
        ),
        name="attend_back",
    )(first_row, queries, keys, values, query_mark, key_mark, log_total, mixed, d_mixed)


class Layout:
    def __init__(self, slots):
        self.tensor = lax.axis_size("tensor")
        self.seq = lax.axis_size("seq")
        self.slots = slots
        self.spread = self.tensor // slots
        self.place = lax.axis_index("tensor")
        self.half = lax.axis_index("seq")
        self.row_groups = [
            [j * slots + u for u in range(slots)] for j in range(self.spread)
        ]
        self.slot_groups = [
            [j * slots + u for j in range(self.spread)] for u in range(slots)
        ]

    def to_slots(self, block):
        rows = lax.all_to_all(
            block, "tensor", 0, 1, axis_index_groups=self.row_groups, tiled=True
        )
        return rows.reshape(-1, block.shape[2])

    def from_slots(self, rows):
        block = rows.reshape(1, rows.shape[0], rows.shape[1])
        return lax.all_to_all(
            block, "tensor", 1, 0, axis_index_groups=self.row_groups, tiled=True
        )

    def gather_keys(self, rows):
        if self.spread > 1:
            rows = lax.all_gather(
                rows, "tensor", axis=0, axis_index_groups=self.slot_groups, tiled=True
            )
        return lax.all_gather(rows, "seq", axis=0, tiled=True)

    def scatter_keys(self, rows):
        rows = lax.psum_scatter(rows, "seq", scatter_dimension=0, tiled=True)
        if self.spread > 1:
            rows = lax.psum_scatter(
                rows,
                "tensor",
                scatter_dimension=0,
                axis_index_groups=self.slot_groups,
                tiled=True,
            )
        return rows

    def gather_weight(self, shard):
        part = shard.shape[0] // self.seq
        own = lax.dynamic_slice_in_dim(shard, self.half * part, part, 0)
        return lax.all_gather(own, ("tensor", "seq"), axis=0, tiled=True)

    def gather_columns(self, shard):
        depth, blocks, own = shard.shape
        whole = self.gather_weight(shard.reshape(depth, blocks * own))
        whole = whole.reshape(self.tensor, depth, blocks, own)
        return jnp.transpose(whole, (1, 2, 0, 3)).reshape(depth, blocks * self.tensor * own)

    def reduce_rows(self, gradient):
        rows, width = gradient.shape
        parts = gradient.reshape(self.tensor, rows // self.tensor, self.seq, width // self.seq)
        parts = jnp.transpose(parts, (2, 0, 1, 3)).reshape(
            self.seq * rows, width // self.seq
        )
        return self.reduce(parts)

    def reduce_columns(self, gradient, blocks):
        depth, width = gradient.shape
        own = width // blocks // self.tensor
        parts = gradient.reshape(self.seq, depth // self.seq, blocks, self.tensor, own)
        parts = jnp.transpose(parts, (0, 3, 1, 2, 4)).reshape(
            self.seq * self.tensor * depth // self.seq, blocks * own
        )
        return self.reduce(parts).reshape(depth // self.seq, blocks, own)

    def reduce(self, parts):
        own = lax.psum_scatter(parts, ("seq", "tensor"), scatter_dimension=0, tiled=True)
        return lax.psum(own, "dp").astype(F32)


def local(
    source,
    target,
    out_grad,
    source_segments,
    target_segments,
    enc_gain,
    enc_shift,
    enc_qkv,
    enc_proj,
    enc_up,
    enc_down,
    dec_gain,
    dec_shift,
    dec_self_qkv,
    dec_self_proj,
    dec_cross_q,
    dec_cross_kv,
    dec_cross_proj,
    dec_up,
    dec_down,
):
    width = source.shape[2]
    lay = Layout(source.shape[0])
    w_enc_qkv = lay.gather_columns(enc_qkv)
    w_self_qkv = lay.gather_columns(dec_self_qkv)
    w_enc_proj = lay.gather_weight(enc_proj)
    w_self_proj = lay.gather_weight(dec_self_proj)
    w_enc_up = lay.gather_columns(enc_up[:, None])
    w_enc_down = lay.gather_weight(enc_down)
    w_cross_q = lay.gather_columns(dec_cross_q[:, None])
    w_cross_kv = lay.gather_columns(dec_cross_kv)
    w_cross_proj = lay.gather_weight(dec_cross_proj)
    w_dec_up = lay.gather_columns(dec_up[:, None])
    w_dec_down = lay.gather_weight(dec_down)
    slot = lax.rem(lay.place, lay.slots)
    rows = source.shape[1] * lay.slots
    first_row = (lay.half * lay.spread + lay.place // lay.slots) * rows
    source_ids = lax.dynamic_index_in_dim(source_segments, slot, 0, keepdims=False)
    target_ids = lax.dynamic_index_in_dim(target_segments, slot, 0, keepdims=False)
    ids = jnp.arange(LANES, dtype=jnp.int32) % HEAD_DIM
    own_source = lax.dynamic_slice_in_dim(source_ids, first_row, rows, 0)
    own_target = lax.dynamic_slice_in_dim(target_ids, first_row, rows, 0)
    source_query = jnp.where(own_source[:, None] == ids[None], NEG, 0.0).astype(BF16)
    target_query = jnp.where(own_target[:, None] == ids[None], NEG, 0.0).astype(BF16)
    counted = ids[None] < IDS
    source_key = ((source_ids[:, None] != ids[None]) & counted).astype(BF16)
    target_key = ((target_ids[:, None] != ids[None]) & counted).astype(BF16)
    first = first_row[None].astype(jnp.int32)

    x_source = lay.to_slots(source).astype(F32)
    x_target = lay.to_slots(target).astype(F32)
    cotangent = lay.to_slots(out_grad).astype(F32)

    rows_a = layer_norm(x_source, enc_gain[0], enc_shift[0]).astype(BF16)
    qkv_a = project(rows_a, w_enc_qkv).astype(BF16)
    query_a = qkv_a[:, :width]
    pairs_a = lay.gather_keys(qkv_a[:, width:])
    mixed_a, total_a = attend(
        query_a, pairs_a[:, :width], pairs_a[:, width:], source_query, source_key, first, False
    )
    hidden = x_source + project(mixed_a, w_enc_proj)
    rows_c = layer_norm(x_target, dec_gain[0], dec_shift[0]).astype(BF16)
    qkv_c = project(rows_c, w_self_qkv).astype(BF16)
    query_c = qkv_c[:, :width]
    pairs_c = lay.gather_keys(qkv_c[:, width:])
    mixed_c, total_c = attend(
        query_c, pairs_c[:, :width], pairs_c[:, width:], target_query, target_key, first, True
    )
    after_self = x_target + project(mixed_c, w_self_proj)
    rows_b = layer_norm(hidden, enc_gain[1], enc_shift[1]).astype(BF16)
    inner_b = project(rows_b, w_enc_up)
    active_b = exact_gelu(inner_b).astype(BF16)
    encoded = hidden + project(active_b, w_enc_down)
    rows_m = layer_norm(encoded, enc_gain[2], enc_shift[2]).astype(BF16)
    pairs_m = lay.gather_keys(project(rows_m, w_cross_kv).astype(BF16))
    rows_e = layer_norm(after_self, dec_gain[1], dec_shift[1]).astype(BF16)
    query_e = project(rows_e, w_cross_q).astype(BF16)
    mixed_e, total_e = attend(
        query_e, pairs_m[:, :width], pairs_m[:, width:], target_query, source_key, first, False
    )
    after_cross = after_self + project(mixed_e, w_cross_proj)
    rows_f = layer_norm(after_cross, dec_gain[2], dec_shift[2]).astype(BF16)
    inner_f = project(rows_f, w_dec_up)
    active_f = exact_gelu(inner_f).astype(BF16)
    final_rows = after_cross + project(active_f, w_dec_down)
    decoded, final_back = jax.vjp(layer_norm, final_rows, dec_gain[3], dec_shift[3])

    d_final, dec_gain_three, dec_shift_three = final_back(cotangent)

    def ffn_back(d_out, rows_in, inner, active, weight_up, weight_down):
        d_low = d_out.astype(BF16)
        grad_down = lay.reduce_rows(weight_grad(active, d_low))
        d_active = back_project(d_low, weight_down)
        _, gelu_back = jax.vjp(exact_gelu, inner)
        d_inner = gelu_back(d_active)[0].astype(BF16)
        grad_up = lay.reduce_columns(weight_grad(rows_in, d_inner), 1)[:, 0]
        return back_project(d_inner, weight_up), grad_up, grad_down

    d_normed, grad_dec_up, grad_dec_down = ffn_back(
        d_final, rows_f, inner_f, active_f, w_dec_up, w_dec_down
    )
    d_input, dec_gain_two, dec_shift_two = norm_back(
        after_cross, dec_gain[2], dec_shift[2], d_normed
    )
    d_cross = d_final + d_input
    d_low = d_cross.astype(BF16)
    grad_cross_proj = lay.reduce_rows(weight_grad(mixed_e, d_low))
    d_mixed = back_project(d_low, w_cross_proj).astype(BF16)
    d_query, d_keys, d_values = attend_back(
        query_e,
        pairs_m[:, :width],
        pairs_m[:, width:],
        target_query,
        source_key,
        first,
        False,
        total_e,
        mixed_e,
        d_mixed,
    )
    d_pairs = lay.scatter_keys(jnp.concatenate([d_keys, d_values], 1))
    grad_cross_q = lay.reduce_columns(weight_grad(rows_e, d_query), 1)[:, 0]
    grad_cross_kv = lay.reduce_columns(weight_grad(rows_m, d_pairs), 2)
    d_normed = back_project(d_query, w_cross_q)
    d_memory = back_project(d_pairs, w_cross_kv)
    d_input, dec_gain_one, dec_shift_one = norm_back(
        after_self, dec_gain[1], dec_shift[1], d_normed
    )
    d_self = d_cross + d_input
    d_encoded, enc_gain_two, enc_shift_two = norm_back(encoded, enc_gain[2], enc_shift[2], d_memory)
    d_normed, grad_enc_up, grad_enc_down = ffn_back(
        d_encoded, rows_b, inner_b, active_b, w_enc_up, w_enc_down
    )
    d_input, enc_gain_one, enc_shift_one = norm_back(hidden, enc_gain[1], enc_shift[1], d_normed)
    d_hidden = d_encoded + d_input

    def self_back(d_out, rows_in, query, pairs, marks, causal, totals, mixed, w_qkv, w_proj):
        d_low = d_out.astype(BF16)
        grad_proj = lay.reduce_rows(weight_grad(mixed, d_low))
        d_mixed = back_project(d_low, w_proj).astype(BF16)
        d_query, d_keys, d_values = attend_back(
            query,
            pairs[:, :width],
            pairs[:, width:],
            marks[0],
            marks[1],
            first,
            causal,
            totals,
            mixed,
            d_mixed,
        )
        d_pairs = lay.scatter_keys(jnp.concatenate([d_keys, d_values], 1))
        d_qkv = jnp.concatenate([d_query, d_pairs], 1)
        grad_qkv = lay.reduce_columns(weight_grad(rows_in, d_qkv), 3)
        return back_project(d_qkv, w_qkv), grad_qkv, grad_proj

    d_normed, grad_self_qkv, grad_self_proj = self_back(
        d_self,
        rows_c,
        query_c,
        pairs_c,
        (target_query, target_key),
        True,
        total_c,
        mixed_c,
        w_self_qkv,
        w_self_proj,
    )
    d_input, dec_gain_zero, dec_shift_zero = norm_back(
        x_target, dec_gain[0], dec_shift[0], d_normed
    )
    target_grad = d_self + d_input
    d_normed, grad_enc_qkv, grad_enc_proj = self_back(
        d_hidden,
        rows_a,
        query_a,
        pairs_a,
        (source_query, source_key),
        False,
        total_a,
        mixed_a,
        w_enc_qkv,
        w_enc_proj,
    )
    d_input, enc_gain_zero, enc_shift_zero = norm_back(
        x_source, enc_gain[0], enc_shift[0], d_normed
    )
    source_grad = d_hidden + d_input
    norms = jnp.stack(
        [
            enc_gain_zero,
            enc_gain_one,
            enc_gain_two,
            enc_shift_zero,
            enc_shift_one,
            enc_shift_two,
            dec_gain_zero,
            dec_gain_one,
            dec_gain_two,
            dec_gain_three,
            dec_shift_zero,
            dec_shift_one,
            dec_shift_two,
            dec_shift_three,
        ]
    )
    part = width // lay.seq
    norms = lax.dynamic_slice_in_dim(
        lax.psum(norms, ("dp", "seq", "tensor")), lay.half * part, part, 1
    )
    return (
        lay.from_slots(decoded.astype(BF16)),
        lay.from_slots(source_grad.astype(BF16)).astype(F32),
        lay.from_slots(target_grad.astype(BF16)).astype(F32),
        norms[0:3],
        norms[3:6],
        grad_enc_qkv,
        grad_enc_proj,
        grad_enc_up,
        grad_enc_down,
        norms[6:10],
        norms[10:14],
        grad_self_qkv,
        grad_self_proj,
        grad_cross_q,
        grad_cross_kv,
        grad_cross_proj,
        grad_dec_up,
        grad_dec_down,
    )


def swap_pairs(count, bit):
    return [(i, i ^ bit) for i in range(count)]


def norm_parts(inputs):
    centred = inputs - jnp.mean(inputs, -1, keepdims=True)
    scale = lax.rsqrt(jnp.mean(centred * centred, -1, keepdims=True) + EPS)
    return centred * scale, scale


def norm_pull(hat, scale, gain, cotangent):
    tilted = cotangent * gain
    return scale * (
        tilted
        - jnp.mean(tilted, -1, keepdims=True)
        - hat * jnp.mean(tilted * hat, -1, keepdims=True)
    )


ROW_BLOCK = 256
VMEM = 56 << 20


def row_call(kernel, inputs, vectors, outs, sums, name):
    rows, width = inputs[0].shape
    block = pl.BlockSpec((ROW_BLOCK, width), lambda i: (i, 0))
    whole = pl.BlockSpec((1, width), lambda i: (0, 0))
    return pl.pallas_call(
        kernel,
        grid=(rows // ROW_BLOCK,),
        in_specs=[block] * len(inputs) + [whole] * len(vectors),
        out_specs=[block] * len(outs) + [whole] * sums,
        out_shape=[jax.ShapeDtypeStruct((rows, width), kind) for kind in outs]
        + [jax.ShapeDtypeStruct((1, width), F32)] * sums,
        compiler_params=pltpu.CompilerParams(vmem_limit_bytes=VMEM),
        cost_estimate=pl.CostEstimate(
            flops=20 * rows * width,
            bytes_accessed=4 * rows * width * (len(inputs) + len(outs)),
            transcendentals=rows,
        ),
        name=name,
    )(*inputs, *vectors)


def norm_kernel(x_ref, gain_ref, shift_ref, low_ref):
    hat, _ = norm_parts(x_ref[...].astype(F32))
    low_ref[...] = (hat * gain_ref[...] + shift_ref[...]).astype(BF16)


def norm_rows(inputs, gain, shift):
    return row_call(norm_kernel, [inputs], [gain, shift], [BF16], 0, "norm_rows")[0]


def add_norm_kernel(x_ref, own_ref, other_ref, gain_ref, shift_ref, sum_ref, low_ref):
    total = (
        x_ref[...].astype(F32) + own_ref[...].astype(F32) + other_ref[...].astype(F32)
    )
    sum_ref[...] = total
    hat, _ = norm_parts(total)
    low_ref[...] = (hat * gain_ref[...] + shift_ref[...]).astype(BF16)


def add_norm(inputs, own, other, gain, shift):
    return row_call(
        add_norm_kernel, [inputs, own, other], [gain, shift], [F32, BF16], 0, "add_norm"
    )


def add_sums(first, gain_out, shift_out, cotangent, hat):
    @pl.when(first)
    def _():
        gain_out[...] = jnp.zeros_like(gain_out)
        shift_out[...] = jnp.zeros_like(shift_out)

    gain_out[...] += jnp.sum(cotangent * hat, 0, keepdims=True)
    shift_out[...] += jnp.sum(cotangent, 0, keepdims=True)


def last_norm_kernel(
    x_ref, own_ref, other_ref, cot_ref, gain_ref, shift_ref, y_ref, d_ref, low_ref, dg_ref, ds_ref
):
    total = (
        x_ref[...].astype(F32) + own_ref[...].astype(F32) + other_ref[...].astype(F32)
    )
    hat, scale = norm_parts(total)
    y_ref[...] = (hat * gain_ref[...] + shift_ref[...]).astype(BF16)
    cotangent = cot_ref[...].astype(F32)
    d_total = norm_pull(hat, scale, gain_ref[...], cotangent)
    d_ref[...] = d_total
    low_ref[...] = d_total.astype(BF16)
    add_sums(pl.program_id(0) == 0, dg_ref, ds_ref, cotangent, hat)


def last_norm(inputs, own, other, cotangent, gain, shift):
    return row_call(
        last_norm_kernel,
        [inputs, own, other, cotangent],
        [gain, shift],
        [BF16, F32, BF16],
        2,
        "last_norm",
    )


def norm_back_kernel(residual, low, *refs):
    x_ref, own_ref, other_ref = refs[:3]
    refs = refs[3:]
    if residual:
        res_ref, refs = refs[0], refs[1:]
    gain_ref, refs = refs[0], refs[1:]
    hat, scale = norm_parts(x_ref[...].astype(F32))
    cotangent = own_ref[...].astype(F32) + other_ref[...].astype(F32)
    d_total = norm_pull(hat, scale, gain_ref[...], cotangent)
    if residual:
        d_total = d_total + res_ref[...]
    refs[0][...] = d_total.astype(refs[0].dtype)
    if low:
        refs[1][...] = d_total.astype(BF16)
    add_sums(pl.program_id(0) == 0, refs[-2], refs[-1], cotangent, hat)


def norm_back_rows(inputs, own, other, gain, residual, kinds):
    return row_call(
        functools.partial(norm_back_kernel, residual is not None, len(kinds) > 1),
        [inputs, own, other] + ([] if residual is None else [residual]),
        [gain],
        kinds,
        2,
        "norm_back",
    )


def chip_attend_kernel(causal, q_ref, k_ref, v_ref, qa_ref, ka_ref, o_ref, lse_ref):
    rows = q_ref.shape[0]
    block = 256
    low_half = lax.broadcasted_iota(jnp.int32, (1, LANES), 1) < HEAD_DIM
    for start in range(0, rows, block):
        keys = start + block if causal else k_ref.shape[0]
        query = q_ref[pl.ds(start, block), :] * BF16(SCALE)
        query_mark = qa_ref[pl.ds(start, block), :]
        key_block = k_ref[:keys, :]
        key_mark = ka_ref[:keys, :]
        values = v_ref[:keys, :]
        halves = []
        lses = []
        for head in range(2):
            keep = low_half if head == 0 else jnp.logical_not(low_half)
            scores = mxu(
                jnp.where(keep, query, query_mark), jnp.where(keep, key_block, key_mark), NT
            )
            if causal:
                scores = jnp.where(
                    lax.broadcasted_iota(jnp.int32, (block, keys), 1)
                    <= start + lax.broadcasted_iota(jnp.int32, (block, keys), 0),
                    scores,
                    NEG,
                )
            top = jnp.max(scores, -1, keepdims=True)
            weights = jnp.exp(scores - top)
            total = jnp.sum(weights, -1, keepdims=True)
            mixed = mxu(weights.astype(BF16), values, NN)
            halves.append(mixed / total)
            lses.append(top + jnp.log(total))
        o_ref[pl.ds(start, block), :] = jnp.where(low_half, halves[0], halves[1]).astype(BF16)
        turned = jnp.where(low_half, lses[0], lses[1]).T
        lse_ref[0, 0:1, pl.ds(start, block)] = turned[0:1]
        lse_ref[0, 1:2, pl.ds(start, block)] = turned[HEAD_DIM : HEAD_DIM + 1]


def pair_spec(rows, stride, offset):
    return pl.BlockSpec((rows, LANES), lambda p: (0, stride * p + offset))


def chip_attend(queries, q_at, pairs, k_at, v_at, query_mark, key_mark, causal):
    rows = queries.shape[0]
    keys = pairs.shape[0]
    count = queries.shape[1] // LANES // q_at[0]
    return pl.pallas_call(
        functools.partial(chip_attend_kernel, causal),
        grid=(count,),
        in_specs=[
            pair_spec(rows, *q_at),
            pair_spec(keys, *k_at),
            pair_spec(keys, *v_at),
            pl.BlockSpec((rows, LANES), lambda p: (0, 0)),
            pl.BlockSpec((keys, LANES), lambda p: (0, 0)),
        ],
        out_specs=[
            pair_spec(rows, 1, 0),
            pl.BlockSpec((1, 2, rows), lambda p: (p, 0, 0)),
        ],
        out_shape=[
            jax.ShapeDtypeStruct((rows, count * LANES), BF16),
            jax.ShapeDtypeStruct((count, 2, rows), F32),
        ],
        compiler_params=pltpu.CompilerParams(vmem_limit_bytes=VMEM),
        cost_estimate=pl.CostEstimate(
            flops=8 * rows * keys * count * LANES,
            bytes_accessed=16 * rows * count * LANES,
            transcendentals=2 * rows * keys * count,
        ),
        name="attend",
    )(queries, pairs, pairs, query_mark, key_mark)


def chip_attend_back_kernel(causal, fused, *refs):
    q_ref, k_ref, v_ref, qa_ref, ka_ref, lse_ref, o_ref, do_ref = refs[:8]
    outs, (dk_acc, dv_acc) = refs[8:-2], refs[-2:]
    rows = q_ref.shape[0]
    block = 256
    low_half = lax.broadcasted_iota(jnp.int32, (1, LANES), 1) < HEAD_DIM
    zero = jnp.zeros((), BF16)
    dk_acc[...] = jnp.zeros_like(dk_acc)
    dv_acc[...] = jnp.zeros_like(dv_acc)
    for start in range(0, rows, block):
        keys = start + block if causal else k_ref.shape[0]
        span = pl.ds(start, block)
        query = q_ref[span, :] * BF16(SCALE)
        query_mark = qa_ref[span, :]
        key_block = k_ref[:keys, :]
        key_mark = ka_ref[:keys, :]
        values = v_ref[:keys, :]
        d_out = do_ref[span, :]
        inner = (d_out.astype(F32) * o_ref[span, :].astype(F32)).T
        d_query = None
        for head in range(2):
            keep = low_half if head == 0 else jnp.logical_not(low_half)
            delta = jnp.sum(
                inner[head * HEAD_DIM : (head + 1) * HEAD_DIM], axis=0, keepdims=True
            )
            scores = mxu(
                jnp.where(keep, key_block, key_mark), jnp.where(keep, query, query_mark), NT
            )
            if causal:
                scores = jnp.where(
                    lax.broadcasted_iota(jnp.int32, (keys, block), 0)
                    <= start + lax.broadcasted_iota(jnp.int32, (keys, block), 1),
                    scores,
                    NEG,
                )
            probs = jnp.exp(scores - lse_ref[0, head : head + 1, span])
            own_out = jnp.where(keep, d_out, zero)
            d_probs = mxu(values, own_out, NT)
            d_scores = (probs * (d_probs - delta)).astype(BF16)
            dv_acc[:keys, :] += mxu(probs.astype(BF16), own_out, NN)
            dk_acc[:keys, :] += mxu(d_scores, jnp.where(keep, query, zero), NN)
            term = mxu(jnp.where(keep, key_block, zero), d_scores, TN)
            d_query = term if d_query is None else d_query + term
        outs[0][span, :LANES] = (d_query * SCALE).T.astype(BF16)
    if fused:
        outs[0][:, LANES : 2 * LANES] = dk_acc[...].astype(BF16)
        outs[0][:, 2 * LANES :] = dv_acc[...].astype(BF16)
    else:
        outs[1][:, :LANES] = dk_acc[...].astype(BF16)
        outs[1][:, LANES:] = dv_acc[...].astype(BF16)


def chip_attend_back(
    queries, q_at, pairs, k_at, v_at, query_mark, key_mark, causal, log_total, mixed, d_mixed, fused
):
    rows = queries.shape[0]
    keys = pairs.shape[0]
    count = mixed.shape[1] // LANES

    def out(rows, blocks):
        return (
            pl.BlockSpec((rows, blocks * LANES), lambda p: (0, p)),
            jax.ShapeDtypeStruct((rows, count * blocks * LANES), BF16),
        )

    outs = [out(rows, 3)] if fused else [out(rows, 1), out(keys, 2)]
    return pl.pallas_call(
        functools.partial(chip_attend_back_kernel, causal, fused),
        grid=(count,),
        in_specs=[
            pair_spec(rows, *q_at),
            pair_spec(keys, *k_at),
            pair_spec(keys, *v_at),
            pl.BlockSpec((rows, LANES), lambda p: (0, 0)),
            pl.BlockSpec((keys, LANES), lambda p: (0, 0)),
            pl.BlockSpec((1, 2, rows), lambda p: (p, 0, 0)),
            pair_spec(rows, 1, 0),
            pair_spec(rows, 1, 0),
        ],
        out_specs=[spec for spec, _ in outs],
        out_shape=[shape for _, shape in outs],
        scratch_shapes=[pltpu.VMEM((keys, LANES), F32), pltpu.VMEM((keys, LANES), F32)],
        compiler_params=pltpu.CompilerParams(vmem_limit_bytes=VMEM),
        cost_estimate=pl.CostEstimate(
            flops=20 * rows * keys * count * LANES,
            bytes_accessed=32 * rows * count * LANES,
            transcendentals=2 * rows * keys * count,
        ),
        name="attend_back",
    )(queries, pairs, pairs, query_mark, key_mark, log_total, mixed, d_mixed)


def gelu_kernel(x_ref, w_ref, act_ref, slope_ref):
    inner = mxu(x_ref[...], w_ref[...], NN)
    below = 0.5 + 0.5 * lax.erf(inner * (0.5**0.5))
    act_ref[...] = (inner * below).astype(BF16)
    bell = jnp.exp(inner * inner * (-0.5)) * (0.5 / jnp.pi) ** 0.5
    slope_ref[...] = (below + inner * bell).astype(BF16)


def up_gelu(rows_in, weight):
    rows, depth = rows_in.shape
    width = weight.shape[1]
    step = 256
    return pl.pallas_call(
        gelu_kernel,
        grid=(width // step,),
        in_specs=[
            pl.BlockSpec((rows, depth), lambda j: (0, 0)),
            pl.BlockSpec((depth, step), lambda j: (0, j)),
        ],
        out_specs=[pl.BlockSpec((rows, step), lambda j: (0, j))] * 2,
        out_shape=[jax.ShapeDtypeStruct((rows, width), BF16)] * 2,
        compiler_params=pltpu.CompilerParams(vmem_limit_bytes=VMEM),
        cost_estimate=pl.CostEstimate(
            flops=2 * rows * depth * width,
            bytes_accessed=2 * (rows + width) * depth + 4 * rows * width,
            transcendentals=2 * rows * width,
        ),
        name="up_gelu",
    )(rows_in, weight)


def weight_kernel(count, *refs):
    out_ref = refs[-1]
    at = 0
    for i in range(count):
        own = refs[i].shape[1]
        out_ref[pl.ds(at, own), :] = mxu(refs[i][...], refs[count + i][...], TN).astype(BF16)
        at += own


def weight_grads(pairs, part):
    rows, width = pairs[0][1].shape
    owns = [hidden.shape[1] // 4 for hidden, _ in pairs]
    return pl.pallas_call(
        functools.partial(weight_kernel, len(pairs)),
        grid=(2,),
        in_specs=[
            pl.BlockSpec((rows, own), lambda i: (0, 2 * part + i)) for own in owns
        ]
        + [pl.BlockSpec((rows, width), lambda i: (0, 0)) for _ in pairs],
        out_specs=pl.BlockSpec((sum(owns), width), lambda i: (i, 0)),
        out_shape=jax.ShapeDtypeStruct((2 * sum(owns), width), BF16),
        compiler_params=pltpu.CompilerParams(vmem_limit_bytes=VMEM),
        cost_estimate=pl.CostEstimate(
            flops=4 * sum(owns) * width * rows,
            bytes_accessed=4 * sum(owns) * (width + rows) + 2 * len(pairs) * rows * width,
            transcendentals=0,
        ),
        name="weight_grads",
    )(*[hidden for hidden, _ in pairs], *[wide for _, wide in pairs])


CROSS = ("seq", "tensor")


class Chip:
    def __init__(self):
        self.core = lax.axis_index("seq")
        self.place = lax.axis_index("tensor")
        self.line = lax.axis_index("dp")
        self.first = [(i, i ^ 1) for i in range(4)] + [(4 + i, 4 + (i ^ 2)) for i in range(4)]
        self.second = [(i, i ^ 2) for i in range(4)] + [(4 + i, 4 + (i ^ 1)) for i in range(4)]

    def other(self, block):
        return lax.ppermute(block, "seq", swap_pairs(2, 1))

    def gather(self, block):
        near = lax.ppermute(block, CROSS, self.first)
        side = lax.ppermute(block, CROSS, self.second)
        far = lax.ppermute(side, CROSS, self.first)
        return [block, side, near, far]

    def ordered(self, own, other, index):
        first = index == 0
        return jnp.concatenate([jnp.where(first, own, other), jnp.where(first, other, own)], 0)

    def to_slot(self, block):
        rows = lax.all_to_all(block, "tensor", 0, 0, tiled=True)
        rows = rows.reshape(-1, block.shape[2])
        return self.ordered(rows, self.other(rows), self.core)

    def from_slot(self, rows):
        half = rows.shape[0] // 2
        own = lax.dynamic_slice_in_dim(rows, self.core * half, half, 0)
        return lax.all_to_all(own.reshape(4, half // 4, -1), "tensor", 0, 0, tiled=True)

    def send_near(self, block):
        return lax.ppermute(block, CROSS, self.first)

    def send_side(self, block):
        return lax.ppermute(block, CROSS, self.second)

    def split(self, block, index):
        half = block.shape[0] // 2
        return (
            lax.dynamic_slice_in_dim(block, index * half, half, 0),
            lax.dynamic_slice_in_dim(block, (1 - index) * half, half, 0),
        )

    def along(self, block, bit):
        return lax.ppermute(block, "dp", swap_pairs(4, bit))


def add_low(left, right):
    return (left.astype(F32) + right.astype(F32)).astype(BF16)


def chip_local(
    source,
    target,
    out_grad,
    source_segments,
    target_segments,
    enc_gain,
    enc_shift,
    enc_qkv,
    enc_proj,
    enc_up,
    enc_down,
    dec_gain,
    dec_shift,
    dec_self_qkv,
    dec_self_proj,
    dec_cross_q,
    dec_cross_kv,
    dec_cross_proj,
    dec_up,
    dec_down,
):
    chip = Chip()
    core = chip.core
    tie = lax.optimization_barrier

    def own_columns(weight):
        part = weight.shape[-1] // 2
        cut = lax.dynamic_slice_in_dim(weight, core * part, part, weight.ndim - 1)
        return cut.reshape(weight.shape[0], -1)

    def own_rows(weight):
        part = weight.shape[0] // 2
        return lax.dynamic_slice_in_dim(weight, core * part, part, 0)

    def columns(pieces, low, high):
        return jnp.concatenate([piece[:, low:high] for piece in pieces], 1)

    def rows_of(pieces, low, high):
        return jnp.concatenate([piece[low:high] for piece in pieces], 0)

    x_source = chip.to_slot(source)
    x_target = chip.to_slot(target)
    source_ids = lax.dynamic_index_in_dim(source_segments, chip.place, 0, keepdims=False)
    target_ids = lax.dynamic_index_in_dim(target_segments, chip.place, 0, keepdims=False)
    ids = jnp.arange(LANES, dtype=jnp.int32)[None] % HEAD_DIM
    counted = ids < IDS
    source_query = jnp.where(source_ids[:, None] == ids, NEG, 0.0).astype(BF16)
    target_query = jnp.where(target_ids[:, None] == ids, NEG, 0.0).astype(BF16)
    source_key = ((source_ids[:, None] != ids) & counted).astype(BF16)
    target_key = ((target_ids[:, None] != ids) & counted).astype(BF16)

    bundles = [
        jnp.concatenate([own_columns(enc_qkv), own_columns(dec_self_qkv)], 1),
        jnp.concatenate([own_rows(enc_proj), own_rows(dec_self_proj), own_rows(dec_cross_proj)], 0),
        own_columns(enc_up),
        own_rows(enc_down),
        jnp.concatenate(
            [own_columns(dec_cross_q), own_columns(dec_cross_kv), own_columns(dec_up)], 1
        ),
        own_rows(dec_down),
    ]
    gathered = []
    for index, bundle in enumerate(bundles):
        if index >= 2:
            bundle, _ = tie((bundle, gathered[index - 2][1]))
        gathered.append(chip.gather(bundle))
    qkv_width = bundles[0].shape[1] // 2
    proj_rows = bundles[1].shape[0] // 3
    head_width = dec_cross_q.shape[1] // 2
    w_enc_qkv = columns(gathered[0], 0, qkv_width)
    w_self_qkv = columns(gathered[0], qkv_width, 2 * qkv_width)
    w_enc_proj = rows_of(gathered[1], 0, proj_rows)
    w_self_proj = rows_of(gathered[1], proj_rows, 2 * proj_rows)
    w_cross_proj = rows_of(gathered[1], 2 * proj_rows, 3 * proj_rows)
    w_enc_up = jnp.concatenate(gathered[2], 1)
    w_enc_down = jnp.concatenate(gathered[3], 0)
    w_cross_q = columns(gathered[4], 0, head_width)
    w_cross_kv = columns(gathered[4], head_width, 3 * head_width)
    w_dec_up = columns(gathered[4], 3 * head_width, bundles[4].shape[1])
    w_dec_down = jnp.concatenate(gathered[5], 0)

    def enc(index):
        return enc_gain[index : index + 1], enc_shift[index : index + 1]

    def dec(index):
        return dec_gain[index : index + 1], dec_shift[index : index + 1]

    def partial(rows_in, weight):
        own = project(rows_in, weight).astype(BF16)
        return own, chip.other(own)

    def back_partial(grad, weight):
        own = back_project(grad, weight).astype(BF16)
        return own, chip.other(own)

    fused_at = ((3, 0), (3, 1), (3, 2))

    def attend_self(rows_in, weight, marks, causal):
        qkv = project(rows_in, weight).astype(BF16)
        mixed, totals = chip_attend(
            qkv, fused_at[0], qkv, fused_at[1], fused_at[2], marks[0], marks[1], causal
        )
        return qkv, mixed, totals

    rows_a = norm_rows(x_source, *enc(0))
    rows_c = norm_rows(x_target, *dec(0))
    qkv_a, mixed_a, total_a = attend_self(rows_a, w_enc_qkv, (source_query, source_key), False)
    hidden, rows_b = add_norm(x_source, *partial(mixed_a, w_enc_proj), *enc(1))
    qkv_c, mixed_c, total_c = attend_self(rows_c, w_self_qkv, (target_query, target_key), True)
    after_self, rows_e = add_norm(x_target, *partial(mixed_c, w_self_proj), *dec(1))
    cotangent = chip.to_slot(out_grad)
    active_b, slope_b = up_gelu(rows_b, w_enc_up)
    encoded, rows_m = add_norm(hidden, *partial(active_b, w_enc_down), *enc(2))
    query_e = project(rows_e, w_cross_q).astype(BF16)
    pairs_m = project(rows_m, w_cross_kv).astype(BF16)
    mixed_e, total_e = chip_attend(
        query_e, (1, 0), pairs_m, (2, 0), (2, 1), target_query, source_key, False
    )
    after_cross, rows_f = add_norm(after_self, *partial(mixed_e, w_cross_proj), *dec(2))
    active_f, slope_f = up_gelu(rows_f, w_dec_up)
    decoded, d_final, low_final, gain_d3, shift_d3 = last_norm(
        after_cross, *partial(active_f, w_dec_down), cotangent, *dec(3)
    )
    decoded = chip.from_slot(decoded)


    def stage_one(pairs):
        sent = weight_grads(pairs, 1)
        return chip.send_near(sent), weight_grads(pairs, 0)

    def stage_two(state):
        came, kept = state
        half = kept.shape[0] // 2
        sent = add_low(kept[half:], came[half:])
        return chip.send_side(sent), add_low(kept[:half], came[:half])

    low_bit = lax.rem(chip.line, 2)
    high_bit = chip.line // 2

    def stage_three(state):
        came, kept = state
        kept_own, kept_other = chip.split(kept, low_bit)
        came_own, came_other = chip.split(came, low_bit)
        return chip.along(add_low(kept_other, came_other), 1), add_low(kept_own, came_own)

    def stage_four(state):
        came, kept = state
        kept_own, kept_other = chip.split(kept, high_bit)
        came_own, came_other = chip.split(came, high_bit)
        return chip.along(add_low(kept_other, came_other), 2), add_low(kept_own, came_own)

    def stage_five(state):
        own = add_low(*state)
        return chip.along(own, 2), own

    def stage_six(state):
        came, own = state
        half = chip.ordered(own, came, high_bit)
        return chip.along(half, 1), half

    def stage_seven(state):
        came, own = state
        whole = chip.ordered(own, came, low_bit)
        width = whole.shape[1] // 2
        sent = lax.dynamic_slice_in_dim(whole, (1 - core) * width, width, 1)
        own = lax.dynamic_slice_in_dim(whole, core * width, width, 1)
        return chip.other(sent), own

    def stage_eight(state):
        came, own = state
        return chip.ordered(own[None], came[None], core).astype(F32)

    stages = [stage_two, stage_three, stage_four, stage_five, stage_six, stage_seven, stage_eight]

    class Reduction:
        def __init__(self, pairs):
            self.state = stage_one(pairs)
            self.at = 0

        def step(self):
            if self.at < len(stages):
                self.state = stages[self.at](self.state)
                self.at += 1

        def finish(self):
            while self.at < len(stages):
                self.step()
            return self.state

    def ffn_back(low_out, rows_in, slope, weight_up, weight_down):
        d_inner = (back_project(low_out, weight_down) * slope.astype(F32)).astype(BF16)
        return d_inner, back_partial(d_inner, weight_up)

    d_inner_f, (own, other) = ffn_back(low_final, rows_f, slope_f, w_dec_up, w_dec_down)
    red_f = Reduction([(d_inner_f, rows_f), (active_f, low_final)])
    other, _ = tie((other, red_f.state[1]))
    d_cross, low_cross, gain_d2, shift_d2 = norm_back_rows(
        after_cross, own, other, dec(2)[0], d_final, [F32, BF16]
    )
    d_mixed = back_project(low_cross, w_cross_proj).astype(BF16)
    d_query_e, d_pairs_m = chip_attend_back(
        query_e,
        (1, 0),
        pairs_m,
        (2, 0),
        (2, 1),
        target_query,
        source_key,
        False,
        total_e,
        mixed_e,
        d_mixed,
        False,
    )
    own_m, other_m = back_partial(d_pairs_m, w_cross_kv)
    own_e, other_e = back_partial(d_query_e, w_cross_q)
    red_f.step()
    red_x = Reduction([(mixed_e, low_cross), (d_query_e, rows_e), (d_pairs_m, rows_m)])
    other_m, other_e, _, _ = tie((other_m, other_e, red_x.state[1], red_f.state[1]))
    low_encoded_pair = norm_back_rows(encoded, own_m, other_m, enc(2)[0], None, [F32, BF16])
    d_encoded, low_encoded, gain_e2, shift_e2 = low_encoded_pair
    d_self, low_self, gain_d1, shift_d1 = norm_back_rows(
        after_self, own_e, other_e, dec(1)[0], d_cross, [F32, BF16]
    )
    d_inner_b, (own, other) = ffn_back(low_encoded, rows_b, slope_b, w_enc_up, w_enc_down)
    red_f.step()
    red_b = Reduction([(d_inner_b, rows_b), (active_b, low_encoded)])
    red_x.step()
    other, _, _, _ = tie((other, red_b.state[1], red_x.state[1], red_f.state[1]))
    d_hidden, low_hidden, gain_e1, shift_e1 = norm_back_rows(
        hidden, own, other, enc(1)[0], d_encoded, [F32, BF16]
    )

    def self_back(low_out, qkv, marks, causal, totals, mixed, w_qkv, w_proj):
        d_mixed = back_project(low_out, w_proj).astype(BF16)
        (d_qkv,) = chip_attend_back(
            qkv,
            fused_at[0],
            qkv,
            fused_at[1],
            fused_at[2],
            marks[0],
            marks[1],
            causal,
            totals,
            mixed,
            d_mixed,
            True,
        )
        return d_qkv

    d_qkv_c = self_back(
        low_self, qkv_c, (target_query, target_key), True, total_c, mixed_c, w_self_qkv, w_self_proj
    )
    red_c = Reduction([(mixed_c, low_self), (d_qkv_c, rows_c)])
    red_f.step()
    red_x.step()
    red_b.step()
    low_hidden, _, _, _, _ = tie(
        (low_hidden, red_c.state[1], red_f.state[1], red_x.state[1], red_b.state[1])
    )
    d_qkv_a = self_back(
        low_hidden, qkv_a, (source_query, source_key), False, total_a, mixed_a, w_enc_qkv, w_enc_proj
    )
    own_a, other_a = back_partial(d_qkv_a, w_enc_qkv)
    red_a = Reduction([(mixed_a, low_hidden), (d_qkv_a, rows_a)])
    own_c, other_c = back_partial(d_qkv_c, w_self_qkv)
    source_grad, gain_e0, shift_e0 = norm_back_rows(
        x_source, own_a, other_a, enc(0)[0], d_hidden, [BF16]
    )
    target_grad, gain_d0, shift_d0 = norm_back_rows(
        x_target, own_c, other_c, dec(0)[0], d_self, [BF16]
    )
    source_grad = chip.from_slot(source_grad).astype(F32)
    target_grad = chip.from_slot(target_grad).astype(F32)

    norms = jnp.concatenate(
        [
            gain_e0,
            gain_e1,
            gain_e2,
            shift_e0,
            shift_e1,
            shift_e2,
            gain_d0,
            gain_d1,
            gain_d2,
            gain_d3,
            shift_d0,
            shift_d1,
            shift_d2,
            shift_d3,
        ],
        0,
    )
    part = norms.shape[1] // 2
    norms = lax.dynamic_slice_in_dim(norms, core * part, part, 1)
    norms = lax.psum(norms, ("dp", "tensor"))

    def wide(block, blocks):
        cores, rows, width = block.shape
        block = block.reshape(cores, blocks, rows // blocks, width)
        return jnp.transpose(block, (3, 1, 0, 2)).reshape(width, blocks, -1)

    def tall(block):
        return block.reshape(-1, block.shape[2])

    done_f, done_x, done_b, done_c, done_a = (
        red.finish() for red in (red_f, red_x, red_b, red_c, red_a)
    )
    hid = done_f.shape[1] // 2
    n = proj_rows
    return (
        decoded,
        source_grad,
        target_grad,
        norms[0:3],
        norms[3:6],
        wide(done_a[:, n:], 3),
        tall(done_a[:, :n]),
        wide(done_b[:, :hid], 1)[:, 0],
        tall(done_b[:, hid:]),
        norms[6:10],
        norms[10:14],
        wide(done_c[:, n:], 3),
        tall(done_c[:, :n]),
        wide(done_x[:, n : n + head_width], 1)[:, 0],
        wide(done_x[:, n + head_width :], 2),
        tall(done_x[:, :n]),
        wide(done_f[:, :hid], 1)[:, 0],
        tall(done_f[:, hid:]),
    )


def solution(mesh):
    rows = P("dp", ("seq", "tensor"), None)
    segments = P("dp", None)
    shape = dict(mesh.shape)
    chips = shape["dp"] == 4 and shape["seq"] == 2 and shape["tensor"] == 4
    return jax.shard_map(
        chip_local if chips else local,
        mesh=mesh,
        in_specs=(
            rows,
            rows,
            rows,
            segments,
            segments,
            P(),
            P(),
            P(None, None, "tensor"),
            P("tensor", None),
            P(None, "tensor"),
            P("tensor", None),
            P(),
            P(),
            P(None, None, "tensor"),
            P("tensor", None),
            P(None, "tensor"),
            P(None, None, "tensor"),
            P("tensor", None),
            P(None, "tensor"),
            P("tensor", None),
        ),
        out_specs=(
            rows,
            rows,
            rows,
            P(None, "seq"),
            P(None, "seq"),
            P("seq", None, "tensor"),
            P("tensor", "seq"),
            P("seq", "tensor"),
            P("tensor", "seq"),
            P(None, "seq"),
            P(None, "seq"),
            P("seq", None, "tensor"),
            P("tensor", "seq"),
            P("seq", "tensor"),
            P("seq", None, "tensor"),
            P("tensor", "seq"),
            P("seq", "tensor"),
            P("tensor", "seq"),
        ),
        check_vma=False,
    )
```

```python
import functools

import jax
import jax.numpy as jnp
from jax import lax
from jax.experimental import pallas as pl
from jax.experimental.pallas import tpu as pltpu
from jax.sharding import PartitionSpec as P

HEAD_DIM = 64
LANES = 128
IDS = 9
EPS = 1e-05
NEG = -1e30
SCALE = HEAD_DIM ** (-0.5)
F32 = jnp.float32
BF16 = jnp.bfloat16
NT = (((1,), (1,)), ((), ()))
NN = (((1,), (0,)), ((), ()))
TN = (((0,), (0,)), ((), ()))


def mxu(left, right, dims):
    return lax.dot_general(left, right, dims, preferred_element_type=F32)


def layer_norm(inputs, norm_gain, norm_shift):
    row_mean = jnp.mean(inputs, -1, keepdims=True)
    centred = inputs - row_mean
    spread = jnp.mean(centred * centred, -1, keepdims=True)
    return centred * lax.rsqrt(spread + EPS) * norm_gain + norm_shift


def exact_gelu(inputs):
    return jax.nn.gelu(inputs, approximate=False)


def norm_back(inputs, norm_gain, norm_shift, cotangent):
    _, pullback = jax.vjp(layer_norm, inputs, norm_gain, norm_shift)
    return pullback(cotangent)


def project(rows, weight):
    return mxu(rows, weight, NN)


def back_project(grad, weight):
    return mxu(grad, weight, NT)


def weight_grad(rows, grad):
    return mxu(rows, grad, TN).astype(BF16)


def attend_kernel(causal, first_ref, q_ref, k_ref, v_ref, qa_ref, ka_ref, o_ref, lse_ref):
    rows = q_ref.shape[0]
    keys = k_ref.shape[0]
    block = min(rows, 256)
    low_half = lax.broadcasted_iota(jnp.int32, (1, LANES), 1) < HEAD_DIM
    key_block = k_ref[...]
    key_mark = ka_ref[...]
    values = v_ref[...]
    for start in range(0, rows, block):
        query = q_ref[pl.ds(start, block), :] * BF16(SCALE)
        query_mark = qa_ref[pl.ds(start, block), :]
        halves = []
        lses = []
        for head in range(2):
            keep = low_half if head == 0 else jnp.logical_not(low_half)
            scores = mxu(
                jnp.where(keep, query, query_mark), jnp.where(keep, key_block, key_mark), NT
            )
            if causal:
                place = (
                    first_ref[0] + start + lax.broadcasted_iota(jnp.int32, (block, keys), 0)
                )
                scores = jnp.where(
                    lax.broadcasted_iota(jnp.int32, (block, keys), 1) <= place, scores, NEG
                )
            top = jnp.max(scores, -1, keepdims=True)
            weights = jnp.exp(scores - top)
            total = jnp.sum(weights, -1, keepdims=True)
            mixed = mxu(weights.astype(BF16), values, NN)
            halves.append(mixed / total)
            lses.append(top + jnp.log(total))
        o_ref[pl.ds(start, block), :] = jnp.where(low_half, halves[0], halves[1]).astype(BF16)
        both = jnp.where(low_half, lses[0], lses[1])
        turned = both.T
        lse_ref[0, 0:1, pl.ds(start, block)] = turned[0:1]
        lse_ref[0, 1:2, pl.ds(start, block)] = turned[HEAD_DIM : HEAD_DIM + 1]


def attend(queries, keys, values, query_mark, key_mark, first_row, causal):
    rows, width = queries.shape
    key_rows = keys.shape[0]
    pairs = width // LANES
    return pl.pallas_call(
        functools.partial(attend_kernel, causal),
        grid_spec=pltpu.PrefetchScalarGridSpec(
            num_scalar_prefetch=1,
            grid=(pairs,),
            in_specs=[
                pl.BlockSpec((rows, LANES), lambda p, first: (0, p)),
                pl.BlockSpec((key_rows, LANES), lambda p, first: (0, p)),
                pl.BlockSpec((key_rows, LANES), lambda p, first: (0, p)),
                pl.BlockSpec((rows, LANES), lambda p, first: (0, 0)),
                pl.BlockSpec((key_rows, LANES), lambda p, first: (0, 0)),
            ],
            out_specs=[
                pl.BlockSpec((rows, LANES), lambda p, first: (0, p)),
                pl.BlockSpec((1, 2, rows), lambda p, first: (p, 0, 0)),
            ],
        ),
        out_shape=[
            jax.ShapeDtypeStruct((rows, width), BF16),
            jax.ShapeDtypeStruct((pairs, 2, rows), F32),
        ],
        compiler_params=pltpu.CompilerParams(vmem_limit_bytes=40 << 20),
        cost_estimate=pl.CostEstimate(
            flops=4 * rows * key_rows * width * 2,
            bytes_accessed=4 * rows * width + 4 * key_rows * width,
            transcendentals=rows * key_rows * width // HEAD_DIM,
        ),
        name="attend",
    )(first_row, queries, keys, values, query_mark, key_mark)


def attend_back_kernel(
    causal,
    first_ref,
    q_ref,
    k_ref,
    v_ref,
    qa_ref,
    ka_ref,
    lse_ref,
    o_ref,
    do_ref,
    dq_ref,
    dk_ref,
    dv_ref,
    dk_acc,
    dv_acc,
):
    rows = q_ref.shape[0]
    keys = k_ref.shape[0]
    block = min(rows, 256)
    low_half = lax.broadcasted_iota(jnp.int32, (1, LANES), 1) < HEAD_DIM
    key_block = k_ref[...]
    key_mark = ka_ref[...]
    values = v_ref[...]
    zero = jnp.zeros((), BF16)
    dk_acc[...] = jnp.zeros_like(dk_acc)
    dv_acc[...] = jnp.zeros_like(dv_acc)
    for start in range(0, rows, block):
        span = pl.ds(start, block)
        query = q_ref[span, :] * BF16(SCALE)
        query_mark = qa_ref[span, :]
        d_out = do_ref[span, :]
        inner = (d_out.astype(F32) * o_ref[span, :].astype(F32)).T
        d_query = None
        for head in range(2):
            keep = low_half if head == 0 else jnp.logical_not(low_half)
            delta = jnp.sum(
                inner[head * HEAD_DIM : (head + 1) * HEAD_DIM], axis=0, keepdims=True
            )
            scores = mxu(
                jnp.where(keep, key_block, key_mark), jnp.where(keep, query, query_mark), NT
            )
            if causal:
                place = (
                    first_ref[0] + start + lax.broadcasted_iota(jnp.int32, (keys, block), 1)
                )
                scores = jnp.where(
                    lax.broadcasted_iota(jnp.int32, (keys, block), 0) <= place, scores, NEG
                )
            probs = jnp.exp(scores - lse_ref[0, head : head + 1, span])
            own_out = jnp.where(keep, d_out, zero)
            d_probs = mxu(values, own_out, NT)
            d_scores = (probs * (d_probs - delta)).astype(BF16)
            dv_acc[...] += mxu(probs.astype(BF16), own_out, NN)
            dk_acc[...] += mxu(d_scores, jnp.where(keep, query, zero), NN)
            term = mxu(jnp.where(keep, key_block, zero), d_scores, TN)
            d_query = term if d_query is None else d_query + term
        dq_ref[span, :] = (d_query * SCALE).T.astype(BF16)
    dk_ref[...] = dk_acc[...].astype(BF16)
    dv_ref[...] = dv_acc[...].astype(BF16)


def attend_back(
    queries, keys, values, query_mark, key_mark, first_row, causal, log_total, mixed, d_mixed
):
    rows, width = queries.shape
    key_rows = keys.shape[0]
    pairs = width // LANES
    row_spec = pl.BlockSpec((rows, LANES), lambda p, first: (0, p))
    key_spec = pl.BlockSpec((key_rows, LANES), lambda p, first: (0, p))
    return pl.pallas_call(
        functools.partial(attend_back_kernel, causal),
        grid_spec=pltpu.PrefetchScalarGridSpec(
            num_scalar_prefetch=1,
            grid=(pairs,),
            in_specs=[
                row_spec,
                key_spec,
                key_spec,
                pl.BlockSpec((rows, LANES), lambda p, first: (0, 0)),
                pl.BlockSpec((key_rows, LANES), lambda p, first: (0, 0)),
                pl.BlockSpec((1, 2, rows), lambda p, first: (p, 0, 0)),
                row_spec,
                row_spec,
            ],
            out_specs=[row_spec, key_spec, key_spec],
            scratch_shapes=[
                pltpu.VMEM((key_rows, LANES), F32),
                pltpu.VMEM((key_rows, LANES), F32),
            ],
        ),
        out_shape=[
            jax.ShapeDtypeStruct((rows, width), BF16),
            jax.ShapeDtypeStruct((key_rows, width), BF16),
            jax.ShapeDtypeStruct((key_rows, width), BF16),
        ],
        compiler_params=pltpu.CompilerParams(vmem_limit_bytes=40 << 20),
        cost_estimate=pl.CostEstimate(
            flops=10 * rows * key_rows * width * 2,
            bytes_accessed=8 * rows * width + 8 * key_rows * width,
            transcendentals=rows * key_rows * width // HEAD_DIM,
        ),
        name="attend_back",
    )(first_row, queries, keys, values, query_mark, key_mark, log_total, mixed, d_mixed)


class Layout:
    def __init__(self, slots):
        self.tensor = lax.axis_size("tensor")
        self.seq = lax.axis_size("seq")
        self.slots = slots
        self.spread = self.tensor // slots
        self.place = lax.axis_index("tensor")
        self.half = lax.axis_index("seq")
        self.row_groups = [
            [j * slots + u for u in range(slots)] for j in range(self.spread)
        ]
        self.slot_groups = [
            [j * slots + u for j in range(self.spread)] for u in range(slots)
        ]

    def to_slots(self, block):
        rows = lax.all_to_all(
            block, "tensor", 0, 1, axis_index_groups=self.row_groups, tiled=True
        )
        return rows.reshape(-1, block.shape[2])

    def from_slots(self, rows):
        block = rows.reshape(1, rows.shape[0], rows.shape[1])
        return lax.all_to_all(
            block, "tensor", 1, 0, axis_index_groups=self.row_groups, tiled=True
        )

    def gather_keys(self, rows):
        if self.spread > 1:
            rows = lax.all_gather(
                rows, "tensor", axis=0, axis_index_groups=self.slot_groups, tiled=True
            )
        return lax.all_gather(rows, "seq", axis=0, tiled=True)

    def scatter_keys(self, rows):
        rows = lax.psum_scatter(rows, "seq", scatter_dimension=0, tiled=True)
        if self.spread > 1:
            rows = lax.psum_scatter(
                rows,
                "tensor",
                scatter_dimension=0,
                axis_index_groups=self.slot_groups,
                tiled=True,
            )
        return rows

    def gather_weight(self, shard):
        part = shard.shape[0] // self.seq
        own = lax.dynamic_slice_in_dim(shard, self.half * part, part, 0)
        return lax.all_gather(own, ("tensor", "seq"), axis=0, tiled=True)

    def gather_columns(self, shard):
        depth, blocks, own = shard.shape
        whole = self.gather_weight(shard.reshape(depth, blocks * own))
        whole = whole.reshape(self.tensor, depth, blocks, own)
        return jnp.transpose(whole, (1, 2, 0, 3)).reshape(depth, blocks * self.tensor * own)

    def reduce_rows(self, gradient):
        rows, width = gradient.shape
        parts = gradient.reshape(self.tensor, rows // self.tensor, self.seq, width // self.seq)
        parts = jnp.transpose(parts, (2, 0, 1, 3)).reshape(
            self.seq * rows, width // self.seq
        )
        return self.reduce(parts)

    def reduce_columns(self, gradient, blocks):
        depth, width = gradient.shape
        own = width // blocks // self.tensor
        parts = gradient.reshape(self.seq, depth // self.seq, blocks, self.tensor, own)
        parts = jnp.transpose(parts, (0, 3, 1, 2, 4)).reshape(
            self.seq * self.tensor * depth // self.seq, blocks * own
        )
        return self.reduce(parts).reshape(depth // self.seq, blocks, own)

    def reduce(self, parts):
        own = lax.psum_scatter(parts, ("seq", "tensor"), scatter_dimension=0, tiled=True)
        return lax.psum(own, "dp").astype(F32)


def local(
    source,
    target,
    out_grad,
    source_segments,
    target_segments,
    enc_gain,
    enc_shift,
    enc_qkv,
    enc_proj,
    enc_up,
    enc_down,
    dec_gain,
    dec_shift,
    dec_self_qkv,
    dec_self_proj,
    dec_cross_q,
    dec_cross_kv,
    dec_cross_proj,
    dec_up,
    dec_down,
):
    width = source.shape[2]
    lay = Layout(source.shape[0])
    w_enc_qkv = lay.gather_columns(enc_qkv)
    w_self_qkv = lay.gather_columns(dec_self_qkv)
    w_enc_proj = lay.gather_weight(enc_proj)
    w_self_proj = lay.gather_weight(dec_self_proj)
    w_enc_up = lay.gather_columns(enc_up[:, None])
    w_enc_down = lay.gather_weight(enc_down)
    w_cross_q = lay.gather_columns(dec_cross_q[:, None])
    w_cross_kv = lay.gather_columns(dec_cross_kv)
    w_cross_proj = lay.gather_weight(dec_cross_proj)
    w_dec_up = lay.gather_columns(dec_up[:, None])
    w_dec_down = lay.gather_weight(dec_down)
    slot = lax.rem(lay.place, lay.slots)
    rows = source.shape[1] * lay.slots
    first_row = (lay.half * lay.spread + lay.place // lay.slots) * rows
    source_ids = lax.dynamic_index_in_dim(source_segments, slot, 0, keepdims=False)
    target_ids = lax.dynamic_index_in_dim(target_segments, slot, 0, keepdims=False)
    ids = jnp.arange(LANES, dtype=jnp.int32) % HEAD_DIM
    own_source = lax.dynamic_slice_in_dim(source_ids, first_row, rows, 0)
    own_target = lax.dynamic_slice_in_dim(target_ids, first_row, rows, 0)
    source_query = jnp.where(own_source[:, None] == ids[None], NEG, 0.0).astype(BF16)
    target_query = jnp.where(own_target[:, None] == ids[None], NEG, 0.0).astype(BF16)
    counted = ids[None] < IDS
    source_key = ((source_ids[:, None] != ids[None]) & counted).astype(BF16)
    target_key = ((target_ids[:, None] != ids[None]) & counted).astype(BF16)
    first = first_row[None].astype(jnp.int32)

    x_source = lay.to_slots(source).astype(F32)
    x_target = lay.to_slots(target).astype(F32)
    cotangent = lay.to_slots(out_grad).astype(F32)

    rows_a = layer_norm(x_source, enc_gain[0], enc_shift[0]).astype(BF16)
    qkv_a = project(rows_a, w_enc_qkv).astype(BF16)
    query_a = qkv_a[:, :width]
    pairs_a = lay.gather_keys(qkv_a[:, width:])
    mixed_a, total_a = attend(
        query_a, pairs_a[:, :width], pairs_a[:, width:], source_query, source_key, first, False
    )
    hidden = x_source + project(mixed_a, w_enc_proj)
    rows_c = layer_norm(x_target, dec_gain[0], dec_shift[0]).astype(BF16)
    qkv_c = project(rows_c, w_self_qkv).astype(BF16)
    query_c = qkv_c[:, :width]
    pairs_c = lay.gather_keys(qkv_c[:, width:])
    mixed_c, total_c = attend(
        query_c, pairs_c[:, :width], pairs_c[:, width:], target_query, target_key, first, True
    )
    after_self = x_target + project(mixed_c, w_self_proj)
    rows_b = layer_norm(hidden, enc_gain[1], enc_shift[1]).astype(BF16)
    inner_b = project(rows_b, w_enc_up)
    active_b = exact_gelu(inner_b).astype(BF16)
    encoded = hidden + project(active_b, w_enc_down)
    rows_m = layer_norm(encoded, enc_gain[2], enc_shift[2]).astype(BF16)
    pairs_m = lay.gather_keys(project(rows_m, w_cross_kv).astype(BF16))
    rows_e = layer_norm(after_self, dec_gain[1], dec_shift[1]).astype(BF16)
    query_e = project(rows_e, w_cross_q).astype(BF16)
    mixed_e, total_e = attend(
        query_e, pairs_m[:, :width], pairs_m[:, width:], target_query, source_key, first, False
    )
    after_cross = after_self + project(mixed_e, w_cross_proj)
    rows_f = layer_norm(after_cross, dec_gain[2], dec_shift[2]).astype(BF16)
    inner_f = project(rows_f, w_dec_up)
    active_f = exact_gelu(inner_f).astype(BF16)
    final_rows = after_cross + project(active_f, w_dec_down)
    decoded, final_back = jax.vjp(layer_norm, final_rows, dec_gain[3], dec_shift[3])

    d_final, dec_gain_three, dec_shift_three = final_back(cotangent)

    def ffn_back(d_out, rows_in, inner, active, weight_up, weight_down):
        d_low = d_out.astype(BF16)
        grad_down = lay.reduce_rows(weight_grad(active, d_low))
        d_active = back_project(d_low, weight_down)
        _, gelu_back = jax.vjp(exact_gelu, inner)
        d_inner = gelu_back(d_active)[0].astype(BF16)
        grad_up = lay.reduce_columns(weight_grad(rows_in, d_inner), 1)[:, 0]
        return back_project(d_inner, weight_up), grad_up, grad_down

    d_normed, grad_dec_up, grad_dec_down = ffn_back(
        d_final, rows_f, inner_f, active_f, w_dec_up, w_dec_down
    )
    d_input, dec_gain_two, dec_shift_two = norm_back(
        after_cross, dec_gain[2], dec_shift[2], d_normed
    )
    d_cross = d_final + d_input
    d_low = d_cross.astype(BF16)
    grad_cross_proj = lay.reduce_rows(weight_grad(mixed_e, d_low))
    d_mixed = back_project(d_low, w_cross_proj).astype(BF16)
    d_query, d_keys, d_values = attend_back(
        query_e,
        pairs_m[:, :width],
        pairs_m[:, width:],
        target_query,
        source_key,
        first,
        False,
        total_e,
        mixed_e,
        d_mixed,
    )
    d_pairs = lay.scatter_keys(jnp.concatenate([d_keys, d_values], 1))
    grad_cross_q = lay.reduce_columns(weight_grad(rows_e, d_query), 1)[:, 0]
    grad_cross_kv = lay.reduce_columns(weight_grad(rows_m, d_pairs), 2)
    d_normed = back_project(d_query, w_cross_q)
    d_memory = back_project(d_pairs, w_cross_kv)
    d_input, dec_gain_one, dec_shift_one = norm_back(
        after_self, dec_gain[1], dec_shift[1], d_normed
    )
    d_self = d_cross + d_input
    d_encoded, enc_gain_two, enc_shift_two = norm_back(encoded, enc_gain[2], enc_shift[2], d_memory)
    d_normed, grad_enc_up, grad_enc_down = ffn_back(
        d_encoded, rows_b, inner_b, active_b, w_enc_up, w_enc_down
    )
    d_input, enc_gain_one, enc_shift_one = norm_back(hidden, enc_gain[1], enc_shift[1], d_normed)
    d_hidden = d_encoded + d_input

    def self_back(d_out, rows_in, query, pairs, marks, causal, totals, mixed, w_qkv, w_proj):
        d_low = d_out.astype(BF16)
        grad_proj = lay.reduce_rows(weight_grad(mixed, d_low))
        d_mixed = back_project(d_low, w_proj).astype(BF16)
        d_query, d_keys, d_values = attend_back(
            query,
            pairs[:, :width],
            pairs[:, width:],
            marks[0],
            marks[1],
            first,
            causal,
            totals,
            mixed,
            d_mixed,
        )
        d_pairs = lay.scatter_keys(jnp.concatenate([d_keys, d_values], 1))
        d_qkv = jnp.concatenate([d_query, d_pairs], 1)
        grad_qkv = lay.reduce_columns(weight_grad(rows_in, d_qkv), 3)
        return back_project(d_qkv, w_qkv), grad_qkv, grad_proj

    d_normed, grad_self_qkv, grad_self_proj = self_back(
        d_self,
        rows_c,
        query_c,
        pairs_c,
        (target_query, target_key),
        True,
        total_c,
        mixed_c,
        w_self_qkv,
        w_self_proj,
    )
    d_input, dec_gain_zero, dec_shift_zero = norm_back(
        x_target, dec_gain[0], dec_shift[0], d_normed
    )
    target_grad = d_self + d_input
    d_normed, grad_enc_qkv, grad_enc_proj = self_back(
        d_hidden,
        rows_a,
        query_a,
        pairs_a,
        (source_query, source_key),
        False,
        total_a,
        mixed_a,
        w_enc_qkv,
        w_enc_proj,
    )
    d_input, enc_gain_zero, enc_shift_zero = norm_back(
        x_source, enc_gain[0], enc_shift[0], d_normed
    )
    source_grad = d_hidden + d_input
    norms = jnp.stack(
        [
            enc_gain_zero,
            enc_gain_one,
            enc_gain_two,
            enc_shift_zero,
            enc_shift_one,
            enc_shift_two,
            dec_gain_zero,
            dec_gain_one,
            dec_gain_two,
            dec_gain_three,
            dec_shift_zero,
            dec_shift_one,
            dec_shift_two,
            dec_shift_three,
        ]
    )
    part = width // lay.seq
    norms = lax.dynamic_slice_in_dim(
        lax.psum(norms, ("dp", "seq", "tensor")), lay.half * part, part, 1
    )
    return (
        lay.from_slots(decoded.astype(BF16)),
        lay.from_slots(source_grad.astype(BF16)).astype(F32),
        lay.from_slots(target_grad.astype(BF16)).astype(F32),
        norms[0:3],
        norms[3:6],
        grad_enc_qkv,
        grad_enc_proj,
        grad_enc_up,
        grad_enc_down,
        norms[6:10],
        norms[10:14],
        grad_self_qkv,
        grad_self_proj,
        grad_cross_q,
        grad_cross_kv,
        grad_cross_proj,
        grad_dec_up,
        grad_dec_down,
    )


def swap_pairs(count, bit):
    return [(i, i ^ bit) for i in range(count)]


def norm_parts(inputs):
    centred = inputs - jnp.mean(inputs, -1, keepdims=True)
    scale = lax.rsqrt(jnp.mean(centred * centred, -1, keepdims=True) + EPS)
    return centred * scale, scale


def norm_pull(hat, scale, gain, cotangent):
    tilted = cotangent * gain
    return scale * (
        tilted
        - jnp.mean(tilted, -1, keepdims=True)
        - hat * jnp.mean(tilted * hat, -1, keepdims=True)
    )


ROW_BLOCK = 256
VMEM = 56 << 20
LIGHT = pl.CostEstimate(flops=1 << 20, bytes_accessed=1 << 16, transcendentals=0)


def row_call(kernel, inputs, vectors, outs, sums, name):
    rows, width = inputs[0].shape
    block = pl.BlockSpec((ROW_BLOCK, width), lambda i: (i, 0))
    whole = pl.BlockSpec((1, width), lambda i: (0, 0))
    return pl.pallas_call(
        kernel,
        grid=(rows // ROW_BLOCK,),
        in_specs=[block] * len(inputs) + [whole] * len(vectors),
        out_specs=[block] * len(outs) + [whole] * sums,
        out_shape=[jax.ShapeDtypeStruct((rows, width), kind) for kind in outs]
        + [jax.ShapeDtypeStruct((1, width), F32)] * sums,
        compiler_params=pltpu.CompilerParams(vmem_limit_bytes=VMEM),
        cost_estimate=LIGHT,
        name=name,
    )(*inputs, *vectors)


def norm_kernel(x_ref, gain_ref, shift_ref, low_ref):
    hat, _ = norm_parts(x_ref[...].astype(F32))
    low_ref[...] = (hat * gain_ref[...] + shift_ref[...]).astype(BF16)


def norm_rows(inputs, gain, shift):
    return row_call(norm_kernel, [inputs], [gain, shift], [BF16], 0, "norm_rows")[0]


def add_norm_kernel(x_ref, own_ref, other_ref, gain_ref, shift_ref, sum_ref, low_ref):
    total = (
        x_ref[...].astype(F32) + own_ref[...].astype(F32) + other_ref[...].astype(F32)
    )
    sum_ref[...] = total
    hat, _ = norm_parts(total)
    low_ref[...] = (hat * gain_ref[...] + shift_ref[...]).astype(BF16)


def add_norm(inputs, own, other, gain, shift):
    return row_call(
        add_norm_kernel, [inputs, own, other], [gain, shift], [F32, BF16], 0, "add_norm"
    )


def add_sums(first, gain_out, shift_out, cotangent, hat):
    @pl.when(first)
    def _():
        gain_out[...] = jnp.zeros_like(gain_out)
        shift_out[...] = jnp.zeros_like(shift_out)

    gain_out[...] += jnp.sum(cotangent * hat, 0, keepdims=True)
    shift_out[...] += jnp.sum(cotangent, 0, keepdims=True)


def last_norm_kernel(
    x_ref, own_ref, other_ref, cot_ref, gain_ref, shift_ref, y_ref, d_ref, low_ref, dg_ref, ds_ref
):
    total = (
        x_ref[...].astype(F32) + own_ref[...].astype(F32) + other_ref[...].astype(F32)
    )
    hat, scale = norm_parts(total)
    y_ref[...] = (hat * gain_ref[...] + shift_ref[...]).astype(BF16)
    cotangent = cot_ref[...].astype(F32)
    d_total = norm_pull(hat, scale, gain_ref[...], cotangent)
    d_ref[...] = d_total
    low_ref[...] = d_total.astype(BF16)
    add_sums(pl.program_id(0) == 0, dg_ref, ds_ref, cotangent, hat)


def last_norm(inputs, own, other, cotangent, gain, shift):
    return row_call(
        last_norm_kernel,
        [inputs, own, other, cotangent],
        [gain, shift],
        [BF16, F32, BF16],
        2,
        "last_norm",
    )


def norm_back_kernel(residual, low, *refs):
    x_ref, own_ref, other_ref = refs[:3]
    refs = refs[3:]
    if residual:
        res_ref, refs = refs[0], refs[1:]
    gain_ref, refs = refs[0], refs[1:]
    hat, scale = norm_parts(x_ref[...].astype(F32))
    cotangent = own_ref[...].astype(F32) + other_ref[...].astype(F32)
    d_total = norm_pull(hat, scale, gain_ref[...], cotangent)
    if residual:
        d_total = d_total + res_ref[...]
    refs[0][...] = d_total.astype(refs[0].dtype)
    if low:
        refs[1][...] = d_total.astype(BF16)
    add_sums(pl.program_id(0) == 0, refs[-2], refs[-1], cotangent, hat)


def norm_back_rows(inputs, own, other, gain, residual, kinds):
    return row_call(
        functools.partial(norm_back_kernel, residual is not None, len(kinds) > 1),
        [inputs, own, other] + ([] if residual is None else [residual]),
        [gain],
        kinds,
        2,
        "norm_back",
    )


def chip_attend_kernel(causal, q_ref, k_ref, v_ref, qa_ref, ka_ref, o_ref, lse_ref):
    rows = q_ref.shape[0]
    block = 256
    low_half = lax.broadcasted_iota(jnp.int32, (1, LANES), 1) < HEAD_DIM
    for start in range(0, rows, block):
        keys = start + block if causal else k_ref.shape[0]
        query = q_ref[pl.ds(start, block), :] * BF16(SCALE)
        query_mark = qa_ref[pl.ds(start, block), :]
        key_block = k_ref[:keys, :]
        key_mark = ka_ref[:keys, :]
        values = v_ref[:keys, :]
        halves = []
        lses = []
        for head in range(2):
            keep = low_half if head == 0 else jnp.logical_not(low_half)
            scores = mxu(
                jnp.where(keep, query, query_mark), jnp.where(keep, key_block, key_mark), NT
            )
            if causal:
                scores = jnp.where(
                    lax.broadcasted_iota(jnp.int32, (block, keys), 1)
                    <= start + lax.broadcasted_iota(jnp.int32, (block, keys), 0),
                    scores,
                    NEG,
                )
            top = jnp.max(scores, -1, keepdims=True)
            weights = jnp.exp(scores - top)
            total = jnp.sum(weights, -1, keepdims=True)
            mixed = mxu(weights.astype(BF16), values, NN)
            halves.append(mixed / total)
            lses.append(top + jnp.log(total))
        o_ref[pl.ds(start, block), :] = jnp.where(low_half, halves[0], halves[1]).astype(BF16)
        turned = jnp.where(low_half, lses[0], lses[1]).T
        lse_ref[0, 0:1, pl.ds(start, block)] = turned[0:1]
        lse_ref[0, 1:2, pl.ds(start, block)] = turned[HEAD_DIM : HEAD_DIM + 1]


def pair_spec(rows, stride, offset):
    return pl.BlockSpec((rows, LANES), lambda p: (0, stride * p + offset))


def chip_attend(queries, q_at, pairs, k_at, v_at, query_mark, key_mark, causal):
    rows = queries.shape[0]
    keys = pairs.shape[0]
    count = queries.shape[1] // LANES // q_at[0]
    return pl.pallas_call(
        functools.partial(chip_attend_kernel, causal),
        grid=(count,),
        in_specs=[
            pair_spec(rows, *q_at),
            pair_spec(keys, *k_at),
            pair_spec(keys, *v_at),
            pl.BlockSpec((rows, LANES), lambda p: (0, 0)),
            pl.BlockSpec((keys, LANES), lambda p: (0, 0)),
        ],
        out_specs=[
            pair_spec(rows, 1, 0),
            pl.BlockSpec((1, 2, rows), lambda p: (p, 0, 0)),
        ],
        out_shape=[
            jax.ShapeDtypeStruct((rows, count * LANES), BF16),
            jax.ShapeDtypeStruct((count, 2, rows), F32),
        ],
        compiler_params=pltpu.CompilerParams(vmem_limit_bytes=VMEM),
        cost_estimate=LIGHT,
        name="attend",
    )(queries, pairs, pairs, query_mark, key_mark)


def chip_attend_back_kernel(causal, fused, *refs):
    q_ref, k_ref, v_ref, qa_ref, ka_ref, lse_ref, o_ref, do_ref = refs[:8]
    outs, (dk_acc, dv_acc) = refs[8:-2], refs[-2:]
    rows = q_ref.shape[0]
    block = 256
    low_half = lax.broadcasted_iota(jnp.int32, (1, LANES), 1) < HEAD_DIM
    zero = jnp.zeros((), BF16)
    dk_acc[...] = jnp.zeros_like(dk_acc)
    dv_acc[...] = jnp.zeros_like(dv_acc)
    for start in range(0, rows, block):
        keys = start + block if causal else k_ref.shape[0]
        span = pl.ds(start, block)
        query = q_ref[span, :] * BF16(SCALE)
        query_mark = qa_ref[span, :]
        key_block = k_ref[:keys, :]
        key_mark = ka_ref[:keys, :]
        values = v_ref[:keys, :]
        d_out = do_ref[span, :]
        inner = (d_out.astype(F32) * o_ref[span, :].astype(F32)).T
        d_query = None
        for head in range(2):
            keep = low_half if head == 0 else jnp.logical_not(low_half)
            delta = jnp.sum(
                inner[head * HEAD_DIM : (head + 1) * HEAD_DIM], axis=0, keepdims=True
            )
            scores = mxu(
                jnp.where(keep, key_block, key_mark), jnp.where(keep, query, query_mark), NT
            )
            if causal:
                scores = jnp.where(
                    lax.broadcasted_iota(jnp.int32, (keys, block), 0)
                    <= start + lax.broadcasted_iota(jnp.int32, (keys, block), 1),
                    scores,
                    NEG,
                )
            probs = jnp.exp(scores - lse_ref[0, head : head + 1, span])
            own_out = jnp.where(keep, d_out, zero)
            d_probs = mxu(values, own_out, NT)
            d_scores = (probs * (d_probs - delta)).astype(BF16)
            dv_acc[:keys, :] += mxu(probs.astype(BF16), own_out, NN)
            dk_acc[:keys, :] += mxu(d_scores, jnp.where(keep, query, zero), NN)
            term = mxu(jnp.where(keep, key_block, zero), d_scores, TN)
            d_query = term if d_query is None else d_query + term
        outs[0][span, :LANES] = (d_query * SCALE).T.astype(BF16)
    if fused:
        outs[0][:, LANES : 2 * LANES] = dk_acc[...].astype(BF16)
        outs[0][:, 2 * LANES :] = dv_acc[...].astype(BF16)
    else:
        outs[1][:, :LANES] = dk_acc[...].astype(BF16)
        outs[1][:, LANES:] = dv_acc[...].astype(BF16)


def chip_attend_back(
    queries, q_at, pairs, k_at, v_at, query_mark, key_mark, causal, log_total, mixed, d_mixed, fused
):
    rows = queries.shape[0]
    keys = pairs.shape[0]
    count = mixed.shape[1] // LANES

    def out(rows, blocks):
        return (
            pl.BlockSpec((rows, blocks * LANES), lambda p: (0, p)),
            jax.ShapeDtypeStruct((rows, count * blocks * LANES), BF16),
        )

    outs = [out(rows, 3)] if fused else [out(rows, 1), out(keys, 2)]
    return pl.pallas_call(
        functools.partial(chip_attend_back_kernel, causal, fused),
        grid=(count,),
        in_specs=[
            pair_spec(rows, *q_at),
            pair_spec(keys, *k_at),
            pair_spec(keys, *v_at),
            pl.BlockSpec((rows, LANES), lambda p: (0, 0)),
            pl.BlockSpec((keys, LANES), lambda p: (0, 0)),
            pl.BlockSpec((1, 2, rows), lambda p: (p, 0, 0)),
            pair_spec(rows, 1, 0),
            pair_spec(rows, 1, 0),
        ],
        out_specs=[spec for spec, _ in outs],
        out_shape=[shape for _, shape in outs],
        scratch_shapes=[pltpu.VMEM((keys, LANES), F32), pltpu.VMEM((keys, LANES), F32)],
        compiler_params=pltpu.CompilerParams(vmem_limit_bytes=VMEM),
        cost_estimate=LIGHT,
        name="attend_back",
    )(queries, pairs, pairs, query_mark, key_mark, log_total, mixed, d_mixed)


def piece_kernel(kind, low, high, count, x_ref, *refs):
    if count == 1:
        order_ref, stack_ref, rest = refs[0], refs[1], refs[2:]
        weights = [stack_ref.at[order_ref[i]] for i in range(stack_ref.shape[0])]
    else:
        weights, rest = refs[:count], refs[count:]
    own = high - low
    total = None
    for i, ref in enumerate(weights):
        span = pl.ds(i * own, own)
        if kind == "columns":
            rest[-1][:, span] = mxu(x_ref[...], ref[:, low:high], NN).astype(BF16)
        elif kind == "gelu":
            inner = mxu(x_ref[...], ref[:, low:high], NN)
            below = 0.5 + 0.5 * lax.erf(inner * (0.5**0.5))
            rest[0][:, span] = (inner * below).astype(BF16)
            bell = jnp.exp(inner * inner * (-0.5)) * (0.5 / jnp.pi) ** 0.5
            rest[1][:, span] = (below + inner * bell).astype(BF16)
        elif kind == "rows":
            term = mxu(x_ref[:, span], ref[low:high, :], NN)
            total = term if total is None else total + term
        elif kind == "columns_back":
            term = mxu(x_ref[:, span], ref[:, low:high], NT)
            total = term if total is None else total + term
        elif kind == "rows_back":
            rest[-1][:, span] = mxu(x_ref[...], ref[low:high, :], NT).astype(BF16)
        elif kind == "rows_back_slope":
            term = mxu(x_ref[...], ref[low:high, :], NT)
            rest[-1][:, span] = (term * rest[0][:, span].astype(F32)).astype(BF16)
    if total is not None:
        rest[-1][...] = total.astype(BF16)


def piece_product(kind, rows_in, pieces, low, high, slope=None, block=512):
    rows, depth = rows_in.shape
    stacked = len(pieces) == 2
    shape = pieces[1].shape[1:] if stacked else pieces[0].shape
    all_own = 4 * (high - low)
    width = {
        "columns": all_own,
        "gelu": all_own,
        "rows": shape[1],
        "columns_back": shape[0],
        "rows_back": all_own,
        "rows_back_slope": all_own,
    }[kind]
    outs = 2 if kind == "gelu" else 1
    out = pl.BlockSpec((block, width), lambda i: (i, 0))
    results = pl.pallas_call(
        functools.partial(piece_kernel, kind, low, high, 1 if stacked else len(pieces)),
        grid=(rows // block,),
        in_specs=[pl.BlockSpec((block, depth), lambda i: (i, 0))]
        + (
            [
                pl.BlockSpec(memory_space=pltpu.SMEM),
                pl.BlockSpec(pieces[1].shape, lambda i: (0, 0, 0)),
            ]
            if stacked
            else [pl.BlockSpec(piece.shape, lambda i: (0, 0)) for piece in pieces]
        )
        + ([] if slope is None else [out]),
        out_specs=[out] * outs,
        out_shape=[jax.ShapeDtypeStruct((rows, width), BF16)] * outs,
        compiler_params=pltpu.CompilerParams(vmem_limit_bytes=VMEM),
        cost_estimate=LIGHT,
        name="product_" + kind,
    )(rows_in, *pieces, *([] if slope is None else [slope]))
    return results if outs > 1 else results[0]


def weight_kernel(count, *refs):
    out_ref = refs[-1]
    at = 0
    for i in range(count):
        own = refs[i].shape[1]
        out_ref[pl.ds(at, own), :] = mxu(refs[i][...], refs[count + i][...], TN).astype(BF16)
        at += own


def weight_grads(pairs, part):
    rows, width = pairs[0][1].shape
    owns = [hidden.shape[1] // 4 for hidden, _ in pairs]
    return pl.pallas_call(
        functools.partial(weight_kernel, len(pairs)),
        grid=(2,),
        in_specs=[
            pl.BlockSpec((rows, own), lambda i: (0, 2 * part + i)) for own in owns
        ]
        + [pl.BlockSpec((rows, width), lambda i: (0, 0)) for _ in pairs],
        out_specs=pl.BlockSpec((sum(owns), width), lambda i: (i, 0)),
        out_shape=jax.ShapeDtypeStruct((2 * sum(owns), width), BF16),
        compiler_params=pltpu.CompilerParams(vmem_limit_bytes=VMEM),
        cost_estimate=LIGHT,
        name="weight_grads",
    )(*[hidden for hidden, _ in pairs], *[wide for _, wide in pairs])


CROSS = ("seq", "tensor")


class Chip:
    def __init__(self):
        self.core = lax.axis_index("seq")
        self.place = lax.axis_index("tensor")
        self.line = lax.axis_index("dp")
        self.first = [(i, i ^ 1) for i in range(4)] + [(4 + i, 4 + (i ^ 2)) for i in range(4)]
        self.second = [(i, i ^ 2) for i in range(4)] + [(4 + i, 4 + (i ^ 1)) for i in range(4)]

    def other(self, block):
        return lax.ppermute(block, "seq", swap_pairs(2, 1))

    def gather(self, block):
        near = lax.ppermute(block, CROSS, self.first)
        side = lax.ppermute(block, CROSS, self.second)
        far = lax.ppermute(side, CROSS, self.first)
        return [block, side, near, far]

    def ordered(self, own, other, index):
        first = index == 0
        return jnp.concatenate([jnp.where(first, own, other), jnp.where(first, other, own)], 0)

    def swap_start(self, blocks):
        near_bit = 1 + self.core

        def to(bits):
            return lax.dynamic_index_in_dim(blocks, jnp.bitwise_xor(self.place, bits), 0)

        cuts = lax.optimization_barrier((to(0), to(near_bit), to(3 - near_bit), to(3)))
        far = lax.ppermute(cuts[3], "tensor", swap_pairs(4, 3))
        return cuts[0], self.send_near(cuts[1]), self.send_side(cuts[2]), far

    def swap_end(self, parts):
        own, near, side, far = parts
        low, high = lax.rem(self.place, 2), self.place // 2
        first = self.core == 0
        beside, across = jnp.where(first, near, side), jnp.where(first, side, near)
        blocks = self.ordered(self.ordered(own, beside, low), self.ordered(across, far, low), high)
        return blocks.reshape(-1, own.shape[2]) if own.ndim == 3 else blocks

    def swap_rows(self, block):
        return self.swap_end(self.swap_start(block))

    def both_cores(self, rows):
        return self.ordered(rows, self.other(rows), self.core)

    def from_slot(self, rows):
        half = rows.shape[0] // 2
        own = lax.dynamic_slice_in_dim(rows, self.core * half, half, 0)
        rows = self.swap_rows(own.reshape(4, half // 4, -1))
        return rows.reshape(4, half // 4, -1)

    def send_near(self, block):
        return lax.ppermute(block, CROSS, self.first)

    def send_side(self, block):
        return lax.ppermute(block, CROSS, self.second)

    def along(self, block, bit):
        return lax.ppermute(block, "dp", swap_pairs(4, bit))


def add_low(left, right):
    return (left.astype(F32) + right.astype(F32)).astype(BF16)


def chip_local(
    source,
    target,
    out_grad,
    source_segments,
    target_segments,
    enc_gain,
    enc_shift,
    enc_qkv,
    enc_proj,
    enc_up,
    enc_down,
    dec_gain,
    dec_shift,
    dec_self_qkv,
    dec_self_proj,
    dec_cross_q,
    dec_cross_kv,
    dec_cross_proj,
    dec_up,
    dec_down,
):
    chip = Chip()
    core = chip.core
    tie = lax.optimization_barrier

    def own_columns(weight):
        part = weight.shape[-1] // 2
        cut = lax.dynamic_slice_in_dim(weight, core * part, part, weight.ndim - 1)
        return cut.reshape(weight.shape[0], -1)

    def own_rows(weight):
        part = weight.shape[0] // 2
        return lax.dynamic_slice_in_dim(weight, core * part, part, 0)

    def pin(value, *others):
        return tie((value,) + others)[0]

    bundles = [
        own_columns(enc_qkv),
        own_columns(dec_self_qkv),
        jnp.concatenate([own_rows(enc_proj), own_rows(dec_self_proj), own_rows(dec_cross_proj)], 0),
        jnp.concatenate([own_columns(dec_cross_q), own_columns(dec_cross_kv)], 1),
        own_rows(dec_down),
    ]
    near_bit = 1 + core
    order = jnp.bitwise_xor(
        chip.place, jnp.stack([0 * core, 3 - near_bit, near_bit, 0 * core + 3])
    ).astype(jnp.int32)

    def all_groups(own):
        return [order, lax.all_gather(own, "tensor", axis=0)]

    inner = enc_up.shape[1] // 2
    pieces = [None] * len(bundles)

    def launch(index, *after):
        own = pin(bundles[index], *after)
        pieces[index] = [own, chip.send_side(own), chip.send_near(own)]
        return pieces[index][1]

    def relay(index, value):
        side, near, value = tie((pieces[index][1], pieces[index][2], value))
        pieces[index][1:] = [side, near]
        pieces[index].append(chip.send_near(side))
        return value

    def arrived(index, value):
        tied = tie(tuple(pieces[index]) + (value,))
        pieces[index] = list(tied[:-1])
        return tied[-1]

    def enc(index):
        return enc_gain[index : index + 1], enc_shift[index : index + 1]

    def dec(index):
        return dec_gain[index : index + 1], dec_shift[index : index + 1]

    def part_rows(rows_in, weight, low, high):
        own = piece_product("rows", rows_in, weight, low, high)
        return own, chip.other(own)

    def part_back(grad, weight, low, high):
        own = piece_product("columns_back", grad, weight, low, high)
        return own, chip.other(own)

    fused_at = ((3, 0), (3, 1), (3, 2))

    def attend_self(qkv, marks, causal):
        return chip_attend(
            qkv, fused_at[0], qkv, fused_at[1], fused_at[2], marks[0], marks[1], causal
        )

    launch(0)
    swapped = arrived(0, chip.swap_rows(relay(0, source)))
    launch(1, swapped)
    x_source = chip.both_cores(swapped)
    sent_target = chip.swap_start(pin(target, swapped))
    source_ids = lax.dynamic_index_in_dim(source_segments, chip.place, 0, keepdims=False)
    target_ids = lax.dynamic_index_in_dim(target_segments, chip.place, 0, keepdims=False)
    ids = jnp.arange(LANES, dtype=jnp.int32)[None] % HEAD_DIM
    counted = ids < IDS
    source_query = jnp.where(source_ids[:, None] == ids, NEG, 0.0).astype(BF16)
    target_query = jnp.where(target_ids[:, None] == ids, NEG, 0.0).astype(BF16)
    source_key = ((source_ids[:, None] != ids) & counted).astype(BF16)
    target_key = ((target_ids[:, None] != ids) & counted).astype(BF16)
    rows_a = norm_rows(x_source, *enc(0))
    rows_a = pin(rows_a, source_query, source_key)
    qkv_a = piece_product("columns", rows_a, pieces[0], 0, bundles[0].shape[1])
    launch(2, qkv_a)
    mixed_a, total_a = attend_self(qkv_a, (source_query, source_key), False)
    mixed_a, sent_target = tie((relay(1, mixed_a), sent_target))
    x_target = chip.both_cores(chip.swap_end(sent_target))
    w_enc_up = all_groups(pin(own_columns(enc_up), mixed_a))
    rows_c = norm_rows(pin(x_target, target_query, target_key), *dec(0))
    rows_c = arrived(1, rows_c)
    qkv_c = piece_product("columns", rows_c, pieces[1], 0, bundles[1].shape[1])
    qkv_c = relay(2, qkv_c)
    w_enc_down = all_groups(pin(own_rows(enc_down), qkv_c))
    mixed_c, total_c = attend_self(qkv_c, (target_query, target_key), True)
    proj_rows = bundles[2].shape[0] // 3
    mixed_c, mixed_a = tie((arrived(2, mixed_c), mixed_a))
    launch(3, mixed_c)
    w_dec_up = all_groups(pin(own_columns(dec_up), mixed_c))
    own_a, other_a = part_rows(mixed_a, pieces[2], 0, proj_rows)
    own_c, other_c = part_rows(mixed_c, pieces[2], proj_rows, 2 * proj_rows)
    other_a, other_c = tie((other_a, other_c, own_a, own_c))[:2]
    hidden, rows_b = add_norm(x_source, own_a, other_a, *enc(1))
    after_self, rows_e = add_norm(x_target, own_c, other_c, *dec(1))
    rows_b = pin(rows_b, rows_e)
    active_b, slope_b = piece_product("gelu", rows_b, w_enc_up, 0, inner, block=256)
    active_b = relay(3, active_b)
    encoded, rows_m = add_norm(hidden, *part_rows(active_b, w_enc_down, 0, inner), *enc(2))
    rows_m, rows_e = tie((arrived(3, rows_m), rows_e))
    launch(4, rows_m)
    head_width = dec_cross_q.shape[1] // 2
    pairs_m = piece_product("columns", rows_m, pieces[3], head_width, 3 * head_width)
    query_e = piece_product("columns", rows_e, pieces[3], 0, head_width)
    query_e = pin(query_e, pairs_m)
    mixed_e, total_e = chip_attend(
        query_e, (1, 0), pairs_m, (2, 0), (2, 1), target_query, source_key, False
    )
    mixed_e = relay(4, mixed_e)
    after_cross, rows_f = add_norm(
        after_self, *part_rows(mixed_e, pieces[2], 2 * proj_rows, 3 * proj_rows), *dec(2)
    )
    sent_grad = chip.swap_start(pin(out_grad, rows_f))
    active_f, slope_f = piece_product("gelu", rows_f, w_dec_up, 0, inner, block=256)
    active_f, sent_grad = tie((arrived(4, active_f), sent_grad))
    cotangent = chip.both_cores(chip.swap_end(sent_grad))
    w_dec_down = pieces[4]
    decoded, d_final, low_final, gain_d3, shift_d3 = last_norm(
        after_cross, *part_rows(active_f, w_dec_down, 0, inner), cotangent, *dec(3)
    )


    low_bit = lax.rem(chip.line, 2)
    high_bit = chip.line // 2

    def here(value, step, *args):
        args, value = tie((args, value))
        *result, sent = step(*args)
        return pin(value, result[1], *sent), result

    def to_side(came, kept):
        half = kept.shape[0] // 2
        sent = add_low(kept[half:], came[half:])
        return chip.send_side(sent), add_low(kept[:half], came[:half]), [sent]

    def to_line(*states):
        def cut(bits):
            parts = []
            for came, kept in states:
                quarter = kept.shape[0] // 4
                at = jnp.bitwise_xor(chip.line, bits) * quarter
                parts.append(
                    add_low(
                        lax.dynamic_slice_in_dim(kept, at, quarter, 0),
                        lax.dynamic_slice_in_dim(came, at, quarter, 0),
                    )
                )
            return jnp.concatenate(parts, 0)

        sent = [cut(bits) for bits in (3, 2, 1)]
        return [chip.along(part, bits) for part, bits in zip(sent, (3, 2, 1))], cut(0), sent

    def from_line(came, own):
        total = own.astype(F32)
        for block in came:
            total = total + block.astype(F32)
        own = total.astype(BF16)
        return [chip.along(own, bits) for bits in (3, 2, 1)], own, []

    def to_core(came, own):
        far, next_but_one, next_one = came
        first = chip.ordered(own, next_one, low_bit)
        second = chip.ordered(next_but_one, far, low_bit)
        return share(chip.ordered(first, second, high_bit))

    def share(whole):
        width = whole.shape[1] // 2
        sent = lax.dynamic_slice_in_dim(whole, (1 - core) * width, width, 1)
        own = lax.dynamic_slice_in_dim(whole, core * width, width, 1)
        return chip.other(sent), own

    def in_place(came, own):
        return chip.ordered(own[None], came[None], core)

    def sum_line(*states):
        total = jnp.concatenate([add_low(*state) for state in states], 0)
        return None, total, []

    def send_half(value, *pairs):
        sent = weight_grads(list(pairs), 1)
        return pin(value, sent), chip.send_near(sent)

    def keep_half(value, came, *pairs):
        first, value = tie((pairs[0], value))
        kept = weight_grads([first] + list(pairs[1:]), 0)
        return pin(value, kept), (came, kept)

    def ffn_back(low_out, slope, weight):
        return piece_product("rows_back_slope", low_out, weight, 0, inner, slope)

    low_send, near_fd = send_half(low_final, (active_f, low_final))
    d_inner_f = ffn_back(low_send, slope_f, w_dec_down)
    d_inner_f, near_fu = send_half(d_inner_f, (d_inner_f, rows_f))
    own = piece_product("columns_back", d_inner_f, w_dec_up, 0, inner)
    own, near_fd = tie((own, near_fd))
    other = chip.other(own)
    hold, keep_fd = keep_half(own, near_fd, (active_f, low_final))
    hold, side_fd = here(hold, to_side, *keep_fd)
    hold, keep_fu = keep_half(hold, near_fu, (d_inner_f, rows_f))
    d_cross, low_cross, gain_d2, shift_d2 = norm_back_rows(
        after_cross, own, pin(other, hold), dec(2)[0], d_final, [F32, BF16]
    )
    d_mixed = piece_product("rows_back", low_cross, pieces[2], 2 * proj_rows, 3 * proj_rows)
    d_mixed, side_fu = here(d_mixed, to_side, *keep_fu)
    d_query_e, d_pairs_m = chip_attend_back(
        query_e,
        (1, 0),
        pairs_m,
        (2, 0),
        (2, 1),
        target_query,
        source_key,
        False,
        total_e,
        mixed_e,
        d_mixed,
        False,
    )
    d_pairs_m, (_, total_f) = here(d_pairs_m, sum_line, side_fd, side_fu)
    sum_f = lax.psum(total_f, "dp")
    own_m, other_m = part_back(d_pairs_m, pieces[3], head_width, 3 * head_width)
    own_e, other_e = part_back(pin(d_query_e, own_m), pieces[3], 0, head_width)
    d_encoded, low_encoded, gain_e2, shift_e2 = norm_back_rows(
        encoded, own_m, pin(other_m, own_e), enc(2)[0], None, [F32, BF16]
    )
    low_send, near_bd = send_half(low_encoded, (active_b, low_encoded))
    d_inner_b = ffn_back(low_send, slope_b, w_enc_down)
    d_inner_b, near_bu = send_half(d_inner_b, (d_inner_b, rows_b))
    own = piece_product("columns_back", d_inner_b, w_enc_up, 0, inner)
    own, near_bd, other_e = tie((own, near_bd, other_e))
    other = chip.other(own)
    hold, keep_bd = keep_half(own, near_bd, (active_b, low_encoded))
    hold, side_bd = here(hold, to_side, *keep_bd)
    hold, keep_bu = keep_half(hold, near_bu, (d_inner_b, rows_b))
    d_hidden, low_hidden, gain_e1, shift_e1 = norm_back_rows(
        hidden, own, pin(other, hold), enc(1)[0], d_encoded, [F32, BF16]
    )
    pairs_x = ((mixed_e, low_cross), (d_query_e, rows_e), (d_pairs_m, rows_m))
    own_e, side_bu = here(pin(own_e, low_hidden), to_side, *keep_bu)
    pairs_x = tie((pairs_x, own_e))[0]
    own_e, near_x = send_half(own_e, *pairs_x)
    own_e, keep_x = keep_half(own_e, near_x, *pairs_x)
    d_self, low_self, gain_d1, shift_d1 = norm_back_rows(
        after_self, own_e, other_e, dec(1)[0], d_cross, [F32, BF16]
    )

    def self_back(d_mixed, qkv, marks, causal, totals, mixed):
        (d_qkv,) = chip_attend_back(
            qkv,
            fused_at[0],
            qkv,
            fused_at[1],
            fused_at[2],
            marks[0],
            marks[1],
            causal,
            totals,
            mixed,
            d_mixed,
            True,
        )
        return d_qkv

    d_mixed = piece_product("rows_back", low_self, pieces[2], proj_rows, 2 * proj_rows)
    d_mixed, (_, total_b) = here(d_mixed, sum_line, side_bd, side_bu)
    d_qkv_c = self_back(d_mixed, qkv_c, (target_query, target_key), True, total_c, mixed_c)
    d_qkv_c, sum_f, total_b = tie((d_qkv_c, sum_f, total_b))
    sum_b = lax.psum(total_b, "dp")
    d_qkv_c, side_x = here(d_qkv_c, to_side, *keep_x)
    pairs_c = ((mixed_c, low_self), (d_qkv_c, rows_c))
    d_qkv_c, near_c = send_half(d_qkv_c, *pairs_c)
    own_c = piece_product("columns_back", d_qkv_c, pieces[1], 0, 3 * head_width)
    own_c, keep_c = keep_half(own_c, near_c, *pairs_c)
    low_hidden, decoded = tie((low_hidden, decoded, own_c))[:2]
    decoded = chip.from_slot(decoded)
    d_mixed = piece_product("rows_back", low_hidden, pieces[2], 0, proj_rows)
    d_mixed, side_c = here(d_mixed, to_side, *keep_c)
    d_mixed, decoded = tie((d_mixed, decoded))
    d_qkv_a = self_back(d_mixed, qkv_a, (source_query, source_key), False, total_a, mixed_a)
    pairs_a = ((mixed_a, low_hidden), (d_qkv_a, rows_a))
    d_qkv_a, near_a = send_half(d_qkv_a, *pairs_a)
    d_qkv_a, (_, total_xc) = here(d_qkv_a, sum_line, side_x, side_c)
    d_qkv_a, sum_b, total_xc = tie((d_qkv_a, sum_b, total_xc))
    sum_xc = lax.psum(total_xc, "dp")
    own_a, other_a = part_back(d_qkv_a, pieces[0], 0, 3 * head_width)
    other_c = chip.other(pin(own_c, own_a))
    own_a, keep_a = keep_half(own_a, near_a, *pairs_a)
    source_grad, gain_e0, shift_e0 = norm_back_rows(
        x_source, own_a, other_a, enc(0)[0], d_hidden, [BF16]
    )
    own_c = pin(own_c, source_grad)
    own_c, side_a = here(own_c, to_side, *keep_a)
    target_grad, gain_d0, shift_d0 = norm_back_rows(
        x_target, own_c, other_c, dec(0)[0], d_self, [BF16]
    )
    gain_d0, line_a = here(gain_d0, to_line, side_a)
    source_grad = chip.from_slot(pin(source_grad, gain_d0))
    target_grad = chip.from_slot(pin(target_grad, gain_d0))
    line_a, sum_xc = tie((line_a, sum_xc))
    sum_f, sum_b = tie((sum_f, sum_b, gain_d0))[:2]

    norms = jnp.concatenate(
        [
            gain_e0,
            gain_e1,
            gain_e2,
            shift_e0,
            shift_e1,
            shift_e2,
            gain_d0,
            gain_d1,
            gain_d2,
            gain_d3,
            shift_d0,
            shift_d1,
            shift_d2,
            shift_d3,
        ],
        0,
    )
    part = norms.shape[1] // 2
    norms = lax.dynamic_slice_in_dim(norms, core * part, part, 1)
    norms = norms + chip.send_near(norms)
    norms = norms + chip.send_side(norms)
    norms = norms + chip.along(norms, 1)
    norms = norms + chip.along(norms, 2)
    line_a = from_line(*line_a)[:2]
    line_a = to_core(*line_a)

    def wide(block, blocks):
        cores, rows, width = block.shape
        block = block.reshape(cores, blocks, rows // blocks, width)
        return jnp.transpose(block, (3, 1, 0, 2)).reshape(width, blocks, -1).astype(F32)

    def tall(block):
        return block.reshape(-1, block.shape[2]).astype(F32)

    n = proj_rows
    done_f, done_b = in_place(*share(sum_f)), in_place(*share(sum_b))
    done_xc, done_a = in_place(*share(sum_xc)), in_place(*line_a)
    done_x, done_c = done_xc[:, : 4 * n], done_xc[:, 4 * n :]
    source_grad, target_grad = source_grad.astype(F32), target_grad.astype(F32)
    hid = done_f.shape[1] // 2
    return (
        decoded,
        source_grad,
        target_grad,
        norms[0:3],
        norms[3:6],
        wide(done_a[:, n:], 3),
        tall(done_a[:, :n]),
        wide(done_b[:, inner:], 1)[:, 0],
        tall(done_b[:, :inner]),
        norms[6:10],
        norms[10:14],
        wide(done_c[:, n:], 3),
        tall(done_c[:, :n]),
        wide(done_x[:, n : n + head_width], 1)[:, 0],
        wide(done_x[:, n + head_width :], 2),
        tall(done_x[:, :n]),
        wide(done_f[:, hid:], 1)[:, 0],
        tall(done_f[:, :hid]),
    )


def solution(mesh):
    rows = P("dp", ("seq", "tensor"), None)
    segments = P("dp", None)
    shape = dict(mesh.shape)
    chips = shape["dp"] == 4 and shape["seq"] == 2 and shape["tensor"] == 4
    return jax.shard_map(
        chip_local if chips else local,
        mesh=mesh,
        in_specs=(
            rows,
            rows,
            rows,
            segments,
            segments,
            P(),
            P(),
            P(None, None, "tensor"),
            P("tensor", None),
            P(None, "tensor"),
            P("tensor", None),
            P(),
            P(),
            P(None, None, "tensor"),
            P("tensor", None),
            P(None, "tensor"),
            P(None, None, "tensor"),
            P("tensor", None),
            P(None, "tensor"),
            P("tensor", None),
        ),
        out_specs=(
            rows,
            rows,
            rows,
            P(None, "seq"),
            P(None, "seq"),
            P("seq", None, "tensor"),
            P("tensor", "seq"),
            P("seq", "tensor"),
            P("tensor", "seq"),
            P(None, "seq"),
            P(None, "seq"),
            P("seq", None, "tensor"),
            P("tensor", "seq"),
            P("seq", "tensor"),
            P("seq", None, "tensor"),
            P("tensor", "seq"),
            P("seq", "tensor"),
            P("tensor", "seq"),
        ),
        check_vma=False,
    )
```

```python
import functools

import jax
import jax.numpy as jnp
from jax import lax
from jax.experimental import pallas as pl
from jax.experimental.pallas import tpu as pltpu
from jax.sharding import PartitionSpec as P

HEAD_DIM = 64
LANES = 128
IDS = 9
EPS = 1e-05
NEG = -1e30
SCALE = HEAD_DIM ** (-0.5)
F32 = jnp.float32
BF16 = jnp.bfloat16
NT = (((1,), (1,)), ((), ()))
NN = (((1,), (0,)), ((), ()))
TN = (((0,), (0,)), ((), ()))


def mxu(left, right, dims):
    return lax.dot_general(left, right, dims, preferred_element_type=F32)


def layer_norm(inputs, norm_gain, norm_shift):
    row_mean = jnp.mean(inputs, -1, keepdims=True)
    centred = inputs - row_mean
    spread = jnp.mean(centred * centred, -1, keepdims=True)
    return centred * lax.rsqrt(spread + EPS) * norm_gain + norm_shift


def exact_gelu(inputs):
    return jax.nn.gelu(inputs, approximate=False)


def norm_back(inputs, norm_gain, norm_shift, cotangent):
    _, pullback = jax.vjp(layer_norm, inputs, norm_gain, norm_shift)
    return pullback(cotangent)


def project(rows, weight):
    return mxu(rows, weight, NN)


def back_project(grad, weight):
    return mxu(grad, weight, NT)


def weight_grad(rows, grad):
    return mxu(rows, grad, TN).astype(BF16)


def attend_kernel(causal, first_ref, q_ref, k_ref, v_ref, qa_ref, ka_ref, o_ref, lse_ref):
    rows = q_ref.shape[0]
    keys = k_ref.shape[0]
    block = min(rows, 256)
    low_half = lax.broadcasted_iota(jnp.int32, (1, LANES), 1) < HEAD_DIM
    key_block = k_ref[...]
    key_mark = ka_ref[...]
    values = v_ref[...]
    for start in range(0, rows, block):
        query = q_ref[pl.ds(start, block), :] * BF16(SCALE)
        query_mark = qa_ref[pl.ds(start, block), :]
        halves = []
        lses = []
        for head in range(2):
            keep = low_half if head == 0 else jnp.logical_not(low_half)
            scores = mxu(
                jnp.where(keep, query, query_mark), jnp.where(keep, key_block, key_mark), NT
            )
            if causal:
                place = (
                    first_ref[0] + start + lax.broadcasted_iota(jnp.int32, (block, keys), 0)
                )
                scores = jnp.where(
                    lax.broadcasted_iota(jnp.int32, (block, keys), 1) <= place, scores, NEG
                )
            top = jnp.max(scores, -1, keepdims=True)
            weights = jnp.exp(scores - top)
            total = jnp.sum(weights, -1, keepdims=True)
            mixed = mxu(weights.astype(BF16), values, NN)
            halves.append(mixed / total)
            lses.append(top + jnp.log(total))
        o_ref[pl.ds(start, block), :] = jnp.where(low_half, halves[0], halves[1]).astype(BF16)
        both = jnp.where(low_half, lses[0], lses[1])
        turned = both.T
        lse_ref[0, 0:1, pl.ds(start, block)] = turned[0:1]
        lse_ref[0, 1:2, pl.ds(start, block)] = turned[HEAD_DIM : HEAD_DIM + 1]


def attend(queries, keys, values, query_mark, key_mark, first_row, causal):
    rows, width = queries.shape
    key_rows = keys.shape[0]
    pairs = width // LANES
    return pl.pallas_call(
        functools.partial(attend_kernel, causal),
        grid_spec=pltpu.PrefetchScalarGridSpec(
            num_scalar_prefetch=1,
            grid=(pairs,),
            in_specs=[
                pl.BlockSpec((rows, LANES), lambda p, first: (0, p)),
                pl.BlockSpec((key_rows, LANES), lambda p, first: (0, p)),
                pl.BlockSpec((key_rows, LANES), lambda p, first: (0, p)),
                pl.BlockSpec((rows, LANES), lambda p, first: (0, 0)),
                pl.BlockSpec((key_rows, LANES), lambda p, first: (0, 0)),
            ],
            out_specs=[
                pl.BlockSpec((rows, LANES), lambda p, first: (0, p)),
                pl.BlockSpec((1, 2, rows), lambda p, first: (p, 0, 0)),
            ],
        ),
        out_shape=[
            jax.ShapeDtypeStruct((rows, width), BF16),
            jax.ShapeDtypeStruct((pairs, 2, rows), F32),
        ],
        compiler_params=pltpu.CompilerParams(vmem_limit_bytes=40 << 20),
        cost_estimate=pl.CostEstimate(
            flops=4 * rows * key_rows * width * 2,
            bytes_accessed=4 * rows * width + 4 * key_rows * width,
            transcendentals=rows * key_rows * width // HEAD_DIM,
        ),
        name="attend",
    )(first_row, queries, keys, values, query_mark, key_mark)


def attend_back_kernel(
    causal,
    first_ref,
    q_ref,
    k_ref,
    v_ref,
    qa_ref,
    ka_ref,
    lse_ref,
    o_ref,
    do_ref,
    dq_ref,
    dk_ref,
    dv_ref,
    dk_acc,
    dv_acc,
):
    rows = q_ref.shape[0]
    keys = k_ref.shape[0]
    block = min(rows, 256)
    low_half = lax.broadcasted_iota(jnp.int32, (1, LANES), 1) < HEAD_DIM
    key_block = k_ref[...]
    key_mark = ka_ref[...]
    values = v_ref[...]
    zero = jnp.zeros((), BF16)
    dk_acc[...] = jnp.zeros_like(dk_acc)
    dv_acc[...] = jnp.zeros_like(dv_acc)
    for start in range(0, rows, block):
        span = pl.ds(start, block)
        query = q_ref[span, :] * BF16(SCALE)
        query_mark = qa_ref[span, :]
        d_out = do_ref[span, :]
        inner = (d_out.astype(F32) * o_ref[span, :].astype(F32)).T
        d_query = None
        for head in range(2):
            keep = low_half if head == 0 else jnp.logical_not(low_half)
            delta = jnp.sum(
                inner[head * HEAD_DIM : (head + 1) * HEAD_DIM], axis=0, keepdims=True
            )
            scores = mxu(
                jnp.where(keep, key_block, key_mark), jnp.where(keep, query, query_mark), NT
            )
            if causal:
                place = (
                    first_ref[0] + start + lax.broadcasted_iota(jnp.int32, (keys, block), 1)
                )
                scores = jnp.where(
                    lax.broadcasted_iota(jnp.int32, (keys, block), 0) <= place, scores, NEG
                )
            probs = jnp.exp(scores - lse_ref[0, head : head + 1, span])
            own_out = jnp.where(keep, d_out, zero)
            d_probs = mxu(values, own_out, NT)
            d_scores = (probs * (d_probs - delta)).astype(BF16)
            dv_acc[...] += mxu(probs.astype(BF16), own_out, NN)
            dk_acc[...] += mxu(d_scores, jnp.where(keep, query, zero), NN)
            term = mxu(jnp.where(keep, key_block, zero), d_scores, TN)
            d_query = term if d_query is None else d_query + term
        dq_ref[span, :] = (d_query * SCALE).T.astype(BF16)
    dk_ref[...] = dk_acc[...].astype(BF16)
    dv_ref[...] = dv_acc[...].astype(BF16)


def attend_back(
    queries, keys, values, query_mark, key_mark, first_row, causal, log_total, mixed, d_mixed
):
    rows, width = queries.shape
    key_rows = keys.shape[0]
    pairs = width // LANES
    row_spec = pl.BlockSpec((rows, LANES), lambda p, first: (0, p))
    key_spec = pl.BlockSpec((key_rows, LANES), lambda p, first: (0, p))
    return pl.pallas_call(
        functools.partial(attend_back_kernel, causal),
        grid_spec=pltpu.PrefetchScalarGridSpec(
            num_scalar_prefetch=1,
            grid=(pairs,),
            in_specs=[
                row_spec,
                key_spec,
                key_spec,
                pl.BlockSpec((rows, LANES), lambda p, first: (0, 0)),
                pl.BlockSpec((key_rows, LANES), lambda p, first: (0, 0)),
                pl.BlockSpec((1, 2, rows), lambda p, first: (p, 0, 0)),
                row_spec,
                row_spec,
            ],
            out_specs=[row_spec, key_spec, key_spec],
            scratch_shapes=[
                pltpu.VMEM((key_rows, LANES), F32),
                pltpu.VMEM((key_rows, LANES), F32),
            ],
        ),
        out_shape=[
            jax.ShapeDtypeStruct((rows, width), BF16),
            jax.ShapeDtypeStruct((key_rows, width), BF16),
            jax.ShapeDtypeStruct((key_rows, width), BF16),
        ],
        compiler_params=pltpu.CompilerParams(vmem_limit_bytes=40 << 20),
        cost_estimate=pl.CostEstimate(
            flops=10 * rows * key_rows * width * 2,
            bytes_accessed=8 * rows * width + 8 * key_rows * width,
            transcendentals=rows * key_rows * width // HEAD_DIM,
        ),
        name="attend_back",
    )(first_row, queries, keys, values, query_mark, key_mark, log_total, mixed, d_mixed)


class Layout:
    def __init__(self, slots):
        self.tensor = lax.axis_size("tensor")
        self.seq = lax.axis_size("seq")
        self.slots = slots
        self.spread = self.tensor // slots
        self.place = lax.axis_index("tensor")
        self.half = lax.axis_index("seq")
        self.row_groups = [
            [j * slots + u for u in range(slots)] for j in range(self.spread)
        ]
        self.slot_groups = [
            [j * slots + u for j in range(self.spread)] for u in range(slots)
        ]

    def to_slots(self, block):
        rows = lax.all_to_all(
            block, "tensor", 0, 1, axis_index_groups=self.row_groups, tiled=True
        )
        return rows.reshape(-1, block.shape[2])

    def from_slots(self, rows):
        block = rows.reshape(1, rows.shape[0], rows.shape[1])
        return lax.all_to_all(
            block, "tensor", 1, 0, axis_index_groups=self.row_groups, tiled=True
        )

    def gather_keys(self, rows):
        if self.spread > 1:
            rows = lax.all_gather(
                rows, "tensor", axis=0, axis_index_groups=self.slot_groups, tiled=True
            )
        return lax.all_gather(rows, "seq", axis=0, tiled=True)

    def scatter_keys(self, rows):
        rows = lax.psum_scatter(rows, "seq", scatter_dimension=0, tiled=True)
        if self.spread > 1:
            rows = lax.psum_scatter(
                rows,
                "tensor",
                scatter_dimension=0,
                axis_index_groups=self.slot_groups,
                tiled=True,
            )
        return rows

    def gather_weight(self, shard):
        part = shard.shape[0] // self.seq
        own = lax.dynamic_slice_in_dim(shard, self.half * part, part, 0)
        return lax.all_gather(own, ("tensor", "seq"), axis=0, tiled=True)

    def gather_columns(self, shard):
        depth, blocks, own = shard.shape
        whole = self.gather_weight(shard.reshape(depth, blocks * own))
        whole = whole.reshape(self.tensor, depth, blocks, own)
        return jnp.transpose(whole, (1, 2, 0, 3)).reshape(depth, blocks * self.tensor * own)

    def reduce_rows(self, gradient):
        rows, width = gradient.shape
        parts = gradient.reshape(self.tensor, rows // self.tensor, self.seq, width // self.seq)
        parts = jnp.transpose(parts, (2, 0, 1, 3)).reshape(
            self.seq * rows, width // self.seq
        )
        return self.reduce(parts)

    def reduce_columns(self, gradient, blocks):
        depth, width = gradient.shape
        own = width // blocks // self.tensor
        parts = gradient.reshape(self.seq, depth // self.seq, blocks, self.tensor, own)
        parts = jnp.transpose(parts, (0, 3, 1, 2, 4)).reshape(
            self.seq * self.tensor * depth // self.seq, blocks * own
        )
        return self.reduce(parts).reshape(depth // self.seq, blocks, own)

    def reduce(self, parts):
        own = lax.psum_scatter(parts, ("seq", "tensor"), scatter_dimension=0, tiled=True)
        return lax.psum(own, "dp").astype(F32)


def local(
    source,
    target,
    out_grad,
    source_segments,
    target_segments,
    enc_gain,
    enc_shift,
    enc_qkv,
    enc_proj,
    enc_up,
    enc_down,
    dec_gain,
    dec_shift,
    dec_self_qkv,
    dec_self_proj,
    dec_cross_q,
    dec_cross_kv,
    dec_cross_proj,
    dec_up,
    dec_down,
):
    width = source.shape[2]
    lay = Layout(source.shape[0])
    w_enc_qkv = lay.gather_columns(enc_qkv)
    w_self_qkv = lay.gather_columns(dec_self_qkv)
    w_enc_proj = lay.gather_weight(enc_proj)
    w_self_proj = lay.gather_weight(dec_self_proj)
    w_enc_up = lay.gather_columns(enc_up[:, None])
    w_enc_down = lay.gather_weight(enc_down)
    w_cross_q = lay.gather_columns(dec_cross_q[:, None])
    w_cross_kv = lay.gather_columns(dec_cross_kv)
    w_cross_proj = lay.gather_weight(dec_cross_proj)
    w_dec_up = lay.gather_columns(dec_up[:, None])
    w_dec_down = lay.gather_weight(dec_down)
    slot = lax.rem(lay.place, lay.slots)
    rows = source.shape[1] * lay.slots
    first_row = (lay.half * lay.spread + lay.place // lay.slots) * rows
    source_ids = lax.dynamic_index_in_dim(source_segments, slot, 0, keepdims=False)
    target_ids = lax.dynamic_index_in_dim(target_segments, slot, 0, keepdims=False)
    ids = jnp.arange(LANES, dtype=jnp.int32) % HEAD_DIM
    own_source = lax.dynamic_slice_in_dim(source_ids, first_row, rows, 0)
    own_target = lax.dynamic_slice_in_dim(target_ids, first_row, rows, 0)
    source_query = jnp.where(own_source[:, None] == ids[None], NEG, 0.0).astype(BF16)
    target_query = jnp.where(own_target[:, None] == ids[None], NEG, 0.0).astype(BF16)
    counted = ids[None] < IDS
    source_key = ((source_ids[:, None] != ids[None]) & counted).astype(BF16)
    target_key = ((target_ids[:, None] != ids[None]) & counted).astype(BF16)
    first = first_row[None].astype(jnp.int32)

    x_source = lay.to_slots(source).astype(F32)
    x_target = lay.to_slots(target).astype(F32)
    cotangent = lay.to_slots(out_grad).astype(F32)

    rows_a = layer_norm(x_source, enc_gain[0], enc_shift[0]).astype(BF16)
    qkv_a = project(rows_a, w_enc_qkv).astype(BF16)
    query_a = qkv_a[:, :width]
    pairs_a = lay.gather_keys(qkv_a[:, width:])
    mixed_a, total_a = attend(
        query_a, pairs_a[:, :width], pairs_a[:, width:], source_query, source_key, first, False
    )
    hidden = x_source + project(mixed_a, w_enc_proj)
    rows_c = layer_norm(x_target, dec_gain[0], dec_shift[0]).astype(BF16)
    qkv_c = project(rows_c, w_self_qkv).astype(BF16)
    query_c = qkv_c[:, :width]
    pairs_c = lay.gather_keys(qkv_c[:, width:])
    mixed_c, total_c = attend(
        query_c, pairs_c[:, :width], pairs_c[:, width:], target_query, target_key, first, True
    )
    after_self = x_target + project(mixed_c, w_self_proj)
    rows_b = layer_norm(hidden, enc_gain[1], enc_shift[1]).astype(BF16)
    inner_b = project(rows_b, w_enc_up)
    active_b = exact_gelu(inner_b).astype(BF16)
    encoded = hidden + project(active_b, w_enc_down)
    rows_m = layer_norm(encoded, enc_gain[2], enc_shift[2]).astype(BF16)
    pairs_m = lay.gather_keys(project(rows_m, w_cross_kv).astype(BF16))
    rows_e = layer_norm(after_self, dec_gain[1], dec_shift[1]).astype(BF16)
    query_e = project(rows_e, w_cross_q).astype(BF16)
    mixed_e, total_e = attend(
        query_e, pairs_m[:, :width], pairs_m[:, width:], target_query, source_key, first, False
    )
    after_cross = after_self + project(mixed_e, w_cross_proj)
    rows_f = layer_norm(after_cross, dec_gain[2], dec_shift[2]).astype(BF16)
    inner_f = project(rows_f, w_dec_up)
    active_f = exact_gelu(inner_f).astype(BF16)
    final_rows = after_cross + project(active_f, w_dec_down)
    decoded, final_back = jax.vjp(layer_norm, final_rows, dec_gain[3], dec_shift[3])

    d_final, dec_gain_three, dec_shift_three = final_back(cotangent)

    def ffn_back(d_out, rows_in, inner, active, weight_up, weight_down):
        d_low = d_out.astype(BF16)
        grad_down = lay.reduce_rows(weight_grad(active, d_low))
        d_active = back_project(d_low, weight_down)
        _, gelu_back = jax.vjp(exact_gelu, inner)
        d_inner = gelu_back(d_active)[0].astype(BF16)
        grad_up = lay.reduce_columns(weight_grad(rows_in, d_inner), 1)[:, 0]
        return back_project(d_inner, weight_up), grad_up, grad_down

    d_normed, grad_dec_up, grad_dec_down = ffn_back(
        d_final, rows_f, inner_f, active_f, w_dec_up, w_dec_down
    )
    d_input, dec_gain_two, dec_shift_two = norm_back(
        after_cross, dec_gain[2], dec_shift[2], d_normed
    )
    d_cross = d_final + d_input
    d_low = d_cross.astype(BF16)
    grad_cross_proj = lay.reduce_rows(weight_grad(mixed_e, d_low))
    d_mixed = back_project(d_low, w_cross_proj).astype(BF16)
    d_query, d_keys, d_values = attend_back(
        query_e,
        pairs_m[:, :width],
        pairs_m[:, width:],
        target_query,
        source_key,
        first,
        False,
        total_e,
        mixed_e,
        d_mixed,
    )
    d_pairs = lay.scatter_keys(jnp.concatenate([d_keys, d_values], 1))
    grad_cross_q = lay.reduce_columns(weight_grad(rows_e, d_query), 1)[:, 0]
    grad_cross_kv = lay.reduce_columns(weight_grad(rows_m, d_pairs), 2)
    d_normed = back_project(d_query, w_cross_q)
    d_memory = back_project(d_pairs, w_cross_kv)
    d_input, dec_gain_one, dec_shift_one = norm_back(
        after_self, dec_gain[1], dec_shift[1], d_normed
    )
    d_self = d_cross + d_input
    d_encoded, enc_gain_two, enc_shift_two = norm_back(encoded, enc_gain[2], enc_shift[2], d_memory)
    d_normed, grad_enc_up, grad_enc_down = ffn_back(
        d_encoded, rows_b, inner_b, active_b, w_enc_up, w_enc_down
    )
    d_input, enc_gain_one, enc_shift_one = norm_back(hidden, enc_gain[1], enc_shift[1], d_normed)
    d_hidden = d_encoded + d_input

    def self_back(d_out, rows_in, query, pairs, marks, causal, totals, mixed, w_qkv, w_proj):
        d_low = d_out.astype(BF16)
        grad_proj = lay.reduce_rows(weight_grad(mixed, d_low))
        d_mixed = back_project(d_low, w_proj).astype(BF16)
        d_query, d_keys, d_values = attend_back(
            query,
            pairs[:, :width],
            pairs[:, width:],
            marks[0],
            marks[1],
            first,
            causal,
            totals,
            mixed,
            d_mixed,
        )
        d_pairs = lay.scatter_keys(jnp.concatenate([d_keys, d_values], 1))
        d_qkv = jnp.concatenate([d_query, d_pairs], 1)
        grad_qkv = lay.reduce_columns(weight_grad(rows_in, d_qkv), 3)
        return back_project(d_qkv, w_qkv), grad_qkv, grad_proj

    d_normed, grad_self_qkv, grad_self_proj = self_back(
        d_self,
        rows_c,
        query_c,
        pairs_c,
        (target_query, target_key),
        True,
        total_c,
        mixed_c,
        w_self_qkv,
        w_self_proj,
    )
    d_input, dec_gain_zero, dec_shift_zero = norm_back(
        x_target, dec_gain[0], dec_shift[0], d_normed
    )
    target_grad = d_self + d_input
    d_normed, grad_enc_qkv, grad_enc_proj = self_back(
        d_hidden,
        rows_a,
        query_a,
        pairs_a,
        (source_query, source_key),
        False,
        total_a,
        mixed_a,
        w_enc_qkv,
        w_enc_proj,
    )
    d_input, enc_gain_zero, enc_shift_zero = norm_back(
        x_source, enc_gain[0], enc_shift[0], d_normed
    )
    source_grad = d_hidden + d_input
    norms = jnp.stack(
        [
            enc_gain_zero,
            enc_gain_one,
            enc_gain_two,
            enc_shift_zero,
            enc_shift_one,
            enc_shift_two,
            dec_gain_zero,
            dec_gain_one,
            dec_gain_two,
            dec_gain_three,
            dec_shift_zero,
            dec_shift_one,
            dec_shift_two,
            dec_shift_three,
        ]
    )
    part = width // lay.seq
    norms = lax.dynamic_slice_in_dim(
        lax.psum(norms, ("dp", "seq", "tensor")), lay.half * part, part, 1
    )
    return (
        lay.from_slots(decoded.astype(BF16)),
        lay.from_slots(source_grad.astype(BF16)).astype(F32),
        lay.from_slots(target_grad.astype(BF16)).astype(F32),
        norms[0:3],
        norms[3:6],
        grad_enc_qkv,
        grad_enc_proj,
        grad_enc_up,
        grad_enc_down,
        norms[6:10],
        norms[10:14],
        grad_self_qkv,
        grad_self_proj,
        grad_cross_q,
        grad_cross_kv,
        grad_cross_proj,
        grad_dec_up,
        grad_dec_down,
    )


def swap_pairs(count, bit):
    return [(i, i ^ bit) for i in range(count)]


def norm_parts(inputs):
    centred = inputs - jnp.mean(inputs, -1, keepdims=True)
    scale = lax.rsqrt(jnp.mean(centred * centred, -1, keepdims=True) + EPS)
    return centred * scale, scale


def norm_pull(hat, scale, gain, cotangent):
    tilted = cotangent * gain
    return scale * (
        tilted
        - jnp.mean(tilted, -1, keepdims=True)
        - hat * jnp.mean(tilted * hat, -1, keepdims=True)
    )


ROW_BLOCK = 256
VMEM = 56 << 20
LIGHT = pl.CostEstimate(flops=1 << 20, bytes_accessed=1 << 16, transcendentals=0)


def row_call(kernel, inputs, vectors, outs, sums, name):
    rows, width = inputs[0].shape
    block = pl.BlockSpec((ROW_BLOCK, width), lambda i: (i, 0))
    whole = pl.BlockSpec((1, width), lambda i: (0, 0))
    return pl.pallas_call(
        kernel,
        grid=(rows // ROW_BLOCK,),
        in_specs=[block] * len(inputs) + [whole] * len(vectors),
        out_specs=[block] * len(outs) + [whole] * sums,
        out_shape=[jax.ShapeDtypeStruct((rows, width), kind) for kind in outs]
        + [jax.ShapeDtypeStruct((1, width), F32)] * sums,
        compiler_params=pltpu.CompilerParams(vmem_limit_bytes=VMEM),
        cost_estimate=LIGHT,
        name=name,
    )(*inputs, *vectors)


def norm_kernel(x_ref, gain_ref, shift_ref, low_ref):
    hat, _ = norm_parts(x_ref[...].astype(F32))
    low_ref[...] = (hat * gain_ref[...] + shift_ref[...]).astype(BF16)


def norm_rows(inputs, gain, shift):
    return row_call(norm_kernel, [inputs], [gain, shift], [BF16], 0, "norm_rows")[0]


def add_norm_kernel(x_ref, own_ref, other_ref, gain_ref, shift_ref, sum_ref, low_ref):
    total = (
        x_ref[...].astype(F32) + own_ref[...].astype(F32) + other_ref[...].astype(F32)
    )
    sum_ref[...] = total
    hat, _ = norm_parts(total)
    low_ref[...] = (hat * gain_ref[...] + shift_ref[...]).astype(BF16)


def add_norm(inputs, own, other, gain, shift):
    return row_call(
        add_norm_kernel, [inputs, own, other], [gain, shift], [F32, BF16], 0, "add_norm"
    )


def add_sums(first, gain_out, shift_out, cotangent, hat):
    @pl.when(first)
    def _():
        gain_out[...] = jnp.zeros_like(gain_out)
        shift_out[...] = jnp.zeros_like(shift_out)

    gain_out[...] += jnp.sum(cotangent * hat, 0, keepdims=True)
    shift_out[...] += jnp.sum(cotangent, 0, keepdims=True)


def last_norm_kernel(
    x_ref, own_ref, other_ref, cot_ref, gain_ref, shift_ref, y_ref, d_ref, low_ref, dg_ref, ds_ref
):
    total = (
        x_ref[...].astype(F32) + own_ref[...].astype(F32) + other_ref[...].astype(F32)
    )
    hat, scale = norm_parts(total)
    y_ref[...] = (hat * gain_ref[...] + shift_ref[...]).astype(BF16)
    cotangent = cot_ref[...].astype(F32)
    d_total = norm_pull(hat, scale, gain_ref[...], cotangent)
    d_ref[...] = d_total
    low_ref[...] = d_total.astype(BF16)
    add_sums(pl.program_id(0) == 0, dg_ref, ds_ref, cotangent, hat)


def last_norm(inputs, own, other, cotangent, gain, shift):
    return row_call(
        last_norm_kernel,
        [inputs, own, other, cotangent],
        [gain, shift],
        [BF16, F32, BF16],
        2,
        "last_norm",
    )


def norm_back_kernel(residual, low, *refs):
    x_ref, own_ref, other_ref = refs[:3]
    refs = refs[3:]
    if residual:
        res_ref, refs = refs[0], refs[1:]
    gain_ref, refs = refs[0], refs[1:]
    hat, scale = norm_parts(x_ref[...].astype(F32))
    cotangent = own_ref[...].astype(F32) + other_ref[...].astype(F32)
    d_total = norm_pull(hat, scale, gain_ref[...], cotangent)
    if residual:
        d_total = d_total + res_ref[...]
    refs[0][...] = d_total.astype(refs[0].dtype)
    if low:
        refs[1][...] = d_total.astype(BF16)
    add_sums(pl.program_id(0) == 0, refs[-2], refs[-1], cotangent, hat)


def norm_back_rows(inputs, own, other, gain, residual, kinds):
    return row_call(
        functools.partial(norm_back_kernel, residual is not None, len(kinds) > 1),
        [inputs, own, other] + ([] if residual is None else [residual]),
        [gain],
        kinds,
        2,
        "norm_back",
    )


def chip_attend_kernel(causal, q_ref, k_ref, v_ref, qa_ref, ka_ref, o_ref, lse_ref):
    rows = q_ref.shape[0]
    block = 256
    low_half = lax.broadcasted_iota(jnp.int32, (1, LANES), 1) < HEAD_DIM
    for start in range(0, rows, block):
        keys = start + block if causal else k_ref.shape[0]
        query = q_ref[pl.ds(start, block), :] * BF16(SCALE)
        query_mark = qa_ref[pl.ds(start, block), :]
        key_block = k_ref[:keys, :]
        key_mark = ka_ref[:keys, :]
        values = v_ref[:keys, :]
        halves = []
        lses = []
        for head in range(2):
            keep = low_half if head == 0 else jnp.logical_not(low_half)
            scores = mxu(
                jnp.where(keep, query, query_mark), jnp.where(keep, key_block, key_mark), NT
            )
            if causal:
                scores = jnp.where(
                    lax.broadcasted_iota(jnp.int32, (block, keys), 1)
                    <= start + lax.broadcasted_iota(jnp.int32, (block, keys), 0),
                    scores,
                    NEG,
                )
            top = jnp.max(scores, -1, keepdims=True)
            weights = jnp.exp(scores - top)
            total = jnp.sum(weights, -1, keepdims=True)
            mixed = mxu(weights.astype(BF16), values, NN)
            halves.append(mixed / total)
            lses.append(top + jnp.log(total))
        o_ref[pl.ds(start, block), :] = jnp.where(low_half, halves[0], halves[1]).astype(BF16)
        turned = jnp.where(low_half, lses[0], lses[1]).T
        lse_ref[0, 0:1, pl.ds(start, block)] = turned[0:1]
        lse_ref[0, 1:2, pl.ds(start, block)] = turned[HEAD_DIM : HEAD_DIM + 1]


def pair_spec(rows, stride, offset):
    return pl.BlockSpec((rows, LANES), lambda p: (0, stride * p + offset))


def chip_attend(queries, q_at, pairs, k_at, v_at, query_mark, key_mark, causal):
    rows = queries.shape[0]
    keys = pairs.shape[0]
    count = queries.shape[1] // LANES // q_at[0]
    return pl.pallas_call(
        functools.partial(chip_attend_kernel, causal),
        grid=(count,),
        in_specs=[
            pair_spec(rows, *q_at),
            pair_spec(keys, *k_at),
            pair_spec(keys, *v_at),
            pl.BlockSpec((rows, LANES), lambda p: (0, 0)),
            pl.BlockSpec((keys, LANES), lambda p: (0, 0)),
        ],
        out_specs=[
            pair_spec(rows, 1, 0),
            pl.BlockSpec((1, 2, rows), lambda p: (p, 0, 0)),
        ],
        out_shape=[
            jax.ShapeDtypeStruct((rows, count * LANES), BF16),
            jax.ShapeDtypeStruct((count, 2, rows), F32),
        ],
        compiler_params=pltpu.CompilerParams(vmem_limit_bytes=VMEM),
        cost_estimate=LIGHT,
        name="attend",
    )(queries, pairs, pairs, query_mark, key_mark)


def chip_attend_back_kernel(causal, fused, *refs):
    q_ref, k_ref, v_ref, qa_ref, ka_ref, lse_ref, o_ref, do_ref = refs[:8]
    outs, (dk_acc, dv_acc) = refs[8:-2], refs[-2:]
    rows = q_ref.shape[0]
    block = 256
    low_half = lax.broadcasted_iota(jnp.int32, (1, LANES), 1) < HEAD_DIM
    zero = jnp.zeros((), BF16)
    dk_acc[...] = jnp.zeros_like(dk_acc)
    dv_acc[...] = jnp.zeros_like(dv_acc)
    for start in range(0, rows, block):
        keys = start + block if causal else k_ref.shape[0]
        span = pl.ds(start, block)
        query = q_ref[span, :] * BF16(SCALE)
        query_mark = qa_ref[span, :]
        key_block = k_ref[:keys, :]
        key_mark = ka_ref[:keys, :]
        values = v_ref[:keys, :]
        d_out = do_ref[span, :]
        inner = (d_out.astype(F32) * o_ref[span, :].astype(F32)).T
        d_query = None
        for head in range(2):
            keep = low_half if head == 0 else jnp.logical_not(low_half)
            delta = jnp.sum(
                inner[head * HEAD_DIM : (head + 1) * HEAD_DIM], axis=0, keepdims=True
            )
            scores = mxu(
                jnp.where(keep, key_block, key_mark), jnp.where(keep, query, query_mark), NT
            )
            if causal:
                scores = jnp.where(
                    lax.broadcasted_iota(jnp.int32, (keys, block), 0)
                    <= start + lax.broadcasted_iota(jnp.int32, (keys, block), 1),
                    scores,
                    NEG,
                )
            probs = jnp.exp(scores - lse_ref[0, head : head + 1, span])
            own_out = jnp.where(keep, d_out, zero)
            d_probs = mxu(values, own_out, NT)
            d_scores = (probs * (d_probs - delta)).astype(BF16)
            dv_acc[:keys, :] += mxu(probs.astype(BF16), own_out, NN)
            dk_acc[:keys, :] += mxu(d_scores, jnp.where(keep, query, zero), NN)
            term = mxu(jnp.where(keep, key_block, zero), d_scores, TN)
            d_query = term if d_query is None else d_query + term
        outs[0][span, :LANES] = (d_query * SCALE).T.astype(BF16)
    if fused:
        outs[0][:, LANES : 2 * LANES] = dk_acc[...].astype(BF16)
        outs[0][:, 2 * LANES :] = dv_acc[...].astype(BF16)
    else:
        outs[1][:, :LANES] = dk_acc[...].astype(BF16)
        outs[1][:, LANES:] = dv_acc[...].astype(BF16)


def chip_attend_back(
    queries, q_at, pairs, k_at, v_at, query_mark, key_mark, causal, log_total, mixed, d_mixed, fused
):
    rows = queries.shape[0]
    keys = pairs.shape[0]
    count = mixed.shape[1] // LANES

    def out(rows, blocks):
        return (
            pl.BlockSpec((rows, blocks * LANES), lambda p: (0, p)),
            jax.ShapeDtypeStruct((rows, count * blocks * LANES), BF16),
        )

    outs = [out(rows, 3)] if fused else [out(rows, 1), out(keys, 2)]
    return pl.pallas_call(
        functools.partial(chip_attend_back_kernel, causal, fused),
        grid=(count,),
        in_specs=[
            pair_spec(rows, *q_at),
            pair_spec(keys, *k_at),
            pair_spec(keys, *v_at),
            pl.BlockSpec((rows, LANES), lambda p: (0, 0)),
            pl.BlockSpec((keys, LANES), lambda p: (0, 0)),
            pl.BlockSpec((1, 2, rows), lambda p: (p, 0, 0)),
            pair_spec(rows, 1, 0),
            pair_spec(rows, 1, 0),
        ],
        out_specs=[spec for spec, _ in outs],
        out_shape=[shape for _, shape in outs],
        scratch_shapes=[pltpu.VMEM((keys, LANES), F32), pltpu.VMEM((keys, LANES), F32)],
        compiler_params=pltpu.CompilerParams(vmem_limit_bytes=VMEM),
        cost_estimate=LIGHT,
        name="attend_back",
    )(queries, pairs, pairs, query_mark, key_mark, log_total, mixed, d_mixed)


def piece_kernel(kind, low, high, count, x_ref, *refs):
    if count == 1:
        order_ref, stack_ref, rest = refs[0], refs[1], refs[2:]
        weights = [stack_ref.at[order_ref[i]] for i in range(stack_ref.shape[0])]
    else:
        weights, rest = refs[:count], refs[count:]
    own = high - low
    total = None
    for i, ref in enumerate(weights):
        span = pl.ds(i * own, own)
        if kind == "columns":
            rest[-1][:, span] = mxu(x_ref[...], ref[:, low:high], NN).astype(BF16)
        elif kind == "gelu":
            inner = mxu(x_ref[...], ref[:, low:high], NN)
            below = 0.5 + 0.5 * lax.erf(inner * (0.5**0.5))
            rest[0][:, span] = (inner * below).astype(BF16)
            bell = jnp.exp(inner * inner * (-0.5)) * (0.5 / jnp.pi) ** 0.5
            rest[1][:, span] = (below + inner * bell).astype(BF16)
        elif kind == "rows":
            term = mxu(x_ref[:, span], ref[low:high, :], NN)
            total = term if total is None else total + term
        elif kind == "columns_back":
            term = mxu(x_ref[:, span], ref[:, low:high], NT)
            total = term if total is None else total + term
        elif kind == "rows_back":
            rest[-1][:, span] = mxu(x_ref[...], ref[low:high, :], NT).astype(BF16)
        elif kind == "rows_back_slope":
            term = mxu(x_ref[...], ref[low:high, :], NT)
            rest[-1][:, span] = (term * rest[0][:, span].astype(F32)).astype(BF16)
    if total is not None:
        rest[-1][...] = total.astype(BF16)


def piece_product(kind, rows_in, pieces, low, high, slope=None, block=512):
    rows, depth = rows_in.shape
    stacked = len(pieces) == 2
    shape = pieces[1].shape[1:] if stacked else pieces[0].shape
    all_own = 4 * (high - low)
    width = {
        "columns": all_own,
        "gelu": all_own,
        "rows": shape[1],
        "columns_back": shape[0],
        "rows_back": all_own,
        "rows_back_slope": all_own,
    }[kind]
    outs = 2 if kind == "gelu" else 1
    out = pl.BlockSpec((block, width), lambda i: (i, 0))
    results = pl.pallas_call(
        functools.partial(piece_kernel, kind, low, high, 1 if stacked else len(pieces)),
        grid=(rows // block,),
        in_specs=[pl.BlockSpec((block, depth), lambda i: (i, 0))]
        + (
            [
                pl.BlockSpec(memory_space=pltpu.SMEM),
                pl.BlockSpec(pieces[1].shape, lambda i: (0, 0, 0)),
            ]
            if stacked
            else [pl.BlockSpec(piece.shape, lambda i: (0, 0)) for piece in pieces]
        )
        + ([] if slope is None else [out]),
        out_specs=[out] * outs,
        out_shape=[jax.ShapeDtypeStruct((rows, width), BF16)] * outs,
        compiler_params=pltpu.CompilerParams(vmem_limit_bytes=VMEM),
        cost_estimate=LIGHT,
        name="product_" + kind,
    )(rows_in, *pieces, *([] if slope is None else [slope]))
    return results if outs > 1 else results[0]


def weight_kernel(count, *refs):
    out_ref = refs[-1]
    at = 0
    for i in range(count):
        own = refs[i].shape[1]
        out_ref[pl.ds(at, own), :] = mxu(refs[i][...], refs[count + i][...], TN).astype(BF16)
        at += own


def weight_grads(pairs, part):
    rows, width = pairs[0][1].shape
    owns = [hidden.shape[1] // 4 for hidden, _ in pairs]
    return pl.pallas_call(
        functools.partial(weight_kernel, len(pairs)),
        grid=(2,),
        in_specs=[
            pl.BlockSpec((rows, own), lambda i: (0, 2 * part + i)) for own in owns
        ]
        + [pl.BlockSpec((rows, width), lambda i: (0, 0)) for _ in pairs],
        out_specs=pl.BlockSpec((sum(owns), width), lambda i: (i, 0)),
        out_shape=jax.ShapeDtypeStruct((2 * sum(owns), width), BF16),
        compiler_params=pltpu.CompilerParams(vmem_limit_bytes=VMEM),
        cost_estimate=LIGHT,
        name="weight_grads",
    )(*[hidden for hidden, _ in pairs], *[wide for _, wide in pairs])


CROSS = ("seq", "tensor")


class Chip:
    def __init__(self):
        self.core = lax.axis_index("seq")
        self.place = lax.axis_index("tensor")
        self.line = lax.axis_index("dp")
        self.first = [(i, i ^ 1) for i in range(4)] + [(4 + i, 4 + (i ^ 2)) for i in range(4)]
        self.second = [(i, i ^ 2) for i in range(4)] + [(4 + i, 4 + (i ^ 1)) for i in range(4)]

    def other(self, block):
        return lax.ppermute(block, "seq", swap_pairs(2, 1))

    def gather(self, block):
        near = lax.ppermute(block, CROSS, self.first)
        side = lax.ppermute(block, CROSS, self.second)
        far = lax.ppermute(side, CROSS, self.first)
        return [block, side, near, far]

    def ordered(self, own, other, index):
        first = index == 0
        return jnp.concatenate([jnp.where(first, own, other), jnp.where(first, other, own)], 0)

    def swap_start(self, blocks):
        near_bit = 1 + self.core

        def to(bits):
            return lax.dynamic_index_in_dim(blocks, jnp.bitwise_xor(self.place, bits), 0)

        cuts = lax.optimization_barrier((to(0), to(near_bit), to(3 - near_bit), to(3)))
        far = lax.ppermute(cuts[3], "tensor", swap_pairs(4, 3))
        return cuts[0], self.send_near(cuts[1]), self.send_side(cuts[2]), far

    def swap_end(self, parts):
        own, near, side, far = parts
        low, high = lax.rem(self.place, 2), self.place // 2
        first = self.core == 0
        beside, across = jnp.where(first, near, side), jnp.where(first, side, near)
        blocks = self.ordered(self.ordered(own, beside, low), self.ordered(across, far, low), high)
        return blocks.reshape(-1, own.shape[2]) if own.ndim == 3 else blocks

    def swap_rows(self, block):
        return self.swap_end(self.swap_start(block))

    def both_cores(self, rows):
        return self.ordered(rows, self.other(rows), self.core)

    def from_slot(self, rows):
        half = rows.shape[0] // 2
        own = lax.dynamic_slice_in_dim(rows, self.core * half, half, 0)
        rows = self.swap_rows(own.reshape(4, half // 4, -1))
        return rows.reshape(4, half // 4, -1)

    def send_near(self, block):
        return lax.ppermute(block, CROSS, self.first)

    def send_side(self, block):
        return lax.ppermute(block, CROSS, self.second)

    def along(self, block, bit):
        return lax.ppermute(block, "dp", swap_pairs(4, bit))


def add_low(left, right):
    return (left.astype(F32) + right.astype(F32)).astype(BF16)


def chip_local(
    source,
    target,
    out_grad,
    source_segments,
    target_segments,
    enc_gain,
    enc_shift,
    enc_qkv,
    enc_proj,
    enc_up,
    enc_down,
    dec_gain,
    dec_shift,
    dec_self_qkv,
    dec_self_proj,
    dec_cross_q,
    dec_cross_kv,
    dec_cross_proj,
    dec_up,
    dec_down,
):
    chip = Chip()
    core = chip.core
    tie = lax.optimization_barrier

    def own_columns(weight):
        part = weight.shape[-1] // 2
        cut = lax.dynamic_slice_in_dim(weight, core * part, part, weight.ndim - 1)
        return cut.reshape(weight.shape[0], -1)

    def own_rows(weight):
        part = weight.shape[0] // 2
        return lax.dynamic_slice_in_dim(weight, core * part, part, 0)

    def pin(value, *others):
        return tie((value,) + others)[0]

    bundles = [
        own_columns(enc_qkv),
        own_columns(dec_self_qkv),
        jnp.concatenate([own_rows(enc_proj), own_rows(dec_self_proj), own_rows(dec_cross_proj)], 0),
        jnp.concatenate([own_columns(dec_cross_q), own_columns(dec_cross_kv)], 1),
        own_rows(dec_down),
    ]
    near_bit = 1 + core
    order = jnp.bitwise_xor(
        chip.place, jnp.stack([0 * core, 3 - near_bit, near_bit, 0 * core + 3])
    ).astype(jnp.int32)

    def all_groups(own):
        return [order, lax.all_gather(own, "tensor", axis=0)]

    inner = enc_up.shape[1] // 2
    pieces = [None] * len(bundles)

    def launch(index, *after):
        own = pin(bundles[index], *after)
        pieces[index] = [own, chip.send_side(own), chip.send_near(own)]
        return pieces[index][1]

    def relay(index, value):
        side, near, value = tie((pieces[index][1], pieces[index][2], value))
        pieces[index][1:] = [side, near]
        pieces[index].append(chip.send_near(side))
        return value

    def arrived(index, value):
        tied = tie(tuple(pieces[index]) + (value,))
        pieces[index] = list(tied[:-1])
        return tied[-1]

    def enc(index):
        return enc_gain[index : index + 1], enc_shift[index : index + 1]

    def dec(index):
        return dec_gain[index : index + 1], dec_shift[index : index + 1]

    def part_rows(rows_in, weight, low, high):
        own = piece_product("rows", rows_in, weight, low, high)
        return own, chip.other(own)

    def part_back(grad, weight, low, high):
        own = piece_product("columns_back", grad, weight, low, high)
        return own, chip.other(own)

    fused_at = ((3, 0), (3, 1), (3, 2))

    def attend_self(qkv, marks, causal):
        return chip_attend(
            qkv, fused_at[0], qkv, fused_at[1], fused_at[2], marks[0], marks[1], causal
        )

    launch(0)
    swapped = arrived(0, chip.swap_rows(relay(0, source)))
    launch(1, swapped)
    x_source = chip.both_cores(swapped)
    sent_target = chip.swap_start(pin(target, swapped))
    w_enc_up = all_groups(pin(own_columns(enc_up), swapped))
    source_ids = lax.dynamic_index_in_dim(source_segments, chip.place, 0, keepdims=False)
    target_ids = lax.dynamic_index_in_dim(target_segments, chip.place, 0, keepdims=False)
    ids = jnp.arange(LANES, dtype=jnp.int32)[None] % HEAD_DIM
    counted = ids < IDS
    source_query = jnp.where(source_ids[:, None] == ids, NEG, 0.0).astype(BF16)
    target_query = jnp.where(target_ids[:, None] == ids, NEG, 0.0).astype(BF16)
    source_key = ((source_ids[:, None] != ids) & counted).astype(BF16)
    target_key = ((target_ids[:, None] != ids) & counted).astype(BF16)
    rows_a = norm_rows(x_source, *enc(0))
    rows_a = pin(rows_a, source_query, source_key)
    qkv_a = piece_product("columns", rows_a, pieces[0], 0, bundles[0].shape[1])
    launch(2, qkv_a)
    mixed_a, total_a = attend_self(qkv_a, (source_query, source_key), False)
    mixed_a, sent_target = tie((relay(1, mixed_a), sent_target))
    x_target = chip.both_cores(chip.swap_end(sent_target))
    w_enc_down = all_groups(pin(own_rows(enc_down), mixed_a))
    rows_c = norm_rows(pin(x_target, target_query, target_key), *dec(0))
    rows_c = arrived(1, rows_c)
    qkv_c = piece_product("columns", rows_c, pieces[1], 0, bundles[1].shape[1])
    qkv_c = relay(2, qkv_c)
    launch(3, qkv_c)
    w_dec_up = all_groups(pin(own_columns(dec_up), qkv_c))
    mixed_c, total_c = attend_self(qkv_c, (target_query, target_key), True)
    proj_rows = bundles[2].shape[0] // 3
    mixed_c, mixed_a = tie((arrived(2, mixed_c), mixed_a))
    own_a = piece_product("rows", mixed_a, pieces[2], 0, proj_rows)
    own_c = piece_product("rows", mixed_c, pieces[2], proj_rows, 2 * proj_rows)
    own_a, own_c = tie((relay(3, own_a), own_c))
    other_a, other_c = chip.other(own_a), chip.other(own_c)
    hidden, rows_b = add_norm(x_source, own_a, other_a, *enc(1))
    after_self, rows_e = add_norm(x_target, own_c, other_c, *dec(1))
    rows_b = pin(rows_b, rows_e)
    active_b, slope_b = piece_product("gelu", rows_b, w_enc_up, 0, inner, block=256)
    own_b = arrived(3, piece_product("rows", active_b, w_enc_down, 0, inner))
    encoded, rows_m = add_norm(hidden, own_b, chip.other(own_b), *enc(2))
    rows_m, rows_e = tie((rows_m, rows_e))
    launch(4, rows_m)
    head_width = dec_cross_q.shape[1] // 2
    pairs_m = piece_product("columns", rows_m, pieces[3], head_width, 3 * head_width)
    query_e = piece_product("columns", rows_e, pieces[3], 0, head_width)
    query_e = pin(query_e, pairs_m)
    mixed_e, total_e = chip_attend(
        query_e, (1, 0), pairs_m, (2, 0), (2, 1), target_query, source_key, False
    )
    mixed_e = relay(4, mixed_e)
    after_cross, rows_f = add_norm(
        after_self, *part_rows(mixed_e, pieces[2], 2 * proj_rows, 3 * proj_rows), *dec(2)
    )
    sent_grad = chip.swap_start(pin(out_grad, rows_f))
    active_f, slope_f = piece_product("gelu", rows_f, w_dec_up, 0, inner, block=256)
    active_f, sent_grad = tie((arrived(4, active_f), sent_grad))
    cotangent = chip.both_cores(chip.swap_end(sent_grad))
    w_dec_down = pieces[4]
    decoded, d_final, low_final, gain_d3, shift_d3 = last_norm(
        after_cross, *part_rows(active_f, w_dec_down, 0, inner), cotangent, *dec(3)
    )


    low_bit = lax.rem(chip.line, 2)
    high_bit = chip.line // 2

    def here(value, step, *args):
        args, value = tie((args, value))
        *result, sent = step(*args)
        return pin(value, result[1], *sent), result

    def to_side(came, kept):
        half = kept.shape[0] // 2
        sent = add_low(kept[half:], came[half:])
        return chip.send_side(sent), add_low(kept[:half], came[:half]), [sent]

    def to_line(*states):
        def cut(bits):
            parts = []
            for came, kept in states:
                quarter = kept.shape[0] // 4
                at = jnp.bitwise_xor(chip.line, bits) * quarter
                parts.append(
                    add_low(
                        lax.dynamic_slice_in_dim(kept, at, quarter, 0),
                        lax.dynamic_slice_in_dim(came, at, quarter, 0),
                    )
                )
            return jnp.concatenate(parts, 0)

        sent = [cut(bits) for bits in (3, 2, 1)]
        return [chip.along(part, bits) for part, bits in zip(sent, (3, 2, 1))], cut(0), sent

    def from_line(came, own):
        total = own.astype(F32)
        for block in came:
            total = total + block.astype(F32)
        own = total.astype(BF16)
        return [chip.along(own, bits) for bits in (3, 2, 1)], own, []

    def to_core(came, own):
        far, next_but_one, next_one = came
        first = chip.ordered(own, next_one, low_bit)
        second = chip.ordered(next_but_one, far, low_bit)
        return share(chip.ordered(first, second, high_bit))

    def share(whole):
        width = whole.shape[1] // 2
        sent = lax.dynamic_slice_in_dim(whole, (1 - core) * width, width, 1)
        own = lax.dynamic_slice_in_dim(whole, core * width, width, 1)
        return chip.other(sent), own

    def in_place(came, own):
        return chip.ordered(own[None], came[None], core)

    def sum_line(*states):
        total = jnp.concatenate([add_low(*state) for state in states], 0)
        return None, total, []

    def send_half(value, *pairs):
        sent = weight_grads(list(pairs), 1)
        return pin(value, sent), chip.send_near(sent)

    def keep_half(value, came, *pairs):
        first, value = tie((pairs[0], value))
        kept = weight_grads([first] + list(pairs[1:]), 0)
        return pin(value, kept), (came, kept)

    def ffn_back(low_out, slope, weight):
        return piece_product("rows_back_slope", low_out, weight, 0, inner, slope)

    low_send, near_fd = send_half(low_final, (active_f, low_final))
    d_inner_f = ffn_back(low_send, slope_f, w_dec_down)
    d_inner_f, near_fu = send_half(d_inner_f, (d_inner_f, rows_f))
    own = piece_product("columns_back", d_inner_f, w_dec_up, 0, inner)
    own, near_fd = tie((own, near_fd))
    other = chip.other(own)
    hold, keep_fd = keep_half(own, near_fd, (active_f, low_final))
    hold, side_fd = here(hold, to_side, *keep_fd)
    hold, keep_fu = keep_half(hold, near_fu, (d_inner_f, rows_f))
    d_cross, low_cross, gain_d2, shift_d2 = norm_back_rows(
        after_cross, own, pin(other, hold), dec(2)[0], d_final, [F32, BF16]
    )
    d_mixed = piece_product("rows_back", low_cross, pieces[2], 2 * proj_rows, 3 * proj_rows)
    d_mixed, side_fu = here(d_mixed, to_side, *keep_fu)
    d_query_e, d_pairs_m = chip_attend_back(
        query_e,
        (1, 0),
        pairs_m,
        (2, 0),
        (2, 1),
        target_query,
        source_key,
        False,
        total_e,
        mixed_e,
        d_mixed,
        False,
    )
    d_pairs_m, (_, total_f) = here(d_pairs_m, sum_line, side_fd, side_fu)
    sum_f = lax.psum(total_f, "dp")
    own_m, other_m = part_back(d_pairs_m, pieces[3], head_width, 3 * head_width)
    own_e, other_e = part_back(pin(d_query_e, own_m), pieces[3], 0, head_width)
    d_encoded, low_encoded, gain_e2, shift_e2 = norm_back_rows(
        encoded, own_m, pin(other_m, own_e), enc(2)[0], None, [F32, BF16]
    )
    low_send, near_bd = send_half(low_encoded, (active_b, low_encoded))
    d_inner_b = ffn_back(low_send, slope_b, w_enc_down)
    d_inner_b, near_bu = send_half(d_inner_b, (d_inner_b, rows_b))
    own = piece_product("columns_back", d_inner_b, w_enc_up, 0, inner)
    own, near_bd, other_e = tie((own, near_bd, other_e))
    other = chip.other(own)
    hold, keep_bd = keep_half(own, near_bd, (active_b, low_encoded))
    hold, side_bd = here(hold, to_side, *keep_bd)
    hold, keep_bu = keep_half(hold, near_bu, (d_inner_b, rows_b))
    d_hidden, low_hidden, gain_e1, shift_e1 = norm_back_rows(
        hidden, own, pin(other, hold), enc(1)[0], d_encoded, [F32, BF16]
    )
    pairs_x = ((mixed_e, low_cross), (d_query_e, rows_e), (d_pairs_m, rows_m))
    own_e, side_bu = here(pin(own_e, low_hidden), to_side, *keep_bu)
    pairs_x = tie((pairs_x, own_e))[0]
    own_e, near_x = send_half(own_e, *pairs_x)
    own_e, keep_x = keep_half(own_e, near_x, *pairs_x)
    d_self, low_self, gain_d1, shift_d1 = norm_back_rows(
        after_self, own_e, other_e, dec(1)[0], d_cross, [F32, BF16]
    )

    def self_back(d_mixed, qkv, marks, causal, totals, mixed):
        (d_qkv,) = chip_attend_back(
            qkv,
            fused_at[0],
            qkv,
            fused_at[1],
            fused_at[2],
            marks[0],
            marks[1],
            causal,
            totals,
            mixed,
            d_mixed,
            True,
        )
        return d_qkv

    d_mixed = piece_product("rows_back", low_self, pieces[2], proj_rows, 2 * proj_rows)
    d_mixed, (_, total_b) = here(d_mixed, sum_line, side_bd, side_bu)
    d_qkv_c = self_back(d_mixed, qkv_c, (target_query, target_key), True, total_c, mixed_c)
    d_qkv_c, sum_f, total_b = tie((d_qkv_c, sum_f, total_b))
    sum_b = lax.psum(total_b, "dp")
    d_qkv_c, side_x = here(d_qkv_c, to_side, *keep_x)
    pairs_c = ((mixed_c, low_self), (d_qkv_c, rows_c))
    d_qkv_c, near_c = send_half(d_qkv_c, *pairs_c)
    own_c = piece_product("columns_back", d_qkv_c, pieces[1], 0, 3 * head_width)
    own_c, keep_c = keep_half(own_c, near_c, *pairs_c)
    low_hidden, decoded = tie((low_hidden, decoded, own_c))[:2]
    decoded = chip.from_slot(decoded)
    d_mixed = piece_product("rows_back", low_hidden, pieces[2], 0, proj_rows)
    d_mixed, side_c = here(d_mixed, to_side, *keep_c)
    d_mixed, decoded = tie((d_mixed, decoded))
    d_qkv_a = self_back(d_mixed, qkv_a, (source_query, source_key), False, total_a, mixed_a)
    pairs_a = ((mixed_a, low_hidden), (d_qkv_a, rows_a))
    d_qkv_a, near_a = send_half(d_qkv_a, *pairs_a)
    d_qkv_a, (_, total_xc) = here(d_qkv_a, sum_line, side_x, side_c)
    d_qkv_a, sum_b, total_xc = tie((d_qkv_a, sum_b, total_xc))
    sum_xc = lax.psum(total_xc, "dp")
    own_a, other_a = part_back(d_qkv_a, pieces[0], 0, 3 * head_width)
    other_c = chip.other(pin(own_c, own_a))
    own_a, keep_a = keep_half(own_a, near_a, *pairs_a)
    source_grad, gain_e0, shift_e0 = norm_back_rows(
        x_source, own_a, other_a, enc(0)[0], d_hidden, [BF16]
    )
    own_c = pin(own_c, source_grad)
    own_c, side_a = here(own_c, to_side, *keep_a)
    target_grad, gain_d0, shift_d0 = norm_back_rows(
        x_target, own_c, other_c, dec(0)[0], d_self, [BF16]
    )
    gain_d0, line_a = here(gain_d0, to_line, side_a)
    source_grad = chip.from_slot(pin(source_grad, gain_d0))
    target_grad = chip.from_slot(pin(target_grad, gain_d0))
    line_a, sum_xc = tie((line_a, sum_xc))

    norms = jnp.concatenate(
        [
            gain_e0,
            gain_e1,
            gain_e2,
            shift_e0,
            shift_e1,
            shift_e2,
            gain_d0,
            gain_d1,
            gain_d2,
            gain_d3,
            shift_d0,
            shift_d1,
            shift_d2,
            shift_d3,
        ],
        0,
    )
    part = norms.shape[1] // 2
    norms = lax.dynamic_slice_in_dim(norms, core * part, part, 1)
    norms = norms + chip.send_near(norms)
    norms = norms + chip.send_side(norms)
    norms = norms + chip.along(norms, 1)
    norms = norms + chip.along(norms, 2)
    line_a = from_line(*line_a)[:2]
    line_a = to_core(*line_a)

    def wide(block, blocks):
        cores, rows, width = block.shape
        block = block.reshape(cores, blocks, rows // blocks, width)
        return jnp.transpose(block, (3, 1, 0, 2)).reshape(width, blocks, -1).astype(F32)

    def tall(block):
        return block.reshape(-1, block.shape[2]).astype(F32)

    n = proj_rows
    done_f, done_b = in_place(*share(sum_f)), in_place(*share(sum_b))
    done_xc, done_a = in_place(*share(sum_xc)), in_place(*line_a)
    done_x, done_c = done_xc[:, : 4 * n], done_xc[:, 4 * n :]
    source_grad, target_grad = source_grad.astype(F32), target_grad.astype(F32)
    hid = done_f.shape[1] // 2
    return (
        decoded,
        source_grad,
        target_grad,
        norms[0:3],
        norms[3:6],
        wide(done_a[:, n:], 3),
        tall(done_a[:, :n]),
        wide(done_b[:, inner:], 1)[:, 0],
        tall(done_b[:, :inner]),
        norms[6:10],
        norms[10:14],
        wide(done_c[:, n:], 3),
        tall(done_c[:, :n]),
        wide(done_x[:, n : n + head_width], 1)[:, 0],
        wide(done_x[:, n + head_width :], 2),
        tall(done_x[:, :n]),
        wide(done_f[:, hid:], 1)[:, 0],
        tall(done_f[:, :hid]),
    )


def solution(mesh):
    rows = P("dp", ("seq", "tensor"), None)
    segments = P("dp", None)
    shape = dict(mesh.shape)
    chips = shape["dp"] == 4 and shape["seq"] == 2 and shape["tensor"] == 4
    return jax.shard_map(
        chip_local if chips else local,
        mesh=mesh,
        in_specs=(
            rows,
            rows,
            rows,
            segments,
            segments,
            P(),
            P(),
            P(None, None, "tensor"),
            P("tensor", None),
            P(None, "tensor"),
            P("tensor", None),
            P(),
            P(),
            P(None, None, "tensor"),
            P("tensor", None),
            P(None, "tensor"),
            P(None, None, "tensor"),
            P("tensor", None),
            P(None, "tensor"),
            P("tensor", None),
        ),
        out_specs=(
            rows,
            rows,
            rows,
            P(None, "seq"),
            P(None, "seq"),
            P("seq", None, "tensor"),
            P("tensor", "seq"),
            P("seq", "tensor"),
            P("tensor", "seq"),
            P(None, "seq"),
            P(None, "seq"),
            P("seq", None, "tensor"),
            P("tensor", "seq"),
            P("seq", "tensor"),
            P("seq", None, "tensor"),
            P("tensor", "seq"),
            P("seq", "tensor"),
            P("tensor", "seq"),
        ),
        check_vma=False,
    )
```

```python
import functools

import jax
import jax.numpy as jnp
from jax import lax
from jax.experimental import pallas as pl
from jax.experimental.pallas import tpu as pltpu
from jax.sharding import PartitionSpec as P

HEAD_DIM = 64
LANES = 128
IDS = 9
EPS = 1e-05
NEG = -1e30
SCALE = HEAD_DIM ** (-0.5)
F32 = jnp.float32
BF16 = jnp.bfloat16
NT = (((1,), (1,)), ((), ()))
NN = (((1,), (0,)), ((), ()))
TN = (((0,), (0,)), ((), ()))


def mxu(left, right, dims):
    return lax.dot_general(left, right, dims, preferred_element_type=F32)


def layer_norm(inputs, norm_gain, norm_shift):
    row_mean = jnp.mean(inputs, -1, keepdims=True)
    centred = inputs - row_mean
    spread = jnp.mean(centred * centred, -1, keepdims=True)
    return centred * lax.rsqrt(spread + EPS) * norm_gain + norm_shift


def exact_gelu(inputs):
    return jax.nn.gelu(inputs, approximate=False)


def norm_back(inputs, norm_gain, norm_shift, cotangent):
    _, pullback = jax.vjp(layer_norm, inputs, norm_gain, norm_shift)
    return pullback(cotangent)


def project(rows, weight):
    return mxu(rows, weight, NN)


def back_project(grad, weight):
    return mxu(grad, weight, NT)


def weight_grad(rows, grad):
    return mxu(rows, grad, TN).astype(BF16)


def attend_kernel(causal, first_ref, q_ref, k_ref, v_ref, qa_ref, ka_ref, o_ref, lse_ref):
    rows = q_ref.shape[0]
    keys = k_ref.shape[0]
    block = min(rows, 256)
    low_half = lax.broadcasted_iota(jnp.int32, (1, LANES), 1) < HEAD_DIM
    key_block = k_ref[...]
    key_mark = ka_ref[...]
    values = v_ref[...]
    for start in range(0, rows, block):
        query = q_ref[pl.ds(start, block), :] * BF16(SCALE)
        query_mark = qa_ref[pl.ds(start, block), :]
        halves = []
        lses = []
        for head in range(2):
            keep = low_half if head == 0 else jnp.logical_not(low_half)
            scores = mxu(
                jnp.where(keep, query, query_mark), jnp.where(keep, key_block, key_mark), NT
            )
            if causal:
                place = (
                    first_ref[0] + start + lax.broadcasted_iota(jnp.int32, (block, keys), 0)
                )
                scores = jnp.where(
                    lax.broadcasted_iota(jnp.int32, (block, keys), 1) <= place, scores, NEG
                )
            top = jnp.max(scores, -1, keepdims=True)
            weights = jnp.exp(scores - top)
            total = jnp.sum(weights, -1, keepdims=True)
            mixed = mxu(weights.astype(BF16), values, NN)
            halves.append(mixed / total)
            lses.append(top + jnp.log(total))
        o_ref[pl.ds(start, block), :] = jnp.where(low_half, halves[0], halves[1]).astype(BF16)
        both = jnp.where(low_half, lses[0], lses[1])
        turned = both.T
        lse_ref[0, 0:1, pl.ds(start, block)] = turned[0:1]
        lse_ref[0, 1:2, pl.ds(start, block)] = turned[HEAD_DIM : HEAD_DIM + 1]


def attend(queries, keys, values, query_mark, key_mark, first_row, causal):
    rows, width = queries.shape
    key_rows = keys.shape[0]
    pairs = width // LANES
    return pl.pallas_call(
        functools.partial(attend_kernel, causal),
        grid_spec=pltpu.PrefetchScalarGridSpec(
            num_scalar_prefetch=1,
            grid=(pairs,),
            in_specs=[
                pl.BlockSpec((rows, LANES), lambda p, first: (0, p)),
                pl.BlockSpec((key_rows, LANES), lambda p, first: (0, p)),
                pl.BlockSpec((key_rows, LANES), lambda p, first: (0, p)),
                pl.BlockSpec((rows, LANES), lambda p, first: (0, 0)),
                pl.BlockSpec((key_rows, LANES), lambda p, first: (0, 0)),
            ],
            out_specs=[
                pl.BlockSpec((rows, LANES), lambda p, first: (0, p)),
                pl.BlockSpec((1, 2, rows), lambda p, first: (p, 0, 0)),
            ],
        ),
        out_shape=[
            jax.ShapeDtypeStruct((rows, width), BF16),
            jax.ShapeDtypeStruct((pairs, 2, rows), F32),
        ],
        compiler_params=pltpu.CompilerParams(vmem_limit_bytes=40 << 20),
        cost_estimate=pl.CostEstimate(
            flops=4 * rows * key_rows * width * 2,
            bytes_accessed=4 * rows * width + 4 * key_rows * width,
            transcendentals=rows * key_rows * width // HEAD_DIM,
        ),
        name="attend",
    )(first_row, queries, keys, values, query_mark, key_mark)


def attend_back_kernel(
    causal,
    first_ref,
    q_ref,
    k_ref,
    v_ref,
    qa_ref,
    ka_ref,
    lse_ref,
    o_ref,
    do_ref,
    dq_ref,
    dk_ref,
    dv_ref,
    dk_acc,
    dv_acc,
):
    rows = q_ref.shape[0]
    keys = k_ref.shape[0]
    block = min(rows, 256)
    low_half = lax.broadcasted_iota(jnp.int32, (1, LANES), 1) < HEAD_DIM
    key_block = k_ref[...]
    key_mark = ka_ref[...]
    values = v_ref[...]
    zero = jnp.zeros((), BF16)
    dk_acc[...] = jnp.zeros_like(dk_acc)
    dv_acc[...] = jnp.zeros_like(dv_acc)
    for start in range(0, rows, block):
        span = pl.ds(start, block)
        query = q_ref[span, :] * BF16(SCALE)
        query_mark = qa_ref[span, :]
        d_out = do_ref[span, :]
        inner = (d_out.astype(F32) * o_ref[span, :].astype(F32)).T
        d_query = None
        for head in range(2):
            keep = low_half if head == 0 else jnp.logical_not(low_half)
            delta = jnp.sum(
                inner[head * HEAD_DIM : (head + 1) * HEAD_DIM], axis=0, keepdims=True
            )
            scores = mxu(
                jnp.where(keep, key_block, key_mark), jnp.where(keep, query, query_mark), NT
            )
            if causal:
                place = (
                    first_ref[0] + start + lax.broadcasted_iota(jnp.int32, (keys, block), 1)
                )
                scores = jnp.where(
                    lax.broadcasted_iota(jnp.int32, (keys, block), 0) <= place, scores, NEG
                )
            probs = jnp.exp(scores - lse_ref[0, head : head + 1, span])
            own_out = jnp.where(keep, d_out, zero)
            d_probs = mxu(values, own_out, NT)
            d_scores = (probs * (d_probs - delta)).astype(BF16)
            dv_acc[...] += mxu(probs.astype(BF16), own_out, NN)
            dk_acc[...] += mxu(d_scores, jnp.where(keep, query, zero), NN)
            term = mxu(jnp.where(keep, key_block, zero), d_scores, TN)
            d_query = term if d_query is None else d_query + term
        dq_ref[span, :] = (d_query * SCALE).T.astype(BF16)
    dk_ref[...] = dk_acc[...].astype(BF16)
    dv_ref[...] = dv_acc[...].astype(BF16)


def attend_back(
    queries, keys, values, query_mark, key_mark, first_row, causal, log_total, mixed, d_mixed
):
    rows, width = queries.shape
    key_rows = keys.shape[0]
    pairs = width // LANES
    row_spec = pl.BlockSpec((rows, LANES), lambda p, first: (0, p))
    key_spec = pl.BlockSpec((key_rows, LANES), lambda p, first: (0, p))
    return pl.pallas_call(
        functools.partial(attend_back_kernel, causal),
        grid_spec=pltpu.PrefetchScalarGridSpec(
            num_scalar_prefetch=1,
            grid=(pairs,),
            in_specs=[
                row_spec,
                key_spec,
                key_spec,
                pl.BlockSpec((rows, LANES), lambda p, first: (0, 0)),
                pl.BlockSpec((key_rows, LANES), lambda p, first: (0, 0)),
                pl.BlockSpec((1, 2, rows), lambda p, first: (p, 0, 0)),
                row_spec,
                row_spec,
            ],
            out_specs=[row_spec, key_spec, key_spec],
            scratch_shapes=[
                pltpu.VMEM((key_rows, LANES), F32),
                pltpu.VMEM((key_rows, LANES), F32),
            ],
        ),
        out_shape=[
            jax.ShapeDtypeStruct((rows, width), BF16),
            jax.ShapeDtypeStruct((key_rows, width), BF16),
            jax.ShapeDtypeStruct((key_rows, width), BF16),
        ],
        compiler_params=pltpu.CompilerParams(vmem_limit_bytes=40 << 20),
        cost_estimate=pl.CostEstimate(
            flops=10 * rows * key_rows * width * 2,
            bytes_accessed=8 * rows * width + 8 * key_rows * width,
            transcendentals=rows * key_rows * width // HEAD_DIM,
        ),
        name="attend_back",
    )(first_row, queries, keys, values, query_mark, key_mark, log_total, mixed, d_mixed)


class Layout:
    def __init__(self, slots):
        self.tensor = lax.axis_size("tensor")
        self.seq = lax.axis_size("seq")
        self.slots = slots
        self.spread = self.tensor // slots
        self.place = lax.axis_index("tensor")
        self.half = lax.axis_index("seq")
        self.row_groups = [
            [j * slots + u for u in range(slots)] for j in range(self.spread)
        ]
        self.slot_groups = [
            [j * slots + u for j in range(self.spread)] for u in range(slots)
        ]

    def to_slots(self, block):
        rows = lax.all_to_all(
            block, "tensor", 0, 1, axis_index_groups=self.row_groups, tiled=True
        )
        return rows.reshape(-1, block.shape[2])

    def from_slots(self, rows):
        block = rows.reshape(1, rows.shape[0], rows.shape[1])
        return lax.all_to_all(
            block, "tensor", 1, 0, axis_index_groups=self.row_groups, tiled=True
        )

    def gather_keys(self, rows):
        if self.spread > 1:
            rows = lax.all_gather(
                rows, "tensor", axis=0, axis_index_groups=self.slot_groups, tiled=True
            )
        return lax.all_gather(rows, "seq", axis=0, tiled=True)

    def scatter_keys(self, rows):
        rows = lax.psum_scatter(rows, "seq", scatter_dimension=0, tiled=True)
        if self.spread > 1:
            rows = lax.psum_scatter(
                rows,
                "tensor",
                scatter_dimension=0,
                axis_index_groups=self.slot_groups,
                tiled=True,
            )
        return rows

    def gather_weight(self, shard):
        part = shard.shape[0] // self.seq
        own = lax.dynamic_slice_in_dim(shard, self.half * part, part, 0)
        return lax.all_gather(own, ("tensor", "seq"), axis=0, tiled=True)

    def gather_columns(self, shard):
        depth, blocks, own = shard.shape
        whole = self.gather_weight(shard.reshape(depth, blocks * own))
        whole = whole.reshape(self.tensor, depth, blocks, own)
        return jnp.transpose(whole, (1, 2, 0, 3)).reshape(depth, blocks * self.tensor * own)

    def reduce_rows(self, gradient):
        rows, width = gradient.shape
        parts = gradient.reshape(self.tensor, rows // self.tensor, self.seq, width // self.seq)
        parts = jnp.transpose(parts, (2, 0, 1, 3)).reshape(
            self.seq * rows, width // self.seq
        )
        return self.reduce(parts)

    def reduce_columns(self, gradient, blocks):
        depth, width = gradient.shape
        own = width // blocks // self.tensor
        parts = gradient.reshape(self.seq, depth // self.seq, blocks, self.tensor, own)
        parts = jnp.transpose(parts, (0, 3, 1, 2, 4)).reshape(
            self.seq * self.tensor * depth // self.seq, blocks * own
        )
        return self.reduce(parts).reshape(depth // self.seq, blocks, own)

    def reduce(self, parts):
        own = lax.psum_scatter(parts, ("seq", "tensor"), scatter_dimension=0, tiled=True)
        return lax.psum(own, "dp").astype(F32)


def local(
    source,
    target,
    out_grad,
    source_segments,
    target_segments,
    enc_gain,
    enc_shift,
    enc_qkv,
    enc_proj,
    enc_up,
    enc_down,
    dec_gain,
    dec_shift,
    dec_self_qkv,
    dec_self_proj,
    dec_cross_q,
    dec_cross_kv,
    dec_cross_proj,
    dec_up,
    dec_down,
):
    width = source.shape[2]
    lay = Layout(source.shape[0])
    w_enc_qkv = lay.gather_columns(enc_qkv)
    w_self_qkv = lay.gather_columns(dec_self_qkv)
    w_enc_proj = lay.gather_weight(enc_proj)
    w_self_proj = lay.gather_weight(dec_self_proj)
    w_enc_up = lay.gather_columns(enc_up[:, None])
    w_enc_down = lay.gather_weight(enc_down)
    w_cross_q = lay.gather_columns(dec_cross_q[:, None])
    w_cross_kv = lay.gather_columns(dec_cross_kv)
    w_cross_proj = lay.gather_weight(dec_cross_proj)
    w_dec_up = lay.gather_columns(dec_up[:, None])
    w_dec_down = lay.gather_weight(dec_down)
    slot = lax.rem(lay.place, lay.slots)
    rows = source.shape[1] * lay.slots
    first_row = (lay.half * lay.spread + lay.place // lay.slots) * rows
    source_ids = lax.dynamic_index_in_dim(source_segments, slot, 0, keepdims=False)
    target_ids = lax.dynamic_index_in_dim(target_segments, slot, 0, keepdims=False)
    ids = jnp.arange(LANES, dtype=jnp.int32) % HEAD_DIM
    own_source = lax.dynamic_slice_in_dim(source_ids, first_row, rows, 0)
    own_target = lax.dynamic_slice_in_dim(target_ids, first_row, rows, 0)
    source_query = jnp.where(own_source[:, None] == ids[None], NEG, 0.0).astype(BF16)
    target_query = jnp.where(own_target[:, None] == ids[None], NEG, 0.0).astype(BF16)
    counted = ids[None] < IDS
    source_key = ((source_ids[:, None] != ids[None]) & counted).astype(BF16)
    target_key = ((target_ids[:, None] != ids[None]) & counted).astype(BF16)
    first = first_row[None].astype(jnp.int32)

    x_source = lay.to_slots(source).astype(F32)
    x_target = lay.to_slots(target).astype(F32)
    cotangent = lay.to_slots(out_grad).astype(F32)

    rows_a = layer_norm(x_source, enc_gain[0], enc_shift[0]).astype(BF16)
    qkv_a = project(rows_a, w_enc_qkv).astype(BF16)
    query_a = qkv_a[:, :width]
    pairs_a = lay.gather_keys(qkv_a[:, width:])
    mixed_a, total_a = attend(
        query_a, pairs_a[:, :width], pairs_a[:, width:], source_query, source_key, first, False
    )
    hidden = x_source + project(mixed_a, w_enc_proj)
    rows_c = layer_norm(x_target, dec_gain[0], dec_shift[0]).astype(BF16)
    qkv_c = project(rows_c, w_self_qkv).astype(BF16)
    query_c = qkv_c[:, :width]
    pairs_c = lay.gather_keys(qkv_c[:, width:])
    mixed_c, total_c = attend(
        query_c, pairs_c[:, :width], pairs_c[:, width:], target_query, target_key, first, True
    )
    after_self = x_target + project(mixed_c, w_self_proj)
    rows_b = layer_norm(hidden, enc_gain[1], enc_shift[1]).astype(BF16)
    inner_b = project(rows_b, w_enc_up)
    active_b = exact_gelu(inner_b).astype(BF16)
    encoded = hidden + project(active_b, w_enc_down)
    rows_m = layer_norm(encoded, enc_gain[2], enc_shift[2]).astype(BF16)
    pairs_m = lay.gather_keys(project(rows_m, w_cross_kv).astype(BF16))
    rows_e = layer_norm(after_self, dec_gain[1], dec_shift[1]).astype(BF16)
    query_e = project(rows_e, w_cross_q).astype(BF16)
    mixed_e, total_e = attend(
        query_e, pairs_m[:, :width], pairs_m[:, width:], target_query, source_key, first, False
    )
    after_cross = after_self + project(mixed_e, w_cross_proj)
    rows_f = layer_norm(after_cross, dec_gain[2], dec_shift[2]).astype(BF16)
    inner_f = project(rows_f, w_dec_up)
    active_f = exact_gelu(inner_f).astype(BF16)
    final_rows = after_cross + project(active_f, w_dec_down)
    decoded, final_back = jax.vjp(layer_norm, final_rows, dec_gain[3], dec_shift[3])

    d_final, dec_gain_three, dec_shift_three = final_back(cotangent)

    def ffn_back(d_out, rows_in, inner, active, weight_up, weight_down):
        d_low = d_out.astype(BF16)
        grad_down = lay.reduce_rows(weight_grad(active, d_low))
        d_active = back_project(d_low, weight_down)
        _, gelu_back = jax.vjp(exact_gelu, inner)
        d_inner = gelu_back(d_active)[0].astype(BF16)
        grad_up = lay.reduce_columns(weight_grad(rows_in, d_inner), 1)[:, 0]
        return back_project(d_inner, weight_up), grad_up, grad_down

    d_normed, grad_dec_up, grad_dec_down = ffn_back(
        d_final, rows_f, inner_f, active_f, w_dec_up, w_dec_down
    )
    d_input, dec_gain_two, dec_shift_two = norm_back(
        after_cross, dec_gain[2], dec_shift[2], d_normed
    )
    d_cross = d_final + d_input
    d_low = d_cross.astype(BF16)
    grad_cross_proj = lay.reduce_rows(weight_grad(mixed_e, d_low))
    d_mixed = back_project(d_low, w_cross_proj).astype(BF16)
    d_query, d_keys, d_values = attend_back(
        query_e,
        pairs_m[:, :width],
        pairs_m[:, width:],
        target_query,
        source_key,
        first,
        False,
        total_e,
        mixed_e,
        d_mixed,
    )
    d_pairs = lay.scatter_keys(jnp.concatenate([d_keys, d_values], 1))
    grad_cross_q = lay.reduce_columns(weight_grad(rows_e, d_query), 1)[:, 0]
    grad_cross_kv = lay.reduce_columns(weight_grad(rows_m, d_pairs), 2)
    d_normed = back_project(d_query, w_cross_q)
    d_memory = back_project(d_pairs, w_cross_kv)
    d_input, dec_gain_one, dec_shift_one = norm_back(
        after_self, dec_gain[1], dec_shift[1], d_normed
    )
    d_self = d_cross + d_input
    d_encoded, enc_gain_two, enc_shift_two = norm_back(encoded, enc_gain[2], enc_shift[2], d_memory)
    d_normed, grad_enc_up, grad_enc_down = ffn_back(
        d_encoded, rows_b, inner_b, active_b, w_enc_up, w_enc_down
    )
    d_input, enc_gain_one, enc_shift_one = norm_back(hidden, enc_gain[1], enc_shift[1], d_normed)
    d_hidden = d_encoded + d_input

    def self_back(d_out, rows_in, query, pairs, marks, causal, totals, mixed, w_qkv, w_proj):
        d_low = d_out.astype(BF16)
        grad_proj = lay.reduce_rows(weight_grad(mixed, d_low))
        d_mixed = back_project(d_low, w_proj).astype(BF16)
        d_query, d_keys, d_values = attend_back(
            query,
            pairs[:, :width],
            pairs[:, width:],
            marks[0],
            marks[1],
            first,
            causal,
            totals,
            mixed,
            d_mixed,
        )
        d_pairs = lay.scatter_keys(jnp.concatenate([d_keys, d_values], 1))
        d_qkv = jnp.concatenate([d_query, d_pairs], 1)
        grad_qkv = lay.reduce_columns(weight_grad(rows_in, d_qkv), 3)
        return back_project(d_qkv, w_qkv), grad_qkv, grad_proj

    d_normed, grad_self_qkv, grad_self_proj = self_back(
        d_self,
        rows_c,
        query_c,
        pairs_c,
        (target_query, target_key),
        True,
        total_c,
        mixed_c,
        w_self_qkv,
        w_self_proj,
    )
    d_input, dec_gain_zero, dec_shift_zero = norm_back(
        x_target, dec_gain[0], dec_shift[0], d_normed
    )
    target_grad = d_self + d_input
    d_normed, grad_enc_qkv, grad_enc_proj = self_back(
        d_hidden,
        rows_a,
        query_a,
        pairs_a,
        (source_query, source_key),
        False,
        total_a,
        mixed_a,
        w_enc_qkv,
        w_enc_proj,
    )
    d_input, enc_gain_zero, enc_shift_zero = norm_back(
        x_source, enc_gain[0], enc_shift[0], d_normed
    )
    source_grad = d_hidden + d_input
    norms = jnp.stack(
        [
            enc_gain_zero,
            enc_gain_one,
            enc_gain_two,
            enc_shift_zero,
            enc_shift_one,
            enc_shift_two,
            dec_gain_zero,
            dec_gain_one,
            dec_gain_two,
            dec_gain_three,
            dec_shift_zero,
            dec_shift_one,
            dec_shift_two,
            dec_shift_three,
        ]
    )
    part = width // lay.seq
    norms = lax.dynamic_slice_in_dim(
        lax.psum(norms, ("dp", "seq", "tensor")), lay.half * part, part, 1
    )
    return (
        lay.from_slots(decoded.astype(BF16)),
        lay.from_slots(source_grad.astype(BF16)).astype(F32),
        lay.from_slots(target_grad.astype(BF16)).astype(F32),
        norms[0:3],
        norms[3:6],
        grad_enc_qkv,
        grad_enc_proj,
        grad_enc_up,
        grad_enc_down,
        norms[6:10],
        norms[10:14],
        grad_self_qkv,
        grad_self_proj,
        grad_cross_q,
        grad_cross_kv,
        grad_cross_proj,
        grad_dec_up,
        grad_dec_down,
    )


def swap_pairs(count, bit):
    return [(i, i ^ bit) for i in range(count)]


def norm_parts(inputs):
    centred = inputs - jnp.mean(inputs, -1, keepdims=True)
    scale = lax.rsqrt(jnp.mean(centred * centred, -1, keepdims=True) + EPS)
    return centred * scale, scale


def norm_pull(hat, scale, gain, cotangent):
    tilted = cotangent * gain
    return scale * (
        tilted
        - jnp.mean(tilted, -1, keepdims=True)
        - hat * jnp.mean(tilted * hat, -1, keepdims=True)
    )


ROW_BLOCK = 256
VMEM = 56 << 20
LIGHT = pl.CostEstimate(flops=1 << 20, bytes_accessed=1 << 16, transcendentals=0)


def row_call(kernel, inputs, vectors, outs, sums, name):
    rows, width = inputs[0].shape
    block = pl.BlockSpec((ROW_BLOCK, width), lambda i: (i, 0))
    whole = pl.BlockSpec((1, width), lambda i: (0, 0))
    return pl.pallas_call(
        kernel,
        grid=(rows // ROW_BLOCK,),
        in_specs=[block] * len(inputs) + [whole] * len(vectors),
        out_specs=[block] * len(outs) + [whole] * sums,
        out_shape=[jax.ShapeDtypeStruct((rows, width), kind) for kind in outs]
        + [jax.ShapeDtypeStruct((1, width), F32)] * sums,
        compiler_params=pltpu.CompilerParams(vmem_limit_bytes=VMEM),
        cost_estimate=LIGHT,
        name=name,
    )(*inputs, *vectors)


def norm_kernel(x_ref, gain_ref, shift_ref, low_ref):
    hat, _ = norm_parts(x_ref[...].astype(F32))
    low_ref[...] = (hat * gain_ref[...] + shift_ref[...]).astype(BF16)


def norm_rows(inputs, gain, shift):
    return row_call(norm_kernel, [inputs], [gain, shift], [BF16], 0, "norm_rows")[0]


def add_norm_kernel(x_ref, own_ref, other_ref, gain_ref, shift_ref, sum_ref, low_ref):
    total = (
        x_ref[...].astype(F32) + own_ref[...].astype(F32) + other_ref[...].astype(F32)
    )
    sum_ref[...] = total
    hat, _ = norm_parts(total)
    low_ref[...] = (hat * gain_ref[...] + shift_ref[...]).astype(BF16)


def add_norm(inputs, own, other, gain, shift):
    return row_call(
        add_norm_kernel, [inputs, own, other], [gain, shift], [F32, BF16], 0, "add_norm"
    )


def add_sums(first, gain_out, shift_out, cotangent, hat):
    @pl.when(first)
    def _():
        gain_out[...] = jnp.zeros_like(gain_out)
        shift_out[...] = jnp.zeros_like(shift_out)

    gain_out[...] += jnp.sum(cotangent * hat, 0, keepdims=True)
    shift_out[...] += jnp.sum(cotangent, 0, keepdims=True)


def last_norm_kernel(
    x_ref, own_ref, other_ref, cot_ref, gain_ref, shift_ref, y_ref, d_ref, low_ref, dg_ref, ds_ref
):
    total = (
        x_ref[...].astype(F32) + own_ref[...].astype(F32) + other_ref[...].astype(F32)
    )
    hat, scale = norm_parts(total)
    y_ref[...] = (hat * gain_ref[...] + shift_ref[...]).astype(BF16)
    cotangent = cot_ref[...].astype(F32)
    d_total = norm_pull(hat, scale, gain_ref[...], cotangent)
    d_ref[...] = d_total
    low_ref[...] = d_total.astype(BF16)
    add_sums(pl.program_id(0) == 0, dg_ref, ds_ref, cotangent, hat)


def last_norm(inputs, own, other, cotangent, gain, shift):
    return row_call(
        last_norm_kernel,
        [inputs, own, other, cotangent],
        [gain, shift],
        [BF16, F32, BF16],
        2,
        "last_norm",
    )


def norm_back_kernel(residual, low, *refs):
    x_ref, own_ref, other_ref = refs[:3]
    refs = refs[3:]
    if residual:
        res_ref, refs = refs[0], refs[1:]
    gain_ref, refs = refs[0], refs[1:]
    hat, scale = norm_parts(x_ref[...].astype(F32))
    cotangent = own_ref[...].astype(F32) + other_ref[...].astype(F32)
    d_total = norm_pull(hat, scale, gain_ref[...], cotangent)
    if residual:
        d_total = d_total + res_ref[...]
    refs[0][...] = d_total.astype(refs[0].dtype)
    if low:
        refs[1][...] = d_total.astype(BF16)
    add_sums(pl.program_id(0) == 0, refs[-2], refs[-1], cotangent, hat)


def norm_back_rows(inputs, own, other, gain, residual, kinds):
    return row_call(
        functools.partial(norm_back_kernel, residual is not None, len(kinds) > 1),
        [inputs, own, other] + ([] if residual is None else [residual]),
        [gain],
        kinds,
        2,
        "norm_back",
    )


def chip_attend_kernel(causal, q_ref, k_ref, v_ref, qa_ref, ka_ref, o_ref, lse_ref):
    rows = q_ref.shape[0]
    block = 256
    low_half = lax.broadcasted_iota(jnp.int32, (1, LANES), 1) < HEAD_DIM
    for start in range(0, rows, block):
        keys = start + block if causal else k_ref.shape[0]
        query = q_ref[pl.ds(start, block), :] * BF16(SCALE)
        query_mark = qa_ref[pl.ds(start, block), :]
        key_block = k_ref[:keys, :]
        key_mark = ka_ref[:keys, :]
        values = v_ref[:keys, :]
        halves = []
        lses = []
        for head in range(2):
            keep = low_half if head == 0 else jnp.logical_not(low_half)
            scores = mxu(
                jnp.where(keep, query, query_mark), jnp.where(keep, key_block, key_mark), NT
            )
            if causal:
                scores = jnp.where(
                    lax.broadcasted_iota(jnp.int32, (block, keys), 1)
                    <= start + lax.broadcasted_iota(jnp.int32, (block, keys), 0),
                    scores,
                    NEG,
                )
            top = jnp.max(scores, -1, keepdims=True)
            weights = jnp.exp(scores - top)
            total = jnp.sum(weights, -1, keepdims=True)
            mixed = mxu(weights.astype(BF16), values, NN)
            halves.append(mixed / total)
            lses.append(top + jnp.log(total))
        o_ref[pl.ds(start, block), :] = jnp.where(low_half, halves[0], halves[1]).astype(BF16)
        turned = jnp.where(low_half, lses[0], lses[1]).T
        lse_ref[0, 0:1, pl.ds(start, block)] = turned[0:1]
        lse_ref[0, 1:2, pl.ds(start, block)] = turned[HEAD_DIM : HEAD_DIM + 1]


def pair_spec(rows, stride, offset):
    return pl.BlockSpec((rows, LANES), lambda p: (0, stride * p + offset))


def chip_attend(queries, q_at, pairs, k_at, v_at, query_mark, key_mark, causal):
    rows = queries.shape[0]
    keys = pairs.shape[0]
    count = queries.shape[1] // LANES // q_at[0]
    return pl.pallas_call(
        functools.partial(chip_attend_kernel, causal),
        grid=(count,),
        in_specs=[
            pair_spec(rows, *q_at),
            pair_spec(keys, *k_at),
            pair_spec(keys, *v_at),
            pl.BlockSpec((rows, LANES), lambda p: (0, 0)),
            pl.BlockSpec((keys, LANES), lambda p: (0, 0)),
        ],
        out_specs=[
            pair_spec(rows, 1, 0),
            pl.BlockSpec((1, 2, rows), lambda p: (p, 0, 0)),
        ],
        out_shape=[
            jax.ShapeDtypeStruct((rows, count * LANES), BF16),
            jax.ShapeDtypeStruct((count, 2, rows), F32),
        ],
        compiler_params=pltpu.CompilerParams(vmem_limit_bytes=VMEM),
        cost_estimate=LIGHT,
        name="attend",
    )(queries, pairs, pairs, query_mark, key_mark)


def chip_attend_back_kernel(causal, fused, *refs):
    q_ref, k_ref, v_ref, qa_ref, ka_ref, lse_ref, o_ref, do_ref = refs[:8]
    outs, (dk_acc, dv_acc) = refs[8:-2], refs[-2:]
    rows = q_ref.shape[0]
    block = 256
    low_half = lax.broadcasted_iota(jnp.int32, (1, LANES), 1) < HEAD_DIM
    zero = jnp.zeros((), BF16)
    dk_acc[...] = jnp.zeros_like(dk_acc)
    dv_acc[...] = jnp.zeros_like(dv_acc)
    for start in range(0, rows, block):
        keys = start + block if causal else k_ref.shape[0]
        span = pl.ds(start, block)
        query = q_ref[span, :] * BF16(SCALE)
        query_mark = qa_ref[span, :]
        key_block = k_ref[:keys, :]
        key_mark = ka_ref[:keys, :]
        values = v_ref[:keys, :]
        d_out = do_ref[span, :]
        inner = (d_out.astype(F32) * o_ref[span, :].astype(F32)).T
        d_query = None
        for head in range(2):
            keep = low_half if head == 0 else jnp.logical_not(low_half)
            delta = jnp.sum(
                inner[head * HEAD_DIM : (head + 1) * HEAD_DIM], axis=0, keepdims=True
            )
            scores = mxu(
                jnp.where(keep, key_block, key_mark), jnp.where(keep, query, query_mark), NT
            )
            if causal:
                scores = jnp.where(
                    lax.broadcasted_iota(jnp.int32, (keys, block), 0)
                    <= start + lax.broadcasted_iota(jnp.int32, (keys, block), 1),
                    scores,
                    NEG,
                )
            probs = jnp.exp(scores - lse_ref[0, head : head + 1, span])
            own_out = jnp.where(keep, d_out, zero)
            d_probs = mxu(values, own_out, NT)
            d_scores = (probs * (d_probs - delta)).astype(BF16)
            dv_acc[:keys, :] += mxu(probs.astype(BF16), own_out, NN)
            dk_acc[:keys, :] += mxu(d_scores, jnp.where(keep, query, zero), NN)
            term = mxu(jnp.where(keep, key_block, zero), d_scores, TN)
            d_query = term if d_query is None else d_query + term
        outs[0][span, :LANES] = (d_query * SCALE).T.astype(BF16)
    if fused:
        outs[0][:, LANES : 2 * LANES] = dk_acc[...].astype(BF16)
        outs[0][:, 2 * LANES :] = dv_acc[...].astype(BF16)
    else:
        outs[1][:, :LANES] = dk_acc[...].astype(BF16)
        outs[1][:, LANES:] = dv_acc[...].astype(BF16)


def chip_attend_back(
    queries, q_at, pairs, k_at, v_at, query_mark, key_mark, causal, log_total, mixed, d_mixed, fused
):
    rows = queries.shape[0]
    keys = pairs.shape[0]
    count = mixed.shape[1] // LANES

    def out(rows, blocks):
        return (
            pl.BlockSpec((rows, blocks * LANES), lambda p: (0, p)),
            jax.ShapeDtypeStruct((rows, count * blocks * LANES), BF16),
        )

    outs = [out(rows, 3)] if fused else [out(rows, 1), out(keys, 2)]
    return pl.pallas_call(
        functools.partial(chip_attend_back_kernel, causal, fused),
        grid=(count,),
        in_specs=[
            pair_spec(rows, *q_at),
            pair_spec(keys, *k_at),
            pair_spec(keys, *v_at),
            pl.BlockSpec((rows, LANES), lambda p: (0, 0)),
            pl.BlockSpec((keys, LANES), lambda p: (0, 0)),
            pl.BlockSpec((1, 2, rows), lambda p: (p, 0, 0)),
            pair_spec(rows, 1, 0),
            pair_spec(rows, 1, 0),
        ],
        out_specs=[spec for spec, _ in outs],
        out_shape=[shape for _, shape in outs],
        scratch_shapes=[pltpu.VMEM((keys, LANES), F32), pltpu.VMEM((keys, LANES), F32)],
        compiler_params=pltpu.CompilerParams(vmem_limit_bytes=VMEM),
        cost_estimate=LIGHT,
        name="attend_back",
    )(queries, pairs, pairs, query_mark, key_mark, log_total, mixed, d_mixed)


def piece_kernel(kind, low, high, count, x_ref, *refs):
    if count == 1:
        order_ref, stack_ref, rest = refs[0], refs[1], refs[2:]
        weights = [stack_ref.at[order_ref[i]] for i in range(stack_ref.shape[0])]
    else:
        weights, rest = refs[:count], refs[count:]
    own = high - low
    total = None
    for i, ref in enumerate(weights):
        span = pl.ds(i * own, own)
        if kind == "columns":
            rest[-1][:, span] = mxu(x_ref[...], ref[:, low:high], NN).astype(BF16)
        elif kind == "gelu":
            inner = mxu(x_ref[...], ref[:, low:high], NN)
            below = 0.5 + 0.5 * lax.erf(inner * (0.5**0.5))
            rest[0][:, span] = (inner * below).astype(BF16)
            bell = jnp.exp(inner * inner * (-0.5)) * (0.5 / jnp.pi) ** 0.5
            rest[1][:, span] = (below + inner * bell).astype(BF16)
        elif kind == "rows":
            term = mxu(x_ref[:, span], ref[low:high, :], NN)
            total = term if total is None else total + term
        elif kind == "columns_back":
            term = mxu(x_ref[:, span], ref[:, low:high], NT)
            total = term if total is None else total + term
        elif kind == "rows_back":
            rest[-1][:, span] = mxu(x_ref[...], ref[low:high, :], NT).astype(BF16)
        elif kind == "rows_back_slope":
            term = mxu(x_ref[...], ref[low:high, :], NT)
            rest[-1][:, span] = (term * rest[0][:, span].astype(F32)).astype(BF16)
    if total is not None:
        rest[-1][...] = total.astype(BF16)


def piece_product(kind, rows_in, pieces, low, high, slope=None, block=512):
    rows, depth = rows_in.shape
    stacked = len(pieces) == 2
    shape = pieces[1].shape[1:] if stacked else pieces[0].shape
    all_own = 4 * (high - low)
    width = {
        "columns": all_own,
        "gelu": all_own,
        "rows": shape[1],
        "columns_back": shape[0],
        "rows_back": all_own,
        "rows_back_slope": all_own,
    }[kind]
    outs = 2 if kind == "gelu" else 1
    out = pl.BlockSpec((block, width), lambda i: (i, 0))
    results = pl.pallas_call(
        functools.partial(piece_kernel, kind, low, high, 1 if stacked else len(pieces)),
        grid=(rows // block,),
        in_specs=[pl.BlockSpec((block, depth), lambda i: (i, 0))]
        + (
            [
                pl.BlockSpec(memory_space=pltpu.SMEM),
                pl.BlockSpec(pieces[1].shape, lambda i: (0, 0, 0)),
            ]
            if stacked
            else [pl.BlockSpec(piece.shape, lambda i: (0, 0)) for piece in pieces]
        )
        + ([] if slope is None else [out]),
        out_specs=[out] * outs,
        out_shape=[jax.ShapeDtypeStruct((rows, width), BF16)] * outs,
        compiler_params=pltpu.CompilerParams(vmem_limit_bytes=VMEM),
        cost_estimate=LIGHT,
        name="product_" + kind,
    )(rows_in, *pieces, *([] if slope is None else [slope]))
    return results if outs > 1 else results[0]


def weight_kernel(count, *refs):
    out_ref = refs[-1]
    at = 0
    for i in range(count):
        own = refs[i].shape[1]
        out_ref[pl.ds(at, own), :] = mxu(refs[i][...], refs[count + i][...], TN).astype(BF16)
        at += own


def weight_grads(pairs, part):
    rows, width = pairs[0][1].shape
    owns = [hidden.shape[1] // 4 for hidden, _ in pairs]
    return pl.pallas_call(
        functools.partial(weight_kernel, len(pairs)),
        grid=(2,),
        in_specs=[
            pl.BlockSpec((rows, own), lambda i: (0, 2 * part + i)) for own in owns
        ]
        + [pl.BlockSpec((rows, width), lambda i: (0, 0)) for _ in pairs],
        out_specs=pl.BlockSpec((sum(owns), width), lambda i: (i, 0)),
        out_shape=jax.ShapeDtypeStruct((2 * sum(owns), width), BF16),
        compiler_params=pltpu.CompilerParams(vmem_limit_bytes=VMEM),
        cost_estimate=LIGHT,
        name="weight_grads",
    )(*[hidden for hidden, _ in pairs], *[wide for _, wide in pairs])


CROSS = ("seq", "tensor")


class Chip:
    def __init__(self):
        self.core = lax.axis_index("seq")
        self.place = lax.axis_index("tensor")
        self.line = lax.axis_index("dp")
        self.first = [(i, i ^ 1) for i in range(4)] + [(4 + i, 4 + (i ^ 2)) for i in range(4)]
        self.second = [(i, i ^ 2) for i in range(4)] + [(4 + i, 4 + (i ^ 1)) for i in range(4)]

    def other(self, block):
        return lax.ppermute(block, "seq", swap_pairs(2, 1))

    def gather(self, block):
        near = lax.ppermute(block, CROSS, self.first)
        side = lax.ppermute(block, CROSS, self.second)
        far = lax.ppermute(side, CROSS, self.first)
        return [block, side, near, far]

    def ordered(self, own, other, index):
        first = index == 0
        return jnp.concatenate([jnp.where(first, own, other), jnp.where(first, other, own)], 0)

    def swap_start(self, blocks):
        near_bit = 1 + self.core

        def to(bits):
            return lax.dynamic_index_in_dim(blocks, jnp.bitwise_xor(self.place, bits), 0)

        cuts = lax.optimization_barrier((to(0), to(near_bit), to(3 - near_bit), to(3)))
        far = lax.ppermute(cuts[3], "tensor", swap_pairs(4, 3))
        return cuts[0], self.send_near(cuts[1]), self.send_side(cuts[2]), far

    def swap_end(self, parts):
        own, near, side, far = parts
        low, high = lax.rem(self.place, 2), self.place // 2
        first = self.core == 0
        beside, across = jnp.where(first, near, side), jnp.where(first, side, near)
        blocks = self.ordered(self.ordered(own, beside, low), self.ordered(across, far, low), high)
        return blocks.reshape(-1, own.shape[2]) if own.ndim == 3 else blocks

    def swap_rows(self, block):
        return self.swap_end(self.swap_start(block))

    def both_cores(self, rows):
        return self.ordered(rows, self.other(rows), self.core)

    def from_start(self, rows):
        half = rows.shape[0] // 2
        own = lax.dynamic_slice_in_dim(rows, self.core * half, half, 0)
        return self.swap_start(own.reshape(4, half // 4, -1))

    def from_end(self, parts):
        return self.swap_end(parts).reshape((4,) + parts[0].shape[1:])

    def from_slot(self, rows):
        return self.from_end(self.from_start(rows))

    def send_near(self, block):
        return lax.ppermute(block, CROSS, self.first)

    def send_side(self, block):
        return lax.ppermute(block, CROSS, self.second)

    def along(self, block, bit):
        return lax.ppermute(block, "dp", swap_pairs(4, bit))


def add_low(left, right):
    return (left.astype(F32) + right.astype(F32)).astype(BF16)


def chip_local(
    source,
    target,
    out_grad,
    source_segments,
    target_segments,
    enc_gain,
    enc_shift,
    enc_qkv,
    enc_proj,
    enc_up,
    enc_down,
    dec_gain,
    dec_shift,
    dec_self_qkv,
    dec_self_proj,
    dec_cross_q,
    dec_cross_kv,
    dec_cross_proj,
    dec_up,
    dec_down,
):
    chip = Chip()
    core = chip.core
    tie = lax.optimization_barrier

    def own_columns(weight):
        part = weight.shape[-1] // 2
        cut = lax.dynamic_slice_in_dim(weight, core * part, part, weight.ndim - 1)
        return cut.reshape(weight.shape[0], -1)

    def own_rows(weight):
        part = weight.shape[0] // 2
        return lax.dynamic_slice_in_dim(weight, core * part, part, 0)

    def pin(value, *others):
        return tie((value,) + others)[0]

    bundles = [
        own_columns(enc_qkv),
        own_columns(dec_self_qkv),
        jnp.concatenate([own_rows(enc_proj), own_rows(dec_self_proj), own_rows(dec_cross_proj)], 0),
        jnp.concatenate([own_columns(dec_cross_q), own_columns(dec_cross_kv)], 1),
        own_rows(dec_down),
    ]
    near_bit = 1 + core
    order = jnp.bitwise_xor(
        chip.place, jnp.stack([0 * core, 3 - near_bit, near_bit, 0 * core + 3])
    ).astype(jnp.int32)

    def all_groups(own):
        return [order, lax.all_gather(own, "tensor", axis=0)]

    inner = enc_up.shape[1] // 2
    pieces = [None] * len(bundles)

    def launch(index, *after):
        own = pin(bundles[index], *after)
        pieces[index] = [own, chip.send_side(own), chip.send_near(own)]
        return pieces[index][1]

    def relay(index, value):
        side, near, value = tie((pieces[index][1], pieces[index][2], value))
        pieces[index][1:] = [side, near]
        pieces[index].append(chip.send_near(side))
        return value

    def arrived(index, value):
        tied = tie(tuple(pieces[index]) + (value,))
        pieces[index] = list(tied[:-1])
        return tied[-1]

    def enc(index):
        return enc_gain[index : index + 1], enc_shift[index : index + 1]

    def dec(index):
        return dec_gain[index : index + 1], dec_shift[index : index + 1]

    def part_rows(rows_in, weight, low, high):
        own = piece_product("rows", rows_in, weight, low, high)
        return own, chip.other(own)

    def part_back(grad, weight, low, high):
        own = piece_product("columns_back", grad, weight, low, high)
        return own, chip.other(own)

    fused_at = ((3, 0), (3, 1), (3, 2))

    def attend_self(qkv, marks, causal):
        return chip_attend(
            qkv, fused_at[0], qkv, fused_at[1], fused_at[2], marks[0], marks[1], causal
        )

    launch(0)
    swapped = arrived(0, chip.swap_rows(relay(0, source)))
    launch(1, swapped)
    x_source = chip.both_cores(swapped)
    sent_target = chip.swap_start(pin(target, swapped))
    w_enc_up = all_groups(pin(own_columns(enc_up), swapped))
    source_ids = lax.dynamic_index_in_dim(source_segments, chip.place, 0, keepdims=False)
    target_ids = lax.dynamic_index_in_dim(target_segments, chip.place, 0, keepdims=False)
    ids = jnp.arange(LANES, dtype=jnp.int32)[None] % HEAD_DIM
    counted = ids < IDS
    source_query = jnp.where(source_ids[:, None] == ids, NEG, 0.0).astype(BF16)
    target_query = jnp.where(target_ids[:, None] == ids, NEG, 0.0).astype(BF16)
    source_key = ((source_ids[:, None] != ids) & counted).astype(BF16)
    target_key = ((target_ids[:, None] != ids) & counted).astype(BF16)
    rows_a = norm_rows(x_source, *enc(0))
    rows_a = pin(rows_a, source_query, source_key)
    qkv_a = piece_product("columns", rows_a, pieces[0], 0, bundles[0].shape[1])
    launch(2, qkv_a)
    mixed_a, total_a = attend_self(qkv_a, (source_query, source_key), False)
    mixed_a, sent_target = tie((relay(1, mixed_a), sent_target))
    x_target = chip.both_cores(chip.swap_end(sent_target))
    w_enc_down = all_groups(pin(own_rows(enc_down), mixed_a))
    rows_c = norm_rows(pin(x_target, target_query, target_key), *dec(0))
    rows_c = arrived(1, rows_c)
    qkv_c = piece_product("columns", rows_c, pieces[1], 0, bundles[1].shape[1])
    qkv_c = relay(2, qkv_c)
    w_dec_up = all_groups(pin(own_columns(dec_up), qkv_c))
    mixed_c, total_c = attend_self(qkv_c, (target_query, target_key), True)
    proj_rows = bundles[2].shape[0] // 3
    mixed_c, mixed_a = tie((arrived(2, mixed_c), mixed_a))
    launch(3, mixed_c)
    own_a, other_a = part_rows(mixed_a, pieces[2], 0, proj_rows)
    own_c, other_c = part_rows(mixed_c, pieces[2], proj_rows, 2 * proj_rows)
    other_a, other_c = tie((other_a, other_c, own_a, own_c))[:2]
    hidden, rows_b = add_norm(x_source, own_a, other_a, *enc(1))
    after_self, rows_e = add_norm(x_target, own_c, other_c, *dec(1))
    rows_b = pin(rows_b, rows_e)
    active_b, slope_b = piece_product("gelu", rows_b, w_enc_up, 0, inner, block=256)
    active_b = relay(3, active_b)
    encoded, rows_m = add_norm(hidden, *part_rows(active_b, w_enc_down, 0, inner), *enc(2))
    rows_m, rows_e = tie((arrived(3, rows_m), rows_e))
    launch(4, rows_m)
    head_width = dec_cross_q.shape[1] // 2
    pairs_m = piece_product("columns", rows_m, pieces[3], head_width, 3 * head_width)
    query_e = piece_product("columns", rows_e, pieces[3], 0, head_width)
    query_e = pin(query_e, pairs_m)
    mixed_e, total_e = chip_attend(
        query_e, (1, 0), pairs_m, (2, 0), (2, 1), target_query, source_key, False
    )
    mixed_e = relay(4, mixed_e)
    after_cross, rows_f = add_norm(
        after_self, *part_rows(mixed_e, pieces[2], 2 * proj_rows, 3 * proj_rows), *dec(2)
    )
    sent_grad = chip.swap_start(pin(out_grad, rows_f))
    active_f, slope_f = piece_product("gelu", rows_f, w_dec_up, 0, inner, block=256)
    active_f, sent_grad = tie((arrived(4, active_f), sent_grad))
    cotangent = chip.both_cores(chip.swap_end(sent_grad))
    w_dec_down = pieces[4]
    decoded, d_final, low_final, gain_d3, shift_d3 = last_norm(
        after_cross, *part_rows(active_f, w_dec_down, 0, inner), cotangent, *dec(3)
    )


    low_bit = lax.rem(chip.line, 2)
    high_bit = chip.line // 2

    def here(value, step, *args):
        args, value = tie((args, value))
        *result, sent = step(*args)
        return pin(value, result[1], *sent), result

    def to_side(came, kept):
        half = kept.shape[0] // 2
        sent = add_low(kept[half:], came[half:])
        return chip.send_side(sent), add_low(kept[:half], came[:half]), [sent]

    def to_line(*states):
        def cut(bits):
            parts = []
            for came, kept in states:
                quarter = kept.shape[0] // 4
                at = jnp.bitwise_xor(chip.line, bits) * quarter
                parts.append(
                    add_low(
                        lax.dynamic_slice_in_dim(kept, at, quarter, 0),
                        lax.dynamic_slice_in_dim(came, at, quarter, 0),
                    )
                )
            return jnp.concatenate(parts, 0)

        sent = [cut(bits) for bits in (3, 2, 1)]
        return [chip.along(part, bits) for part, bits in zip(sent, (3, 2, 1))], cut(0), sent

    def from_line(came, own):
        total = own.astype(F32)
        for block in came:
            total = total + block.astype(F32)
        own = total.astype(BF16)
        return [chip.along(own, bits) for bits in (3, 2, 1)], own, []

    def to_core(came, own):
        far, next_but_one, next_one = came
        first = chip.ordered(own, next_one, low_bit)
        second = chip.ordered(next_but_one, far, low_bit)
        return share(chip.ordered(first, second, high_bit))

    def share(whole):
        width = whole.shape[1] // 2
        sent = lax.dynamic_slice_in_dim(whole, (1 - core) * width, width, 1)
        own = lax.dynamic_slice_in_dim(whole, core * width, width, 1)
        return chip.other(sent), own

    def in_place(came, own):
        return chip.ordered(own[None], came[None], core)

    def sum_line(*states):
        total = jnp.concatenate([add_low(*state) for state in states], 0)
        return None, total, []

    def send_half(value, *pairs):
        sent = weight_grads(list(pairs), 1)
        return pin(value, sent), chip.send_near(sent)

    def keep_half(value, came, *pairs):
        first, value = tie((pairs[0], value))
        kept = weight_grads([first] + list(pairs[1:]), 0)
        return pin(value, kept), (came, kept)

    def ffn_back(low_out, slope, weight):
        return piece_product("rows_back_slope", low_out, weight, 0, inner, slope)

    low_send, near_fd = send_half(low_final, (active_f, low_final))
    d_inner_f = ffn_back(low_send, slope_f, w_dec_down)
    d_inner_f, near_fu = send_half(d_inner_f, (d_inner_f, rows_f))
    own = piece_product("columns_back", d_inner_f, w_dec_up, 0, inner)
    own, near_fd = tie((own, near_fd))
    other = chip.other(own)
    hold, keep_fd = keep_half(own, near_fd, (active_f, low_final))
    hold, side_fd = here(hold, to_side, *keep_fd)
    hold, keep_fu = keep_half(hold, near_fu, (d_inner_f, rows_f))
    d_cross, low_cross, gain_d2, shift_d2 = norm_back_rows(
        after_cross, own, pin(other, hold), dec(2)[0], d_final, [F32, BF16]
    )
    d_mixed = piece_product("rows_back", low_cross, pieces[2], 2 * proj_rows, 3 * proj_rows)
    d_mixed, side_fu = here(d_mixed, to_side, *keep_fu)
    d_query_e, d_pairs_m = chip_attend_back(
        query_e,
        (1, 0),
        pairs_m,
        (2, 0),
        (2, 1),
        target_query,
        source_key,
        False,
        total_e,
        mixed_e,
        d_mixed,
        False,
    )
    d_pairs_m, (_, total_f) = here(d_pairs_m, sum_line, side_fd, side_fu)
    sum_f = lax.psum(total_f, "dp")
    own_m, other_m = part_back(d_pairs_m, pieces[3], head_width, 3 * head_width)
    own_e, other_e = part_back(pin(d_query_e, own_m), pieces[3], 0, head_width)
    d_encoded, low_encoded, gain_e2, shift_e2 = norm_back_rows(
        encoded, own_m, pin(other_m, own_e), enc(2)[0], None, [F32, BF16]
    )
    low_send, near_bd = send_half(low_encoded, (active_b, low_encoded))
    d_inner_b = ffn_back(low_send, slope_b, w_enc_down)
    d_inner_b, near_bu = send_half(d_inner_b, (d_inner_b, rows_b))
    own = piece_product("columns_back", d_inner_b, w_enc_up, 0, inner)
    own, near_bd, other_e = tie((own, near_bd, other_e))
    other = chip.other(own)
    hold, keep_bd = keep_half(own, near_bd, (active_b, low_encoded))
    hold, side_bd = here(hold, to_side, *keep_bd)
    hold, keep_bu = keep_half(hold, near_bu, (d_inner_b, rows_b))
    d_hidden, low_hidden, gain_e1, shift_e1 = norm_back_rows(
        hidden, own, pin(other, hold), enc(1)[0], d_encoded, [F32, BF16]
    )
    pairs_x = ((mixed_e, low_cross), (d_query_e, rows_e), (d_pairs_m, rows_m))
    own_e, side_bu = here(pin(own_e, low_hidden), to_side, *keep_bu)
    pairs_x = tie((pairs_x, own_e))[0]
    own_e, near_x = send_half(own_e, *pairs_x)
    own_e, keep_x = keep_half(own_e, near_x, *pairs_x)
    d_self, low_self, gain_d1, shift_d1 = norm_back_rows(
        after_self, own_e, other_e, dec(1)[0], d_cross, [F32, BF16]
    )

    def self_back(d_mixed, qkv, marks, causal, totals, mixed):
        (d_qkv,) = chip_attend_back(
            qkv,
            fused_at[0],
            qkv,
            fused_at[1],
            fused_at[2],
            marks[0],
            marks[1],
            causal,
            totals,
            mixed,
            d_mixed,
            True,
        )
        return d_qkv

    d_mixed = piece_product("rows_back", low_self, pieces[2], proj_rows, 2 * proj_rows)
    d_mixed, (_, total_b) = here(d_mixed, sum_line, side_bd, side_bu)
    d_qkv_c = self_back(d_mixed, qkv_c, (target_query, target_key), True, total_c, mixed_c)
    d_qkv_c, sum_f, total_b = tie((d_qkv_c, sum_f, total_b))
    sum_b = lax.psum(total_b, "dp")
    d_qkv_c, side_x = here(d_qkv_c, to_side, *keep_x)
    pairs_c = ((mixed_c, low_self), (d_qkv_c, rows_c))
    d_qkv_c, near_c = send_half(d_qkv_c, *pairs_c)
    own_c = piece_product("columns_back", d_qkv_c, pieces[1], 0, 3 * head_width)
    own_c, keep_c = keep_half(own_c, near_c, *pairs_c)
    low_hidden, decoded = tie((low_hidden, decoded, own_c))[:2]
    sent_decoded = chip.from_start(decoded)
    d_mixed = piece_product("rows_back", low_hidden, pieces[2], 0, proj_rows)
    d_qkv_a = self_back(d_mixed, qkv_a, (source_query, source_key), False, total_a, mixed_a)
    pairs_a = ((mixed_a, low_hidden), (d_qkv_a, rows_a))
    d_qkv_a, near_a = send_half(d_qkv_a, *pairs_a)
    d_qkv_a, side_c = here(d_qkv_a, to_side, *keep_c)
    own_a = piece_product("columns_back", d_qkv_a, pieces[0], 0, 3 * head_width)
    own_a, (_, total_xc) = here(own_a, sum_line, side_x, side_c)
    own_a, sum_b, total_xc, sent_decoded, near_a = tie(
        (own_a, sum_b, total_xc, sent_decoded, near_a)
    )
    decoded = chip.from_end(sent_decoded)
    sum_xc = lax.psum(total_xc, "dp")
    other_a, other_c = chip.other(own_a), chip.other(pin(own_c, own_a))
    own_a, keep_a = keep_half(own_a, near_a, *pairs_a)
    own_a, side_a = here(own_a, to_side, *keep_a)
    source_grad, gain_e0, shift_e0 = norm_back_rows(
        x_source, own_a, other_a, enc(0)[0], d_hidden, [BF16]
    )
    own_c = pin(own_c, source_grad)
    target_grad, gain_d0, shift_d0 = norm_back_rows(
        x_target, own_c, other_c, dec(0)[0], d_self, [BF16]
    )
    gain_d0, line_a = here(gain_d0, to_line, side_a)
    source_grad = chip.from_slot(pin(source_grad, gain_d0))
    target_grad = chip.from_slot(pin(target_grad, gain_d0))
    line_a, sum_xc = tie((line_a, sum_xc))

    norms = jnp.concatenate(
        [
            gain_e0,
            gain_e1,
            gain_e2,
            shift_e0,
            shift_e1,
            shift_e2,
            gain_d0,
            gain_d1,
            gain_d2,
            gain_d3,
            shift_d0,
            shift_d1,
            shift_d2,
            shift_d3,
        ],
        0,
    )
    part = norms.shape[1] // 2
    norms = lax.dynamic_slice_in_dim(norms, core * part, part, 1)
    norms = norms + chip.send_near(norms)
    norms = norms + chip.send_side(norms)
    norms = norms + chip.along(norms, 1)
    norms = norms + chip.along(norms, 2)
    line_a = from_line(*line_a)[:2]
    line_a = to_core(*line_a)

    def wide(block, blocks):
        cores, rows, width = block.shape
        block = block.reshape(cores, blocks, rows // blocks, width)
        return jnp.transpose(block, (3, 1, 0, 2)).reshape(width, blocks, -1).astype(F32)

    def tall(block):
        return block.reshape(-1, block.shape[2]).astype(F32)

    n = proj_rows
    done_f, done_b = in_place(*share(sum_f)), in_place(*share(sum_b))
    done_xc, done_a = in_place(*share(sum_xc)), in_place(*line_a)
    done_x, done_c = done_xc[:, : 4 * n], done_xc[:, 4 * n :]
    source_grad, target_grad = source_grad.astype(F32), target_grad.astype(F32)
    hid = done_f.shape[1] // 2
    return (
        decoded,
        source_grad,
        target_grad,
        norms[0:3],
        norms[3:6],
        wide(done_a[:, n:], 3),
        tall(done_a[:, :n]),
        wide(done_b[:, inner:], 1)[:, 0],
        tall(done_b[:, :inner]),
        norms[6:10],
        norms[10:14],
        wide(done_c[:, n:], 3),
        tall(done_c[:, :n]),
        wide(done_x[:, n : n + head_width], 1)[:, 0],
        wide(done_x[:, n + head_width :], 2),
        tall(done_x[:, :n]),
        wide(done_f[:, hid:], 1)[:, 0],
        tall(done_f[:, :hid]),
    )


def solution(mesh):
    rows = P("dp", ("seq", "tensor"), None)
    segments = P("dp", None)
    shape = dict(mesh.shape)
    chips = shape["dp"] == 4 and shape["seq"] == 2 and shape["tensor"] == 4
    return jax.shard_map(
        chip_local if chips else local,
        mesh=mesh,
        in_specs=(
            rows,
            rows,
            rows,
            segments,
            segments,
            P(),
            P(),
            P(None, None, "tensor"),
            P("tensor", None),
            P(None, "tensor"),
            P("tensor", None),
            P(),
            P(),
            P(None, None, "tensor"),
            P("tensor", None),
            P(None, "tensor"),
            P(None, None, "tensor"),
            P("tensor", None),
            P(None, "tensor"),
            P("tensor", None),
        ),
        out_specs=(
            rows,
            rows,
            rows,
            P(None, "seq"),
            P(None, "seq"),
            P("seq", None, "tensor"),
            P("tensor", "seq"),
            P("seq", "tensor"),
            P("tensor", "seq"),
            P(None, "seq"),
            P(None, "seq"),
            P("seq", None, "tensor"),
            P("tensor", "seq"),
            P("seq", "tensor"),
            P("seq", None, "tensor"),
            P("tensor", "seq"),
            P("seq", "tensor"),
            P("tensor", "seq"),
        ),
        check_vma=False,
    )
```

```python
import functools

import jax
import jax.numpy as jnp
from jax import lax
from jax.experimental import pallas as pl
from jax.experimental.pallas import tpu as pltpu
from jax.sharding import PartitionSpec as P

HEAD_DIM = 64
LANES = 128
IDS = 9
EPS = 1e-05
NEG = -1e30
SCALE = HEAD_DIM ** (-0.5)
F32 = jnp.float32
BF16 = jnp.bfloat16
NT = (((1,), (1,)), ((), ()))
NN = (((1,), (0,)), ((), ()))
TN = (((0,), (0,)), ((), ()))


def mxu(left, right, dims):
    return lax.dot_general(left, right, dims, preferred_element_type=F32)


def layer_norm(inputs, norm_gain, norm_shift):
    row_mean = jnp.mean(inputs, -1, keepdims=True)
    centred = inputs - row_mean
    spread = jnp.mean(centred * centred, -1, keepdims=True)
    return centred * lax.rsqrt(spread + EPS) * norm_gain + norm_shift


def exact_gelu(inputs):
    return jax.nn.gelu(inputs, approximate=False)


def norm_back(inputs, norm_gain, norm_shift, cotangent):
    _, pullback = jax.vjp(layer_norm, inputs, norm_gain, norm_shift)
    return pullback(cotangent)


def project(rows, weight):
    return mxu(rows, weight, NN)


def back_project(grad, weight):
    return mxu(grad, weight, NT)


def weight_grad(rows, grad):
    return mxu(rows, grad, TN).astype(BF16)


def attend_kernel(causal, first_ref, q_ref, k_ref, v_ref, qa_ref, ka_ref, o_ref, lse_ref):
    rows = q_ref.shape[0]
    keys = k_ref.shape[0]
    block = min(rows, 256)
    low_half = lax.broadcasted_iota(jnp.int32, (1, LANES), 1) < HEAD_DIM
    key_block = k_ref[...]
    key_mark = ka_ref[...]
    values = v_ref[...]
    for start in range(0, rows, block):
        query = q_ref[pl.ds(start, block), :] * BF16(SCALE)
        query_mark = qa_ref[pl.ds(start, block), :]
        halves = []
        lses = []
        for head in range(2):
            keep = low_half if head == 0 else jnp.logical_not(low_half)
            scores = mxu(
                jnp.where(keep, query, query_mark), jnp.where(keep, key_block, key_mark), NT
            )
            if causal:
                place = (
                    first_ref[0] + start + lax.broadcasted_iota(jnp.int32, (block, keys), 0)
                )
                scores = jnp.where(
                    lax.broadcasted_iota(jnp.int32, (block, keys), 1) <= place, scores, NEG
                )
            top = jnp.max(scores, -1, keepdims=True)
            weights = jnp.exp(scores - top)
            total = jnp.sum(weights, -1, keepdims=True)
            mixed = mxu(weights.astype(BF16), values, NN)
            halves.append(mixed / total)
            lses.append(top + jnp.log(total))
        o_ref[pl.ds(start, block), :] = jnp.where(low_half, halves[0], halves[1]).astype(BF16)
        both = jnp.where(low_half, lses[0], lses[1])
        turned = both.T
        lse_ref[0, 0:1, pl.ds(start, block)] = turned[0:1]
        lse_ref[0, 1:2, pl.ds(start, block)] = turned[HEAD_DIM : HEAD_DIM + 1]


def attend(queries, keys, values, query_mark, key_mark, first_row, causal):
    rows, width = queries.shape
    key_rows = keys.shape[0]
    pairs = width // LANES
    return pl.pallas_call(
        functools.partial(attend_kernel, causal),
        grid_spec=pltpu.PrefetchScalarGridSpec(
            num_scalar_prefetch=1,
            grid=(pairs,),
            in_specs=[
                pl.BlockSpec((rows, LANES), lambda p, first: (0, p)),
                pl.BlockSpec((key_rows, LANES), lambda p, first: (0, p)),
                pl.BlockSpec((key_rows, LANES), lambda p, first: (0, p)),
                pl.BlockSpec((rows, LANES), lambda p, first: (0, 0)),
                pl.BlockSpec((key_rows, LANES), lambda p, first: (0, 0)),
            ],
            out_specs=[
                pl.BlockSpec((rows, LANES), lambda p, first: (0, p)),
                pl.BlockSpec((1, 2, rows), lambda p, first: (p, 0, 0)),
            ],
        ),
        out_shape=[
            jax.ShapeDtypeStruct((rows, width), BF16),
            jax.ShapeDtypeStruct((pairs, 2, rows), F32),
        ],
        compiler_params=pltpu.CompilerParams(vmem_limit_bytes=40 << 20),
        cost_estimate=pl.CostEstimate(
            flops=4 * rows * key_rows * width * 2,
            bytes_accessed=4 * rows * width + 4 * key_rows * width,
            transcendentals=rows * key_rows * width // HEAD_DIM,
        ),
        name="attend",
    )(first_row, queries, keys, values, query_mark, key_mark)


def attend_back_kernel(
    causal,
    first_ref,
    q_ref,
    k_ref,
    v_ref,
    qa_ref,
    ka_ref,
    lse_ref,
    o_ref,
    do_ref,
    dq_ref,
    dk_ref,
    dv_ref,
    dk_acc,
    dv_acc,
):
    rows = q_ref.shape[0]
    keys = k_ref.shape[0]
    block = min(rows, 256)
    low_half = lax.broadcasted_iota(jnp.int32, (1, LANES), 1) < HEAD_DIM
    key_block = k_ref[...]
    key_mark = ka_ref[...]
    values = v_ref[...]
    zero = jnp.zeros((), BF16)
    dk_acc[...] = jnp.zeros_like(dk_acc)
    dv_acc[...] = jnp.zeros_like(dv_acc)
    for start in range(0, rows, block):
        span = pl.ds(start, block)
        query = q_ref[span, :] * BF16(SCALE)
        query_mark = qa_ref[span, :]
        d_out = do_ref[span, :]
        inner = (d_out.astype(F32) * o_ref[span, :].astype(F32)).T
        d_query = None
        for head in range(2):
            keep = low_half if head == 0 else jnp.logical_not(low_half)
            delta = jnp.sum(
                inner[head * HEAD_DIM : (head + 1) * HEAD_DIM], axis=0, keepdims=True
            )
            scores = mxu(
                jnp.where(keep, key_block, key_mark), jnp.where(keep, query, query_mark), NT
            )
            if causal:
                place = (
                    first_ref[0] + start + lax.broadcasted_iota(jnp.int32, (keys, block), 1)
                )
                scores = jnp.where(
                    lax.broadcasted_iota(jnp.int32, (keys, block), 0) <= place, scores, NEG
                )
            probs = jnp.exp(scores - lse_ref[0, head : head + 1, span])
            own_out = jnp.where(keep, d_out, zero)
            d_probs = mxu(values, own_out, NT)
            d_scores = (probs * (d_probs - delta)).astype(BF16)
            dv_acc[...] += mxu(probs.astype(BF16), own_out, NN)
            dk_acc[...] += mxu(d_scores, jnp.where(keep, query, zero), NN)
            term = mxu(jnp.where(keep, key_block, zero), d_scores, TN)
            d_query = term if d_query is None else d_query + term
        dq_ref[span, :] = (d_query * SCALE).T.astype(BF16)
    dk_ref[...] = dk_acc[...].astype(BF16)
    dv_ref[...] = dv_acc[...].astype(BF16)


def attend_back(
    queries, keys, values, query_mark, key_mark, first_row, causal, log_total, mixed, d_mixed
):
    rows, width = queries.shape
    key_rows = keys.shape[0]
    pairs = width // LANES
    row_spec = pl.BlockSpec((rows, LANES), lambda p, first: (0, p))
    key_spec = pl.BlockSpec((key_rows, LANES), lambda p, first: (0, p))
    return pl.pallas_call(
        functools.partial(attend_back_kernel, causal),
        grid_spec=pltpu.PrefetchScalarGridSpec(
            num_scalar_prefetch=1,
            grid=(pairs,),
            in_specs=[
                row_spec,
                key_spec,
                key_spec,
                pl.BlockSpec((rows, LANES), lambda p, first: (0, 0)),
                pl.BlockSpec((key_rows, LANES), lambda p, first: (0, 0)),
                pl.BlockSpec((1, 2, rows), lambda p, first: (p, 0, 0)),
                row_spec,
                row_spec,
            ],
            out_specs=[row_spec, key_spec, key_spec],
            scratch_shapes=[
                pltpu.VMEM((key_rows, LANES), F32),
                pltpu.VMEM((key_rows, LANES), F32),
            ],
        ),
        out_shape=[
            jax.ShapeDtypeStruct((rows, width), BF16),
            jax.ShapeDtypeStruct((key_rows, width), BF16),
            jax.ShapeDtypeStruct((key_rows, width), BF16),
        ],
        compiler_params=pltpu.CompilerParams(vmem_limit_bytes=40 << 20),
        cost_estimate=pl.CostEstimate(
            flops=10 * rows * key_rows * width * 2,
            bytes_accessed=8 * rows * width + 8 * key_rows * width,
            transcendentals=rows * key_rows * width // HEAD_DIM,
        ),
        name="attend_back",
    )(first_row, queries, keys, values, query_mark, key_mark, log_total, mixed, d_mixed)


class Layout:
    def __init__(self, slots):
        self.tensor = lax.axis_size("tensor")
        self.seq = lax.axis_size("seq")
        self.slots = slots
        self.spread = self.tensor // slots
        self.place = lax.axis_index("tensor")
        self.half = lax.axis_index("seq")
        self.row_groups = [
            [j * slots + u for u in range(slots)] for j in range(self.spread)
        ]
        self.slot_groups = [
            [j * slots + u for j in range(self.spread)] for u in range(slots)
        ]

    def to_slots(self, block):
        rows = lax.all_to_all(
            block, "tensor", 0, 1, axis_index_groups=self.row_groups, tiled=True
        )
        return rows.reshape(-1, block.shape[2])

    def from_slots(self, rows):
        block = rows.reshape(1, rows.shape[0], rows.shape[1])
        return lax.all_to_all(
            block, "tensor", 1, 0, axis_index_groups=self.row_groups, tiled=True
        )

    def gather_keys(self, rows):
        if self.spread > 1:
            rows = lax.all_gather(
                rows, "tensor", axis=0, axis_index_groups=self.slot_groups, tiled=True
            )
        return lax.all_gather(rows, "seq", axis=0, tiled=True)

    def scatter_keys(self, rows):
        rows = lax.psum_scatter(rows, "seq", scatter_dimension=0, tiled=True)
        if self.spread > 1:
            rows = lax.psum_scatter(
                rows,
                "tensor",
                scatter_dimension=0,
                axis_index_groups=self.slot_groups,
                tiled=True,
            )
        return rows

    def gather_weight(self, shard):
        part = shard.shape[0] // self.seq
        own = lax.dynamic_slice_in_dim(shard, self.half * part, part, 0)
        return lax.all_gather(own, ("tensor", "seq"), axis=0, tiled=True)

    def gather_columns(self, shard):
        depth, blocks, own = shard.shape
        whole = self.gather_weight(shard.reshape(depth, blocks * own))
        whole = whole.reshape(self.tensor, depth, blocks, own)
        return jnp.transpose(whole, (1, 2, 0, 3)).reshape(depth, blocks * self.tensor * own)

    def reduce_rows(self, gradient):
        rows, width = gradient.shape
        parts = gradient.reshape(self.tensor, rows // self.tensor, self.seq, width // self.seq)
        parts = jnp.transpose(parts, (2, 0, 1, 3)).reshape(
            self.seq * rows, width // self.seq
        )
        return self.reduce(parts)

    def reduce_columns(self, gradient, blocks):
        depth, width = gradient.shape
        own = width // blocks // self.tensor
        parts = gradient.reshape(self.seq, depth // self.seq, blocks, self.tensor, own)
        parts = jnp.transpose(parts, (0, 3, 1, 2, 4)).reshape(
            self.seq * self.tensor * depth // self.seq, blocks * own
        )
        return self.reduce(parts).reshape(depth // self.seq, blocks, own)

    def reduce(self, parts):
        own = lax.psum_scatter(parts, ("seq", "tensor"), scatter_dimension=0, tiled=True)
        return lax.psum(own, "dp").astype(F32)


def local(
    source,
    target,
    out_grad,
    source_segments,
    target_segments,
    enc_gain,
    enc_shift,
    enc_qkv,
    enc_proj,
    enc_up,
    enc_down,
    dec_gain,
    dec_shift,
    dec_self_qkv,
    dec_self_proj,
    dec_cross_q,
    dec_cross_kv,
    dec_cross_proj,
    dec_up,
    dec_down,
):
    width = source.shape[2]
    lay = Layout(source.shape[0])
    w_enc_qkv = lay.gather_columns(enc_qkv)
    w_self_qkv = lay.gather_columns(dec_self_qkv)
    w_enc_proj = lay.gather_weight(enc_proj)
    w_self_proj = lay.gather_weight(dec_self_proj)
    w_enc_up = lay.gather_columns(enc_up[:, None])
    w_enc_down = lay.gather_weight(enc_down)
    w_cross_q = lay.gather_columns(dec_cross_q[:, None])
    w_cross_kv = lay.gather_columns(dec_cross_kv)
    w_cross_proj = lay.gather_weight(dec_cross_proj)
    w_dec_up = lay.gather_columns(dec_up[:, None])
    w_dec_down = lay.gather_weight(dec_down)
    slot = lax.rem(lay.place, lay.slots)
    rows = source.shape[1] * lay.slots
    first_row = (lay.half * lay.spread + lay.place // lay.slots) * rows
    source_ids = lax.dynamic_index_in_dim(source_segments, slot, 0, keepdims=False)
    target_ids = lax.dynamic_index_in_dim(target_segments, slot, 0, keepdims=False)
    ids = jnp.arange(LANES, dtype=jnp.int32) % HEAD_DIM
    own_source = lax.dynamic_slice_in_dim(source_ids, first_row, rows, 0)
    own_target = lax.dynamic_slice_in_dim(target_ids, first_row, rows, 0)
    source_query = jnp.where(own_source[:, None] == ids[None], NEG, 0.0).astype(BF16)
    target_query = jnp.where(own_target[:, None] == ids[None], NEG, 0.0).astype(BF16)
    counted = ids[None] < IDS
    source_key = ((source_ids[:, None] != ids[None]) & counted).astype(BF16)
    target_key = ((target_ids[:, None] != ids[None]) & counted).astype(BF16)
    first = first_row[None].astype(jnp.int32)

    x_source = lay.to_slots(source).astype(F32)
    x_target = lay.to_slots(target).astype(F32)
    cotangent = lay.to_slots(out_grad).astype(F32)

    rows_a = layer_norm(x_source, enc_gain[0], enc_shift[0]).astype(BF16)
    qkv_a = project(rows_a, w_enc_qkv).astype(BF16)
    query_a = qkv_a[:, :width]
    pairs_a = lay.gather_keys(qkv_a[:, width:])
    mixed_a, total_a = attend(
        query_a, pairs_a[:, :width], pairs_a[:, width:], source_query, source_key, first, False
    )
    hidden = x_source + project(mixed_a, w_enc_proj)
    rows_c = layer_norm(x_target, dec_gain[0], dec_shift[0]).astype(BF16)
    qkv_c = project(rows_c, w_self_qkv).astype(BF16)
    query_c = qkv_c[:, :width]
    pairs_c = lay.gather_keys(qkv_c[:, width:])
    mixed_c, total_c = attend(
        query_c, pairs_c[:, :width], pairs_c[:, width:], target_query, target_key, first, True
    )
    after_self = x_target + project(mixed_c, w_self_proj)
    rows_b = layer_norm(hidden, enc_gain[1], enc_shift[1]).astype(BF16)
    inner_b = project(rows_b, w_enc_up)
    active_b = exact_gelu(inner_b).astype(BF16)
    encoded = hidden + project(active_b, w_enc_down)
    rows_m = layer_norm(encoded, enc_gain[2], enc_shift[2]).astype(BF16)
    pairs_m = lay.gather_keys(project(rows_m, w_cross_kv).astype(BF16))
    rows_e = layer_norm(after_self, dec_gain[1], dec_shift[1]).astype(BF16)
    query_e = project(rows_e, w_cross_q).astype(BF16)
    mixed_e, total_e = attend(
        query_e, pairs_m[:, :width], pairs_m[:, width:], target_query, source_key, first, False
    )
    after_cross = after_self + project(mixed_e, w_cross_proj)
    rows_f = layer_norm(after_cross, dec_gain[2], dec_shift[2]).astype(BF16)
    inner_f = project(rows_f, w_dec_up)
    active_f = exact_gelu(inner_f).astype(BF16)
    final_rows = after_cross + project(active_f, w_dec_down)
    decoded, final_back = jax.vjp(layer_norm, final_rows, dec_gain[3], dec_shift[3])

    d_final, dec_gain_three, dec_shift_three = final_back(cotangent)

    def ffn_back(d_out, rows_in, inner, active, weight_up, weight_down):
        d_low = d_out.astype(BF16)
        grad_down = lay.reduce_rows(weight_grad(active, d_low))
        d_active = back_project(d_low, weight_down)
        _, gelu_back = jax.vjp(exact_gelu, inner)
        d_inner = gelu_back(d_active)[0].astype(BF16)
        grad_up = lay.reduce_columns(weight_grad(rows_in, d_inner), 1)[:, 0]
        return back_project(d_inner, weight_up), grad_up, grad_down

    d_normed, grad_dec_up, grad_dec_down = ffn_back(
        d_final, rows_f, inner_f, active_f, w_dec_up, w_dec_down
    )
    d_input, dec_gain_two, dec_shift_two = norm_back(
        after_cross, dec_gain[2], dec_shift[2], d_normed
    )
    d_cross = d_final + d_input
    d_low = d_cross.astype(BF16)
    grad_cross_proj = lay.reduce_rows(weight_grad(mixed_e, d_low))
    d_mixed = back_project(d_low, w_cross_proj).astype(BF16)
    d_query, d_keys, d_values = attend_back(
        query_e,
        pairs_m[:, :width],
        pairs_m[:, width:],
        target_query,
        source_key,
        first,
        False,
        total_e,
        mixed_e,
        d_mixed,
    )
    d_pairs = lay.scatter_keys(jnp.concatenate([d_keys, d_values], 1))
    grad_cross_q = lay.reduce_columns(weight_grad(rows_e, d_query), 1)[:, 0]
    grad_cross_kv = lay.reduce_columns(weight_grad(rows_m, d_pairs), 2)
    d_normed = back_project(d_query, w_cross_q)
    d_memory = back_project(d_pairs, w_cross_kv)
    d_input, dec_gain_one, dec_shift_one = norm_back(
        after_self, dec_gain[1], dec_shift[1], d_normed
    )
    d_self = d_cross + d_input
    d_encoded, enc_gain_two, enc_shift_two = norm_back(encoded, enc_gain[2], enc_shift[2], d_memory)
    d_normed, grad_enc_up, grad_enc_down = ffn_back(
        d_encoded, rows_b, inner_b, active_b, w_enc_up, w_enc_down
    )
    d_input, enc_gain_one, enc_shift_one = norm_back(hidden, enc_gain[1], enc_shift[1], d_normed)
    d_hidden = d_encoded + d_input

    def self_back(d_out, rows_in, query, pairs, marks, causal, totals, mixed, w_qkv, w_proj):
        d_low = d_out.astype(BF16)
        grad_proj = lay.reduce_rows(weight_grad(mixed, d_low))
        d_mixed = back_project(d_low, w_proj).astype(BF16)
        d_query, d_keys, d_values = attend_back(
            query,
            pairs[:, :width],
            pairs[:, width:],
            marks[0],
            marks[1],
            first,
            causal,
            totals,
            mixed,
            d_mixed,
        )
        d_pairs = lay.scatter_keys(jnp.concatenate([d_keys, d_values], 1))
        d_qkv = jnp.concatenate([d_query, d_pairs], 1)
        grad_qkv = lay.reduce_columns(weight_grad(rows_in, d_qkv), 3)
        return back_project(d_qkv, w_qkv), grad_qkv, grad_proj

    d_normed, grad_self_qkv, grad_self_proj = self_back(
        d_self,
        rows_c,
        query_c,
        pairs_c,
        (target_query, target_key),
        True,
        total_c,
        mixed_c,
        w_self_qkv,
        w_self_proj,
    )
    d_input, dec_gain_zero, dec_shift_zero = norm_back(
        x_target, dec_gain[0], dec_shift[0], d_normed
    )
    target_grad = d_self + d_input
    d_normed, grad_enc_qkv, grad_enc_proj = self_back(
        d_hidden,
        rows_a,
        query_a,
        pairs_a,
        (source_query, source_key),
        False,
        total_a,
        mixed_a,
        w_enc_qkv,
        w_enc_proj,
    )
    d_input, enc_gain_zero, enc_shift_zero = norm_back(
        x_source, enc_gain[0], enc_shift[0], d_normed
    )
    source_grad = d_hidden + d_input
    norms = jnp.stack(
        [
            enc_gain_zero,
            enc_gain_one,
            enc_gain_two,
            enc_shift_zero,
            enc_shift_one,
            enc_shift_two,
            dec_gain_zero,
            dec_gain_one,
            dec_gain_two,
            dec_gain_three,
            dec_shift_zero,
            dec_shift_one,
            dec_shift_two,
            dec_shift_three,
        ]
    )
    part = width // lay.seq
    norms = lax.dynamic_slice_in_dim(
        lax.psum(norms, ("dp", "seq", "tensor")), lay.half * part, part, 1
    )
    return (
        lay.from_slots(decoded.astype(BF16)),
        lay.from_slots(source_grad.astype(BF16)).astype(F32),
        lay.from_slots(target_grad.astype(BF16)).astype(F32),
        norms[0:3],
        norms[3:6],
        grad_enc_qkv,
        grad_enc_proj,
        grad_enc_up,
        grad_enc_down,
        norms[6:10],
        norms[10:14],
        grad_self_qkv,
        grad_self_proj,
        grad_cross_q,
        grad_cross_kv,
        grad_cross_proj,
        grad_dec_up,
        grad_dec_down,
    )


def swap_pairs(count, bit):
    return [(i, i ^ bit) for i in range(count)]


def norm_parts(inputs):
    centred = inputs - jnp.mean(inputs, -1, keepdims=True)
    scale = lax.rsqrt(jnp.mean(centred * centred, -1, keepdims=True) + EPS)
    return centred * scale, scale


def norm_pull(hat, scale, gain, cotangent):
    tilted = cotangent * gain
    return scale * (
        tilted
        - jnp.mean(tilted, -1, keepdims=True)
        - hat * jnp.mean(tilted * hat, -1, keepdims=True)
    )


ROW_BLOCK = 256
VMEM = 56 << 20
LIGHT = pl.CostEstimate(flops=1 << 20, bytes_accessed=1 << 16, transcendentals=0)


def row_call(kernel, inputs, vectors, outs, sums, name):
    rows, width = inputs[0].shape
    block = pl.BlockSpec((ROW_BLOCK, width), lambda i: (i, 0))
    whole = pl.BlockSpec((1, width), lambda i: (0, 0))
    return pl.pallas_call(
        kernel,
        grid=(rows // ROW_BLOCK,),
        in_specs=[block] * len(inputs) + [whole] * len(vectors),
        out_specs=[block] * len(outs) + [whole] * sums,
        out_shape=[jax.ShapeDtypeStruct((rows, width), kind) for kind in outs]
        + [jax.ShapeDtypeStruct((1, width), F32)] * sums,
        compiler_params=pltpu.CompilerParams(vmem_limit_bytes=VMEM),
        cost_estimate=LIGHT,
        name=name,
    )(*inputs, *vectors)


def norm_kernel(x_ref, gain_ref, shift_ref, low_ref):
    hat, _ = norm_parts(x_ref[...].astype(F32))
    low_ref[...] = (hat * gain_ref[...] + shift_ref[...]).astype(BF16)


def norm_rows(inputs, gain, shift):
    return row_call(norm_kernel, [inputs], [gain, shift], [BF16], 0, "norm_rows")[0]


def add_norm_kernel(x_ref, own_ref, other_ref, gain_ref, shift_ref, sum_ref, low_ref):
    total = (
        x_ref[...].astype(F32) + own_ref[...].astype(F32) + other_ref[...].astype(F32)
    )
    sum_ref[...] = total
    hat, _ = norm_parts(total)
    low_ref[...] = (hat * gain_ref[...] + shift_ref[...]).astype(BF16)


def add_norm(inputs, own, other, gain, shift):
    return row_call(
        add_norm_kernel, [inputs, own, other], [gain, shift], [F32, BF16], 0, "add_norm"
    )


def add_sums(first, gain_out, shift_out, cotangent, hat):
    @pl.when(first)
    def _():
        gain_out[...] = jnp.zeros_like(gain_out)
        shift_out[...] = jnp.zeros_like(shift_out)

    gain_out[...] += jnp.sum(cotangent * hat, 0, keepdims=True)
    shift_out[...] += jnp.sum(cotangent, 0, keepdims=True)


def last_norm_kernel(
    x_ref, own_ref, other_ref, cot_ref, gain_ref, shift_ref, y_ref, d_ref, low_ref, dg_ref, ds_ref
):
    total = (
        x_ref[...].astype(F32) + own_ref[...].astype(F32) + other_ref[...].astype(F32)
    )
    hat, scale = norm_parts(total)
    y_ref[...] = (hat * gain_ref[...] + shift_ref[...]).astype(BF16)
    cotangent = cot_ref[...].astype(F32)
    d_total = norm_pull(hat, scale, gain_ref[...], cotangent)
    d_ref[...] = d_total
    low_ref[...] = d_total.astype(BF16)
    add_sums(pl.program_id(0) == 0, dg_ref, ds_ref, cotangent, hat)


def last_norm(inputs, own, other, cotangent, gain, shift):
    return row_call(
        last_norm_kernel,
        [inputs, own, other, cotangent],
        [gain, shift],
        [BF16, F32, BF16],
        2,
        "last_norm",
    )


def norm_back_kernel(residual, low, *refs):
    x_ref, own_ref, other_ref = refs[:3]
    refs = refs[3:]
    if residual:
        res_ref, refs = refs[0], refs[1:]
    gain_ref, refs = refs[0], refs[1:]
    hat, scale = norm_parts(x_ref[...].astype(F32))
    cotangent = own_ref[...].astype(F32) + other_ref[...].astype(F32)
    d_total = norm_pull(hat, scale, gain_ref[...], cotangent)
    if residual:
        d_total = d_total + res_ref[...]
    refs[0][...] = d_total.astype(refs[0].dtype)
    if low:
        refs[1][...] = d_total.astype(BF16)
    add_sums(pl.program_id(0) == 0, refs[-2], refs[-1], cotangent, hat)


def norm_back_rows(inputs, own, other, gain, residual, kinds):
    return row_call(
        functools.partial(norm_back_kernel, residual is not None, len(kinds) > 1),
        [inputs, own, other] + ([] if residual is None else [residual]),
        [gain],
        kinds,
        2,
        "norm_back",
    )


def chip_attend_kernel(causal, q_ref, k_ref, v_ref, qa_ref, ka_ref, o_ref, lse_ref):
    rows = q_ref.shape[0]
    block = 256
    low_half = lax.broadcasted_iota(jnp.int32, (1, LANES), 1) < HEAD_DIM
    for start in range(0, rows, block):
        keys = start + block if causal else k_ref.shape[0]
        query = q_ref[pl.ds(start, block), :] * BF16(SCALE)
        query_mark = qa_ref[pl.ds(start, block), :]
        key_block = k_ref[:keys, :]
        key_mark = ka_ref[:keys, :]
        values = v_ref[:keys, :]
        halves = []
        lses = []
        for head in range(2):
            keep = low_half if head == 0 else jnp.logical_not(low_half)
            scores = mxu(
                jnp.where(keep, query, query_mark), jnp.where(keep, key_block, key_mark), NT
            )
            if causal:
                scores = jnp.where(
                    lax.broadcasted_iota(jnp.int32, (block, keys), 1)
                    <= start + lax.broadcasted_iota(jnp.int32, (block, keys), 0),
                    scores,
                    NEG,
                )
            top = jnp.max(scores, -1, keepdims=True)
            weights = jnp.exp(scores - top)
            total = jnp.sum(weights, -1, keepdims=True)
            mixed = mxu(weights.astype(BF16), values, NN)
            halves.append(mixed / total)
            lses.append(top + jnp.log(total))
        o_ref[pl.ds(start, block), :] = jnp.where(low_half, halves[0], halves[1]).astype(BF16)
        turned = jnp.where(low_half, lses[0], lses[1]).T
        lse_ref[0, 0:1, pl.ds(start, block)] = turned[0:1]
        lse_ref[0, 1:2, pl.ds(start, block)] = turned[HEAD_DIM : HEAD_DIM + 1]


def pair_spec(rows, stride, offset):
    return pl.BlockSpec((rows, LANES), lambda p: (0, stride * p + offset))


def chip_attend(queries, q_at, pairs, k_at, v_at, query_mark, key_mark, causal):
    rows = queries.shape[0]
    keys = pairs.shape[0]
    count = queries.shape[1] // LANES // q_at[0]
    return pl.pallas_call(
        functools.partial(chip_attend_kernel, causal),
        grid=(count,),
        in_specs=[
            pair_spec(rows, *q_at),
            pair_spec(keys, *k_at),
            pair_spec(keys, *v_at),
            pl.BlockSpec((rows, LANES), lambda p: (0, 0)),
            pl.BlockSpec((keys, LANES), lambda p: (0, 0)),
        ],
        out_specs=[
            pair_spec(rows, 1, 0),
            pl.BlockSpec((1, 2, rows), lambda p: (p, 0, 0)),
        ],
        out_shape=[
            jax.ShapeDtypeStruct((rows, count * LANES), BF16),
            jax.ShapeDtypeStruct((count, 2, rows), F32),
        ],
        compiler_params=pltpu.CompilerParams(vmem_limit_bytes=VMEM),
        cost_estimate=LIGHT,
        name="attend",
    )(queries, pairs, pairs, query_mark, key_mark)


def chip_attend_back_kernel(causal, fused, *refs):
    q_ref, k_ref, v_ref, qa_ref, ka_ref, lse_ref, o_ref, do_ref = refs[:8]
    outs, (dk_acc, dv_acc) = refs[8:-2], refs[-2:]
    rows = q_ref.shape[0]
    block = 256
    low_half = lax.broadcasted_iota(jnp.int32, (1, LANES), 1) < HEAD_DIM
    zero = jnp.zeros((), BF16)
    dk_acc[...] = jnp.zeros_like(dk_acc)
    dv_acc[...] = jnp.zeros_like(dv_acc)
    for start in range(0, rows, block):
        keys = start + block if causal else k_ref.shape[0]
        span = pl.ds(start, block)
        query = q_ref[span, :] * BF16(SCALE)
        query_mark = qa_ref[span, :]
        key_block = k_ref[:keys, :]
        key_mark = ka_ref[:keys, :]
        values = v_ref[:keys, :]
        d_out = do_ref[span, :]
        inner = (d_out.astype(F32) * o_ref[span, :].astype(F32)).T
        d_query = None
        for head in range(2):
            keep = low_half if head == 0 else jnp.logical_not(low_half)
            delta = jnp.sum(
                inner[head * HEAD_DIM : (head + 1) * HEAD_DIM], axis=0, keepdims=True
            )
            scores = mxu(
                jnp.where(keep, key_block, key_mark), jnp.where(keep, query, query_mark), NT
            )
            if causal:
                scores = jnp.where(
                    lax.broadcasted_iota(jnp.int32, (keys, block), 0)
                    <= start + lax.broadcasted_iota(jnp.int32, (keys, block), 1),
                    scores,
                    NEG,
                )
            probs = jnp.exp(scores - lse_ref[0, head : head + 1, span])
            own_out = jnp.where(keep, d_out, zero)
            d_probs = mxu(values, own_out, NT)
            d_scores = (probs * (d_probs - delta)).astype(BF16)
            dv_acc[:keys, :] += mxu(probs.astype(BF16), own_out, NN)
            dk_acc[:keys, :] += mxu(d_scores, jnp.where(keep, query, zero), NN)
            term = mxu(jnp.where(keep, key_block, zero), d_scores, TN)
            d_query = term if d_query is None else d_query + term
        outs[0][span, :LANES] = (d_query * SCALE).T.astype(BF16)
    if fused:
        outs[0][:, LANES : 2 * LANES] = dk_acc[...].astype(BF16)
        outs[0][:, 2 * LANES :] = dv_acc[...].astype(BF16)
    else:
        outs[1][:, :LANES] = dk_acc[...].astype(BF16)
        outs[1][:, LANES:] = dv_acc[...].astype(BF16)


def chip_attend_back(
    queries, q_at, pairs, k_at, v_at, query_mark, key_mark, causal, log_total, mixed, d_mixed, fused
):
    rows = queries.shape[0]
    keys = pairs.shape[0]
    count = mixed.shape[1] // LANES

    def out(rows, blocks):
        return (
            pl.BlockSpec((rows, blocks * LANES), lambda p: (0, p)),
            jax.ShapeDtypeStruct((rows, count * blocks * LANES), BF16),
        )

    outs = [out(rows, 3)] if fused else [out(rows, 1), out(keys, 2)]
    return pl.pallas_call(
        functools.partial(chip_attend_back_kernel, causal, fused),
        grid=(count,),
        in_specs=[
            pair_spec(rows, *q_at),
            pair_spec(keys, *k_at),
            pair_spec(keys, *v_at),
            pl.BlockSpec((rows, LANES), lambda p: (0, 0)),
            pl.BlockSpec((keys, LANES), lambda p: (0, 0)),
            pl.BlockSpec((1, 2, rows), lambda p: (p, 0, 0)),
            pair_spec(rows, 1, 0),
            pair_spec(rows, 1, 0),
        ],
        out_specs=[spec for spec, _ in outs],
        out_shape=[shape for _, shape in outs],
        scratch_shapes=[pltpu.VMEM((keys, LANES), F32), pltpu.VMEM((keys, LANES), F32)],
        compiler_params=pltpu.CompilerParams(vmem_limit_bytes=VMEM),
        cost_estimate=LIGHT,
        name="attend_back",
    )(queries, pairs, pairs, query_mark, key_mark, log_total, mixed, d_mixed)


def piece_kernel(kind, low, high, count, x_ref, *refs):
    if count == 1:
        order_ref, stack_ref, rest = refs[0], refs[1], refs[2:]
        weights = [stack_ref.at[order_ref[i]] for i in range(stack_ref.shape[0])]
    else:
        weights, rest = refs[:count], refs[count:]
    own = high - low
    total = None
    for i, ref in enumerate(weights):
        span = pl.ds(i * own, own)
        if kind == "columns":
            rest[-1][:, span] = mxu(x_ref[...], ref[:, low:high], NN).astype(BF16)
        elif kind == "gelu":
            inner = mxu(x_ref[...], ref[:, low:high], NN)
            below = 0.5 + 0.5 * lax.erf(inner * (0.5**0.5))
            rest[0][:, span] = (inner * below).astype(BF16)
            bell = jnp.exp(inner * inner * (-0.5)) * (0.5 / jnp.pi) ** 0.5
            rest[1][:, span] = (below + inner * bell).astype(BF16)
        elif kind == "rows":
            term = mxu(x_ref[:, span], ref[low:high, :], NN)
            total = term if total is None else total + term
        elif kind == "columns_back":
            term = mxu(x_ref[:, span], ref[:, low:high], NT)
            total = term if total is None else total + term
        elif kind == "rows_back":
            rest[-1][:, span] = mxu(x_ref[...], ref[low:high, :], NT).astype(BF16)
        elif kind == "rows_back_slope":
            term = mxu(x_ref[...], ref[low:high, :], NT)
            rest[-1][:, span] = (term * rest[0][:, span].astype(F32)).astype(BF16)
    if total is not None:
        rest[-1][...] = total.astype(BF16)


def piece_product(kind, rows_in, pieces, low, high, slope=None, block=512):
    rows, depth = rows_in.shape
    stacked = len(pieces) == 2
    shape = pieces[1].shape[1:] if stacked else pieces[0].shape
    all_own = 4 * (high - low)
    width = {
        "columns": all_own,
        "gelu": all_own,
        "rows": shape[1],
        "columns_back": shape[0],
        "rows_back": all_own,
        "rows_back_slope": all_own,
    }[kind]
    outs = 2 if kind == "gelu" else 1
    out = pl.BlockSpec((block, width), lambda i: (i, 0))
    results = pl.pallas_call(
        functools.partial(piece_kernel, kind, low, high, 1 if stacked else len(pieces)),
        grid=(rows // block,),
        in_specs=[pl.BlockSpec((block, depth), lambda i: (i, 0))]
        + (
            [
                pl.BlockSpec(memory_space=pltpu.SMEM),
                pl.BlockSpec(pieces[1].shape, lambda i: (0, 0, 0)),
            ]
            if stacked
            else [pl.BlockSpec(piece.shape, lambda i: (0, 0)) for piece in pieces]
        )
        + ([] if slope is None else [out]),
        out_specs=[out] * outs,
        out_shape=[jax.ShapeDtypeStruct((rows, width), BF16)] * outs,
        compiler_params=pltpu.CompilerParams(vmem_limit_bytes=VMEM),
        cost_estimate=LIGHT,
        name="product_" + kind,
    )(rows_in, *pieces, *([] if slope is None else [slope]))
    return results if outs > 1 else results[0]


def weight_kernel(count, *refs):
    out_ref = refs[-1]
    at = 0
    for i in range(count):
        own = refs[i].shape[1]
        out_ref[pl.ds(at, own), :] = mxu(refs[i][...], refs[count + i][...], TN).astype(BF16)
        at += own


def weight_grads(pairs, part):
    rows, width = pairs[0][1].shape
    owns = [hidden.shape[1] // 4 for hidden, _ in pairs]
    return pl.pallas_call(
        functools.partial(weight_kernel, len(pairs)),
        grid=(2,),
        in_specs=[
            pl.BlockSpec((rows, own), lambda i: (0, 2 * part + i)) for own in owns
        ]
        + [pl.BlockSpec((rows, width), lambda i: (0, 0)) for _ in pairs],
        out_specs=pl.BlockSpec((sum(owns), width), lambda i: (i, 0)),
        out_shape=jax.ShapeDtypeStruct((2 * sum(owns), width), BF16),
        compiler_params=pltpu.CompilerParams(vmem_limit_bytes=VMEM),
        cost_estimate=LIGHT,
        name="weight_grads",
    )(*[hidden for hidden, _ in pairs], *[wide for _, wide in pairs])


CROSS = ("seq", "tensor")


class Chip:
    def __init__(self):
        self.core = lax.axis_index("seq")
        self.place = lax.axis_index("tensor")
        self.line = lax.axis_index("dp")
        self.first = [(i, i ^ 1) for i in range(4)] + [(4 + i, 4 + (i ^ 2)) for i in range(4)]
        self.second = [(i, i ^ 2) for i in range(4)] + [(4 + i, 4 + (i ^ 1)) for i in range(4)]

    def other(self, block):
        return lax.ppermute(block, "seq", swap_pairs(2, 1))

    def gather(self, block):
        near = lax.ppermute(block, CROSS, self.first)
        side = lax.ppermute(block, CROSS, self.second)
        far = lax.ppermute(side, CROSS, self.first)
        return [block, side, near, far]

    def ordered(self, own, other, index):
        first = index == 0
        return jnp.concatenate([jnp.where(first, own, other), jnp.where(first, other, own)], 0)

    def swap_start(self, blocks):
        near_bit = 1 + self.core

        def to(bits):
            return lax.dynamic_index_in_dim(blocks, jnp.bitwise_xor(self.place, bits), 0)

        cuts = lax.optimization_barrier((to(0), to(near_bit), to(3 - near_bit), to(3)))
        far = lax.ppermute(cuts[3], "tensor", swap_pairs(4, 3))
        return cuts[0], self.send_near(cuts[1]), self.send_side(cuts[2]), far

    def swap_end(self, parts):
        own, near, side, far = parts
        low, high = lax.rem(self.place, 2), self.place // 2
        first = self.core == 0
        beside, across = jnp.where(first, near, side), jnp.where(first, side, near)
        blocks = self.ordered(self.ordered(own, beside, low), self.ordered(across, far, low), high)
        return blocks.reshape(-1, own.shape[2]) if own.ndim == 3 else blocks

    def swap_rows(self, block):
        return self.swap_end(self.swap_start(block))

    def both_cores(self, rows):
        return self.ordered(rows, self.other(rows), self.core)

    def from_start(self, rows):
        half = rows.shape[0] // 2
        own = lax.dynamic_slice_in_dim(rows, self.core * half, half, 0)
        return self.swap_start(own.reshape(4, half // 4, -1))

    def from_end(self, parts):
        return self.swap_end(parts).reshape((4,) + parts[0].shape[1:])

    def from_slot(self, rows):
        return self.from_end(self.from_start(rows))

    def send_near(self, block):
        return lax.ppermute(block, CROSS, self.first)

    def send_side(self, block):
        return lax.ppermute(block, CROSS, self.second)

    def along(self, block, bit):
        return lax.ppermute(block, "dp", swap_pairs(4, bit))


def add_low(left, right):
    return (left.astype(F32) + right.astype(F32)).astype(BF16)


def chip_local(
    source,
    target,
    out_grad,
    source_segments,
    target_segments,
    enc_gain,
    enc_shift,
    enc_qkv,
    enc_proj,
    enc_up,
    enc_down,
    dec_gain,
    dec_shift,
    dec_self_qkv,
    dec_self_proj,
    dec_cross_q,
    dec_cross_kv,
    dec_cross_proj,
    dec_up,
    dec_down,
):
    chip = Chip()
    core = chip.core
    tie = lax.optimization_barrier

    def own_columns(weight):
        part = weight.shape[-1] // 2
        cut = lax.dynamic_slice_in_dim(weight, core * part, part, weight.ndim - 1)
        return cut.reshape(weight.shape[0], -1)

    def own_rows(weight):
        part = weight.shape[0] // 2
        return lax.dynamic_slice_in_dim(weight, core * part, part, 0)

    def pin(value, *others):
        return tie((value,) + others)[0]

    bundles = [
        own_columns(enc_qkv),
        own_columns(dec_self_qkv),
        jnp.concatenate([own_rows(enc_proj), own_rows(dec_self_proj), own_rows(dec_cross_proj)], 0),
        jnp.concatenate([own_columns(dec_cross_q), own_columns(dec_cross_kv)], 1),
        own_rows(dec_down),
    ]
    near_bit = 1 + core
    order = jnp.bitwise_xor(
        chip.place, jnp.stack([0 * core, 3 - near_bit, near_bit, 0 * core + 3])
    ).astype(jnp.int32)

    def all_groups(own):
        return [order, lax.all_gather(own, "tensor", axis=0)]

    inner = enc_up.shape[1] // 2
    pieces = [None] * len(bundles)

    def launch(index, *after):
        own = pin(bundles[index], *after)
        pieces[index] = [own, chip.send_side(own), chip.send_near(own)]
        return pieces[index][1]

    def relay(index, value):
        side, near, value = tie((pieces[index][1], pieces[index][2], value))
        pieces[index][1:] = [side, near]
        pieces[index].append(chip.send_near(side))
        return value

    def arrived(index, value):
        tied = tie(tuple(pieces[index]) + (value,))
        pieces[index] = list(tied[:-1])
        return tied[-1]

    def enc(index):
        return enc_gain[index : index + 1], enc_shift[index : index + 1]

    def dec(index):
        return dec_gain[index : index + 1], dec_shift[index : index + 1]

    def part_rows(rows_in, weight, low, high):
        own = piece_product("rows", rows_in, weight, low, high)
        return own, chip.other(own)

    def part_back(grad, weight, low, high):
        own = piece_product("columns_back", grad, weight, low, high)
        return own, chip.other(own)

    fused_at = ((3, 0), (3, 1), (3, 2))

    def attend_self(qkv, marks, causal):
        return chip_attend(
            qkv, fused_at[0], qkv, fused_at[1], fused_at[2], marks[0], marks[1], causal
        )

    launch(0)
    swapped = arrived(0, chip.swap_rows(relay(0, source)))
    launch(1, swapped)
    x_source = chip.both_cores(swapped)
    sent_target = chip.swap_start(pin(target, swapped))
    w_enc_up = all_groups(pin(own_columns(enc_up), swapped))
    source_ids = lax.dynamic_index_in_dim(source_segments, chip.place, 0, keepdims=False)
    target_ids = lax.dynamic_index_in_dim(target_segments, chip.place, 0, keepdims=False)
    ids = jnp.arange(LANES, dtype=jnp.int32)[None] % HEAD_DIM
    counted = ids < IDS
    source_query = jnp.where(source_ids[:, None] == ids, NEG, 0.0).astype(BF16)
    target_query = jnp.where(target_ids[:, None] == ids, NEG, 0.0).astype(BF16)
    source_key = ((source_ids[:, None] != ids) & counted).astype(BF16)
    target_key = ((target_ids[:, None] != ids) & counted).astype(BF16)
    rows_a = norm_rows(x_source, *enc(0))
    rows_a = pin(rows_a, source_query, source_key)
    qkv_a = piece_product("columns", rows_a, pieces[0], 0, bundles[0].shape[1])
    launch(2, qkv_a)
    mixed_a, total_a = attend_self(qkv_a, (source_query, source_key), False)
    mixed_a, sent_target = tie((relay(1, mixed_a), sent_target))
    x_target = chip.both_cores(chip.swap_end(sent_target))
    w_enc_down = all_groups(pin(own_rows(enc_down), mixed_a))
    rows_c = norm_rows(pin(x_target, target_query, target_key), *dec(0))
    rows_c = arrived(1, rows_c)
    qkv_c = piece_product("columns", rows_c, pieces[1], 0, bundles[1].shape[1])
    qkv_c = relay(2, qkv_c)
    w_dec_up = all_groups(pin(own_columns(dec_up), qkv_c))
    mixed_c, total_c = attend_self(qkv_c, (target_query, target_key), True)
    proj_rows = bundles[2].shape[0] // 3
    mixed_c, mixed_a = tie((arrived(2, mixed_c), mixed_a))
    launch(3, mixed_c)
    own_a, other_a = part_rows(mixed_a, pieces[2], 0, proj_rows)
    own_c, other_c = part_rows(mixed_c, pieces[2], proj_rows, 2 * proj_rows)
    other_a, other_c = tie((other_a, other_c, own_a, own_c))[:2]
    hidden, rows_b = add_norm(x_source, own_a, other_a, *enc(1))
    after_self, rows_e = add_norm(x_target, own_c, other_c, *dec(1))
    rows_b = pin(rows_b, rows_e)
    active_b, slope_b = piece_product("gelu", rows_b, w_enc_up, 0, inner, block=256)
    active_b = relay(3, active_b)
    encoded, rows_m = add_norm(hidden, *part_rows(active_b, w_enc_down, 0, inner), *enc(2))
    rows_m, rows_e = tie((arrived(3, rows_m), rows_e))
    launch(4, rows_m)
    head_width = dec_cross_q.shape[1] // 2
    pairs_m = piece_product("columns", rows_m, pieces[3], head_width, 3 * head_width)
    query_e = piece_product("columns", rows_e, pieces[3], 0, head_width)
    query_e = pin(query_e, pairs_m)
    mixed_e, total_e = chip_attend(
        query_e, (1, 0), pairs_m, (2, 0), (2, 1), target_query, source_key, False
    )
    mixed_e = relay(4, mixed_e)
    after_cross, rows_f = add_norm(
        after_self, *part_rows(mixed_e, pieces[2], 2 * proj_rows, 3 * proj_rows), *dec(2)
    )
    sent_grad = chip.swap_start(pin(out_grad, rows_f))
    active_f, slope_f = piece_product("gelu", rows_f, w_dec_up, 0, inner, block=256)
    active_f, sent_grad = tie((arrived(4, active_f), sent_grad))
    cotangent = chip.both_cores(chip.swap_end(sent_grad))
    w_dec_down = pieces[4]
    decoded, d_final, low_final, gain_d3, shift_d3 = last_norm(
        after_cross, *part_rows(active_f, w_dec_down, 0, inner), cotangent, *dec(3)
    )


    low_bit = lax.rem(chip.line, 2)
    high_bit = chip.line // 2

    def here(value, step, *args):
        args, value = tie((args, value))
        *result, sent = step(*args)
        return pin(value, result[1], *sent), result

    def to_side(came, kept):
        half = kept.shape[0] // 2
        sent = add_low(kept[half:], came[half:])
        return chip.send_side(sent), add_low(kept[:half], came[:half]), [sent]

    def to_line(*states):
        def cut(bits):
            parts = []
            for came, kept in states:
                quarter = kept.shape[0] // 4
                at = jnp.bitwise_xor(chip.line, bits) * quarter
                parts.append(
                    add_low(
                        lax.dynamic_slice_in_dim(kept, at, quarter, 0),
                        lax.dynamic_slice_in_dim(came, at, quarter, 0),
                    )
                )
            return jnp.concatenate(parts, 0)

        sent = [cut(bits) for bits in (3, 2, 1)]
        return [chip.along(part, bits) for part, bits in zip(sent, (3, 2, 1))], cut(0), sent

    def from_line(came, own):
        total = own.astype(F32)
        for block in came:
            total = total + block.astype(F32)
        own = total.astype(BF16)
        return [chip.along(own, bits) for bits in (3, 2, 1)], own, []

    def to_core(came, own):
        far, next_but_one, next_one = came
        first = chip.ordered(own, next_one, low_bit)
        second = chip.ordered(next_but_one, far, low_bit)
        return share(chip.ordered(first, second, high_bit))

    def share(whole):
        width = whole.shape[1] // 2
        sent = lax.dynamic_slice_in_dim(whole, (1 - core) * width, width, 1)
        own = lax.dynamic_slice_in_dim(whole, core * width, width, 1)
        return chip.other(sent), own

    def in_place(came, own):
        return chip.ordered(own[None], came[None], core)

    def sum_line(*states):
        total = jnp.concatenate([add_low(*state) for state in states], 0)
        return None, total, []

    def send_half(value, *pairs):
        sent = weight_grads(list(pairs), 1)
        return pin(value, sent), chip.send_near(sent)

    def keep_half(value, came, *pairs):
        first, value = tie((pairs[0], value))
        kept = weight_grads([first] + list(pairs[1:]), 0)
        return pin(value, kept), (came, kept)

    def ffn_back(low_out, slope, weight):
        return piece_product("rows_back_slope", low_out, weight, 0, inner, slope)

    low_send, near_fd = send_half(low_final, (active_f, low_final))
    d_inner_f = ffn_back(low_send, slope_f, w_dec_down)
    d_inner_f, near_fu = send_half(d_inner_f, (d_inner_f, rows_f))
    own = piece_product("columns_back", d_inner_f, w_dec_up, 0, inner)
    own, near_fd = tie((own, near_fd))
    other = chip.other(own)
    hold, keep_fd = keep_half(own, near_fd, (active_f, low_final))
    hold, side_fd = here(hold, to_side, *keep_fd)
    hold, keep_fu = keep_half(hold, near_fu, (d_inner_f, rows_f))
    d_cross, low_cross, gain_d2, shift_d2 = norm_back_rows(
        after_cross, own, pin(other, hold), dec(2)[0], d_final, [F32, BF16]
    )
    d_mixed = piece_product("rows_back", low_cross, pieces[2], 2 * proj_rows, 3 * proj_rows)
    d_mixed, side_fu = here(d_mixed, to_side, *keep_fu)
    d_query_e, d_pairs_m = chip_attend_back(
        query_e,
        (1, 0),
        pairs_m,
        (2, 0),
        (2, 1),
        target_query,
        source_key,
        False,
        total_e,
        mixed_e,
        d_mixed,
        False,
    )
    d_pairs_m, (_, total_f) = here(d_pairs_m, sum_line, side_fd, side_fu)
    sum_f = lax.psum(total_f, "dp")
    own_m, other_m = part_back(d_pairs_m, pieces[3], head_width, 3 * head_width)
    own_e, other_e = part_back(pin(d_query_e, own_m), pieces[3], 0, head_width)
    d_encoded, low_encoded, gain_e2, shift_e2 = norm_back_rows(
        encoded, own_m, pin(other_m, own_e), enc(2)[0], None, [F32, BF16]
    )
    low_send, near_bd = send_half(low_encoded, (active_b, low_encoded))
    d_inner_b = ffn_back(low_send, slope_b, w_enc_down)
    d_inner_b, near_bu = send_half(d_inner_b, (d_inner_b, rows_b))
    own = piece_product("columns_back", d_inner_b, w_enc_up, 0, inner)
    own, near_bd, other_e = tie((own, near_bd, other_e))
    other = chip.other(own)
    hold, keep_bd = keep_half(own, near_bd, (active_b, low_encoded))
    hold, side_bd = here(hold, to_side, *keep_bd)
    hold, keep_bu = keep_half(hold, near_bu, (d_inner_b, rows_b))
    d_hidden, low_hidden, gain_e1, shift_e1 = norm_back_rows(
        hidden, own, pin(other, hold), enc(1)[0], d_encoded, [F32, BF16]
    )
    pairs_x = ((mixed_e, low_cross), (d_query_e, rows_e), (d_pairs_m, rows_m))
    own_e, side_bu = here(pin(own_e, low_hidden), to_side, *keep_bu)
    pairs_x = tie((pairs_x, own_e))[0]
    own_e, near_x = send_half(own_e, *pairs_x)
    own_e, keep_x = keep_half(own_e, near_x, *pairs_x)
    d_self, low_self, gain_d1, shift_d1 = norm_back_rows(
        after_self, own_e, other_e, dec(1)[0], d_cross, [F32, BF16]
    )

    def self_back(d_mixed, qkv, marks, causal, totals, mixed):
        (d_qkv,) = chip_attend_back(
            qkv,
            fused_at[0],
            qkv,
            fused_at[1],
            fused_at[2],
            marks[0],
            marks[1],
            causal,
            totals,
            mixed,
            d_mixed,
            True,
        )
        return d_qkv

    d_mixed = piece_product("rows_back", low_self, pieces[2], proj_rows, 2 * proj_rows)
    d_mixed, (_, total_b) = here(d_mixed, sum_line, side_bd, side_bu)
    d_qkv_c = self_back(d_mixed, qkv_c, (target_query, target_key), True, total_c, mixed_c)
    d_qkv_c, sum_f, total_b = tie((d_qkv_c, sum_f, total_b))
    sum_b = lax.psum(total_b, "dp")
    d_qkv_c, side_x = here(d_qkv_c, to_side, *keep_x)
    pairs_c = ((mixed_c, low_self), (d_qkv_c, rows_c))
    d_qkv_c, near_c = send_half(d_qkv_c, *pairs_c)
    own_c = piece_product("columns_back", d_qkv_c, pieces[1], 0, 3 * head_width)
    own_c, keep_c = keep_half(own_c, near_c, *pairs_c)
    low_hidden, decoded = tie((low_hidden, decoded, own_c))[:2]
    sent_decoded = chip.from_start(decoded)
    d_mixed = piece_product("rows_back", low_hidden, pieces[2], 0, proj_rows)
    d_qkv_a = self_back(d_mixed, qkv_a, (source_query, source_key), False, total_a, mixed_a)
    pairs_a = ((mixed_a, low_hidden), (d_qkv_a, rows_a))
    d_qkv_a, near_a = send_half(d_qkv_a, *pairs_a)
    d_qkv_a, side_c = here(d_qkv_a, to_side, *keep_c)
    own_a = piece_product("columns_back", d_qkv_a, pieces[0], 0, 3 * head_width)
    own_a, (_, total_xc) = here(own_a, sum_line, side_x, side_c)
    own_a, sum_b, total_xc, sent_decoded, near_a = tie(
        (own_a, sum_b, total_xc, sent_decoded, near_a)
    )
    decoded = chip.from_end(sent_decoded)
    sum_xc = lax.psum(total_xc, "dp")
    other_a, other_c = chip.other(own_a), chip.other(pin(own_c, own_a))
    own_a, keep_a = keep_half(own_a, near_a, *pairs_a)
    own_a, side_a = here(own_a, to_side, *keep_a)
    source_grad, gain_e0, shift_e0 = norm_back_rows(
        x_source, own_a, other_a, enc(0)[0], d_hidden, [BF16]
    )
    own_c = pin(own_c, source_grad)
    target_grad, gain_d0, shift_d0 = norm_back_rows(
        x_target, own_c, other_c, dec(0)[0], d_self, [BF16]
    )
    gain_d0, line_a = here(gain_d0, to_line, side_a)
    source_grad = chip.from_slot(pin(source_grad, gain_d0))
    sent_grad = chip.from_start(pin(target_grad, gain_d0))
    sent_grad, sum_xc = tie((sent_grad, sum_xc))
    target_grad = chip.from_end(sent_grad)

    norms = jnp.concatenate(
        [
            gain_e0,
            gain_e1,
            gain_e2,
            shift_e0,
            shift_e1,
            shift_e2,
            gain_d0,
            gain_d1,
            gain_d2,
            gain_d3,
            shift_d0,
            shift_d1,
            shift_d2,
            shift_d3,
        ],
        0,
    )
    part = norms.shape[1] // 2
    norms = lax.dynamic_slice_in_dim(norms, core * part, part, 1)
    norms = norms + chip.send_near(norms)
    norms = norms + chip.send_side(norms)
    norms = norms + chip.along(norms, 1)
    norms = norms + chip.along(norms, 2)
    line_a = from_line(*line_a)[:2]
    line_a = to_core(*line_a)

    def wide(block, blocks):
        cores, rows, width = block.shape
        block = block.reshape(cores, blocks, rows // blocks, width)
        return jnp.transpose(block, (3, 1, 0, 2)).reshape(width, blocks, -1).astype(F32)

    def tall(block):
        return block.reshape(-1, block.shape[2]).astype(F32)

    n = proj_rows
    done_f, done_b = in_place(*share(sum_f)), in_place(*share(sum_b))
    done_xc, done_a = in_place(*share(sum_xc)), in_place(*line_a)
    done_x, done_c = done_xc[:, : 4 * n], done_xc[:, 4 * n :]
    source_grad, target_grad = source_grad.astype(F32), target_grad.astype(F32)
    hid = done_f.shape[1] // 2
    return (
        decoded,
        source_grad,
        target_grad,
        norms[0:3],
        norms[3:6],
        wide(done_a[:, n:], 3),
        tall(done_a[:, :n]),
        wide(done_b[:, inner:], 1)[:, 0],
        tall(done_b[:, :inner]),
        norms[6:10],
        norms[10:14],
        wide(done_c[:, n:], 3),
        tall(done_c[:, :n]),
        wide(done_x[:, n : n + head_width], 1)[:, 0],
        wide(done_x[:, n + head_width :], 2),
        tall(done_x[:, :n]),
        wide(done_f[:, hid:], 1)[:, 0],
        tall(done_f[:, :hid]),
    )


def solution(mesh):
    rows = P("dp", ("seq", "tensor"), None)
    segments = P("dp", None)
    shape = dict(mesh.shape)
    chips = shape["dp"] == 4 and shape["seq"] == 2 and shape["tensor"] == 4
    return jax.shard_map(
        chip_local if chips else local,
        mesh=mesh,
        in_specs=(
            rows,
            rows,
            rows,
            segments,
            segments,
            P(),
            P(),
            P(None, None, "tensor"),
            P("tensor", None),
            P(None, "tensor"),
            P("tensor", None),
            P(),
            P(),
            P(None, None, "tensor"),
            P("tensor", None),
            P(None, "tensor"),
            P(None, None, "tensor"),
            P("tensor", None),
            P(None, "tensor"),
            P("tensor", None),
        ),
        out_specs=(
            rows,
            rows,
            rows,
            P(None, "seq"),
            P(None, "seq"),
            P("seq", None, "tensor"),
            P("tensor", "seq"),
            P("seq", "tensor"),
            P("tensor", "seq"),
            P(None, "seq"),
            P(None, "seq"),
            P("seq", None, "tensor"),
            P("tensor", "seq"),
            P("seq", "tensor"),
            P("seq", None, "tensor"),
            P("tensor", "seq"),
            P("seq", "tensor"),
            P("tensor", "seq"),
        ),
        check_vma=False,
    )
```

```python
import functools

import jax
import jax.numpy as jnp
from jax import lax
from jax.experimental import pallas as pl
from jax.experimental.pallas import tpu as pltpu
from jax.sharding import PartitionSpec as P

HEAD_DIM = 64
LANES = 128
IDS = 9
EPS = 1e-05
NEG = -1e30
SCALE = HEAD_DIM ** (-0.5)
F32 = jnp.float32
BF16 = jnp.bfloat16
NT = (((1,), (1,)), ((), ()))
NN = (((1,), (0,)), ((), ()))
TN = (((0,), (0,)), ((), ()))


def mxu(left, right, dims):
    return lax.dot_general(left, right, dims, preferred_element_type=F32)


def layer_norm(inputs, norm_gain, norm_shift):
    row_mean = jnp.mean(inputs, -1, keepdims=True)
    centred = inputs - row_mean
    spread = jnp.mean(centred * centred, -1, keepdims=True)
    return centred * lax.rsqrt(spread + EPS) * norm_gain + norm_shift


def exact_gelu(inputs):
    return jax.nn.gelu(inputs, approximate=False)


def norm_back(inputs, norm_gain, norm_shift, cotangent):
    _, pullback = jax.vjp(layer_norm, inputs, norm_gain, norm_shift)
    return pullback(cotangent)


def project(rows, weight):
    return mxu(rows, weight, NN)


def back_project(grad, weight):
    return mxu(grad, weight, NT)


def weight_grad(rows, grad):
    return mxu(rows, grad, TN).astype(BF16)


def attend_kernel(causal, first_ref, q_ref, k_ref, v_ref, qa_ref, ka_ref, o_ref, lse_ref):
    rows = q_ref.shape[0]
    keys = k_ref.shape[0]
    block = min(rows, 256)
    low_half = lax.broadcasted_iota(jnp.int32, (1, LANES), 1) < HEAD_DIM
    key_block = k_ref[...]
    key_mark = ka_ref[...]
    values = v_ref[...]
    for start in range(0, rows, block):
        query = q_ref[pl.ds(start, block), :] * BF16(SCALE)
        query_mark = qa_ref[pl.ds(start, block), :]
        halves = []
        lses = []
        for head in range(2):
            keep = low_half if head == 0 else jnp.logical_not(low_half)
            scores = mxu(
                jnp.where(keep, query, query_mark), jnp.where(keep, key_block, key_mark), NT
            )
            if causal:
                place = (
                    first_ref[0] + start + lax.broadcasted_iota(jnp.int32, (block, keys), 0)
                )
                scores = jnp.where(
                    lax.broadcasted_iota(jnp.int32, (block, keys), 1) <= place, scores, NEG
                )
            top = jnp.max(scores, -1, keepdims=True)
            weights = jnp.exp(scores - top)
            total = jnp.sum(weights, -1, keepdims=True)
            mixed = mxu(weights.astype(BF16), values, NN)
            halves.append(mixed / total)
            lses.append(top + jnp.log(total))
        o_ref[pl.ds(start, block), :] = jnp.where(low_half, halves[0], halves[1]).astype(BF16)
        both = jnp.where(low_half, lses[0], lses[1])
        turned = both.T
        lse_ref[0, 0:1, pl.ds(start, block)] = turned[0:1]
        lse_ref[0, 1:2, pl.ds(start, block)] = turned[HEAD_DIM : HEAD_DIM + 1]


def attend(queries, keys, values, query_mark, key_mark, first_row, causal):
    rows, width = queries.shape
    key_rows = keys.shape[0]
    pairs = width // LANES
    return pl.pallas_call(
        functools.partial(attend_kernel, causal),
        grid_spec=pltpu.PrefetchScalarGridSpec(
            num_scalar_prefetch=1,
            grid=(pairs,),
            in_specs=[
                pl.BlockSpec((rows, LANES), lambda p, first: (0, p)),
                pl.BlockSpec((key_rows, LANES), lambda p, first: (0, p)),
                pl.BlockSpec((key_rows, LANES), lambda p, first: (0, p)),
                pl.BlockSpec((rows, LANES), lambda p, first: (0, 0)),
                pl.BlockSpec((key_rows, LANES), lambda p, first: (0, 0)),
            ],
            out_specs=[
                pl.BlockSpec((rows, LANES), lambda p, first: (0, p)),
                pl.BlockSpec((1, 2, rows), lambda p, first: (p, 0, 0)),
            ],
        ),
        out_shape=[
            jax.ShapeDtypeStruct((rows, width), BF16),
            jax.ShapeDtypeStruct((pairs, 2, rows), F32),
        ],
        compiler_params=pltpu.CompilerParams(vmem_limit_bytes=40 << 20),
        cost_estimate=pl.CostEstimate(
            flops=4 * rows * key_rows * width * 2,
            bytes_accessed=4 * rows * width + 4 * key_rows * width,
            transcendentals=rows * key_rows * width // HEAD_DIM,
        ),
        name="attend",
    )(first_row, queries, keys, values, query_mark, key_mark)


def attend_back_kernel(
    causal,
    first_ref,
    q_ref,
    k_ref,
    v_ref,
    qa_ref,
    ka_ref,
    lse_ref,
    o_ref,
    do_ref,
    dq_ref,
    dk_ref,
    dv_ref,
    dk_acc,
    dv_acc,
):
    rows = q_ref.shape[0]
    keys = k_ref.shape[0]
    block = min(rows, 256)
    low_half = lax.broadcasted_iota(jnp.int32, (1, LANES), 1) < HEAD_DIM
    key_block = k_ref[...]
    key_mark = ka_ref[...]
    values = v_ref[...]
    zero = jnp.zeros((), BF16)
    dk_acc[...] = jnp.zeros_like(dk_acc)
    dv_acc[...] = jnp.zeros_like(dv_acc)
    for start in range(0, rows, block):
        span = pl.ds(start, block)
        query = q_ref[span, :] * BF16(SCALE)
        query_mark = qa_ref[span, :]
        d_out = do_ref[span, :]
        inner = (d_out.astype(F32) * o_ref[span, :].astype(F32)).T
        d_query = None
        for head in range(2):
            keep = low_half if head == 0 else jnp.logical_not(low_half)
            delta = jnp.sum(
                inner[head * HEAD_DIM : (head + 1) * HEAD_DIM], axis=0, keepdims=True
            )
            scores = mxu(
                jnp.where(keep, key_block, key_mark), jnp.where(keep, query, query_mark), NT
            )
            if causal:
                place = (
                    first_ref[0] + start + lax.broadcasted_iota(jnp.int32, (keys, block), 1)
                )
                scores = jnp.where(
                    lax.broadcasted_iota(jnp.int32, (keys, block), 0) <= place, scores, NEG
                )
            probs = jnp.exp(scores - lse_ref[0, head : head + 1, span])
            own_out = jnp.where(keep, d_out, zero)
            d_probs = mxu(values, own_out, NT)
            d_scores = (probs * (d_probs - delta)).astype(BF16)
            dv_acc[...] += mxu(probs.astype(BF16), own_out, NN)
            dk_acc[...] += mxu(d_scores, jnp.where(keep, query, zero), NN)
            term = mxu(jnp.where(keep, key_block, zero), d_scores, TN)
            d_query = term if d_query is None else d_query + term
        dq_ref[span, :] = (d_query * SCALE).T.astype(BF16)
    dk_ref[...] = dk_acc[...].astype(BF16)
    dv_ref[...] = dv_acc[...].astype(BF16)


def attend_back(
    queries, keys, values, query_mark, key_mark, first_row, causal, log_total, mixed, d_mixed
):
    rows, width = queries.shape
    key_rows = keys.shape[0]
    pairs = width // LANES
    row_spec = pl.BlockSpec((rows, LANES), lambda p, first: (0, p))
    key_spec = pl.BlockSpec((key_rows, LANES), lambda p, first: (0, p))
    return pl.pallas_call(
        functools.partial(attend_back_kernel, causal),
        grid_spec=pltpu.PrefetchScalarGridSpec(
            num_scalar_prefetch=1,
            grid=(pairs,),
            in_specs=[
                row_spec,
                key_spec,
                key_spec,
                pl.BlockSpec((rows, LANES), lambda p, first: (0, 0)),
                pl.BlockSpec((key_rows, LANES), lambda p, first: (0, 0)),
                pl.BlockSpec((1, 2, rows), lambda p, first: (p, 0, 0)),
                row_spec,
                row_spec,
            ],
            out_specs=[row_spec, key_spec, key_spec],
            scratch_shapes=[
                pltpu.VMEM((key_rows, LANES), F32),
                pltpu.VMEM((key_rows, LANES), F32),
            ],
        ),
        out_shape=[
            jax.ShapeDtypeStruct((rows, width), BF16),
            jax.ShapeDtypeStruct((key_rows, width), BF16),
            jax.ShapeDtypeStruct((key_rows, width), BF16),
        ],
        compiler_params=pltpu.CompilerParams(vmem_limit_bytes=40 << 20),
        cost_estimate=pl.CostEstimate(
            flops=10 * rows * key_rows * width * 2,
            bytes_accessed=8 * rows * width + 8 * key_rows * width,
            transcendentals=rows * key_rows * width // HEAD_DIM,
        ),
        name="attend_back",
    )(first_row, queries, keys, values, query_mark, key_mark, log_total, mixed, d_mixed)


class Layout:
    def __init__(self, slots):
        self.tensor = lax.axis_size("tensor")
        self.seq = lax.axis_size("seq")
        self.slots = slots
        self.spread = self.tensor // slots
        self.place = lax.axis_index("tensor")
        self.half = lax.axis_index("seq")
        self.row_groups = [
            [j * slots + u for u in range(slots)] for j in range(self.spread)
        ]
        self.slot_groups = [
            [j * slots + u for j in range(self.spread)] for u in range(slots)
        ]

    def to_slots(self, block):
        rows = lax.all_to_all(
            block, "tensor", 0, 1, axis_index_groups=self.row_groups, tiled=True
        )
        return rows.reshape(-1, block.shape[2])

    def from_slots(self, rows):
        block = rows.reshape(1, rows.shape[0], rows.shape[1])
        return lax.all_to_all(
            block, "tensor", 1, 0, axis_index_groups=self.row_groups, tiled=True
        )

    def gather_keys(self, rows):
        if self.spread > 1:
            rows = lax.all_gather(
                rows, "tensor", axis=0, axis_index_groups=self.slot_groups, tiled=True
            )
        return lax.all_gather(rows, "seq", axis=0, tiled=True)

    def scatter_keys(self, rows):
        rows = lax.psum_scatter(rows, "seq", scatter_dimension=0, tiled=True)
        if self.spread > 1:
            rows = lax.psum_scatter(
                rows,
                "tensor",
                scatter_dimension=0,
                axis_index_groups=self.slot_groups,
                tiled=True,
            )
        return rows

    def gather_weight(self, shard):
        part = shard.shape[0] // self.seq
        own = lax.dynamic_slice_in_dim(shard, self.half * part, part, 0)
        return lax.all_gather(own, ("tensor", "seq"), axis=0, tiled=True)

    def gather_columns(self, shard):
        depth, blocks, own = shard.shape
        whole = self.gather_weight(shard.reshape(depth, blocks * own))
        whole = whole.reshape(self.tensor, depth, blocks, own)
        return jnp.transpose(whole, (1, 2, 0, 3)).reshape(depth, blocks * self.tensor * own)

    def reduce_rows(self, gradient):
        rows, width = gradient.shape
        parts = gradient.reshape(self.tensor, rows // self.tensor, self.seq, width // self.seq)
        parts = jnp.transpose(parts, (2, 0, 1, 3)).reshape(
            self.seq * rows, width // self.seq
        )
        return self.reduce(parts)

    def reduce_columns(self, gradient, blocks):
        depth, width = gradient.shape
        own = width // blocks // self.tensor
        parts = gradient.reshape(self.seq, depth // self.seq, blocks, self.tensor, own)
        parts = jnp.transpose(parts, (0, 3, 1, 2, 4)).reshape(
            self.seq * self.tensor * depth // self.seq, blocks * own
        )
        return self.reduce(parts).reshape(depth // self.seq, blocks, own)

    def reduce(self, parts):
        own = lax.psum_scatter(parts, ("seq", "tensor"), scatter_dimension=0, tiled=True)
        return lax.psum(own, "dp").astype(F32)


def local(
    source,
    target,
    out_grad,
    source_segments,
    target_segments,
    enc_gain,
    enc_shift,
    enc_qkv,
    enc_proj,
    enc_up,
    enc_down,
    dec_gain,
    dec_shift,
    dec_self_qkv,
    dec_self_proj,
    dec_cross_q,
    dec_cross_kv,
    dec_cross_proj,
    dec_up,
    dec_down,
):
    width = source.shape[2]
    lay = Layout(source.shape[0])
    w_enc_qkv = lay.gather_columns(enc_qkv)
    w_self_qkv = lay.gather_columns(dec_self_qkv)
    w_enc_proj = lay.gather_weight(enc_proj)
    w_self_proj = lay.gather_weight(dec_self_proj)
    w_enc_up = lay.gather_columns(enc_up[:, None])
    w_enc_down = lay.gather_weight(enc_down)
    w_cross_q = lay.gather_columns(dec_cross_q[:, None])
    w_cross_kv = lay.gather_columns(dec_cross_kv)
    w_cross_proj = lay.gather_weight(dec_cross_proj)
    w_dec_up = lay.gather_columns(dec_up[:, None])
    w_dec_down = lay.gather_weight(dec_down)
    slot = lax.rem(lay.place, lay.slots)
    rows = source.shape[1] * lay.slots
    first_row = (lay.half * lay.spread + lay.place // lay.slots) * rows
    source_ids = lax.dynamic_index_in_dim(source_segments, slot, 0, keepdims=False)
    target_ids = lax.dynamic_index_in_dim(target_segments, slot, 0, keepdims=False)
    ids = jnp.arange(LANES, dtype=jnp.int32) % HEAD_DIM
    own_source = lax.dynamic_slice_in_dim(source_ids, first_row, rows, 0)
    own_target = lax.dynamic_slice_in_dim(target_ids, first_row, rows, 0)
    source_query = jnp.where(own_source[:, None] == ids[None], NEG, 0.0).astype(BF16)
    target_query = jnp.where(own_target[:, None] == ids[None], NEG, 0.0).astype(BF16)
    counted = ids[None] < IDS
    source_key = ((source_ids[:, None] != ids[None]) & counted).astype(BF16)
    target_key = ((target_ids[:, None] != ids[None]) & counted).astype(BF16)
    first = first_row[None].astype(jnp.int32)

    x_source = lay.to_slots(source).astype(F32)
    x_target = lay.to_slots(target).astype(F32)
    cotangent = lay.to_slots(out_grad).astype(F32)

    rows_a = layer_norm(x_source, enc_gain[0], enc_shift[0]).astype(BF16)
    qkv_a = project(rows_a, w_enc_qkv).astype(BF16)
    query_a = qkv_a[:, :width]
    pairs_a = lay.gather_keys(qkv_a[:, width:])
    mixed_a, total_a = attend(
        query_a, pairs_a[:, :width], pairs_a[:, width:], source_query, source_key, first, False
    )
    hidden = x_source + project(mixed_a, w_enc_proj)
    rows_c = layer_norm(x_target, dec_gain[0], dec_shift[0]).astype(BF16)
    qkv_c = project(rows_c, w_self_qkv).astype(BF16)
    query_c = qkv_c[:, :width]
    pairs_c = lay.gather_keys(qkv_c[:, width:])
    mixed_c, total_c = attend(
        query_c, pairs_c[:, :width], pairs_c[:, width:], target_query, target_key, first, True
    )
    after_self = x_target + project(mixed_c, w_self_proj)
    rows_b = layer_norm(hidden, enc_gain[1], enc_shift[1]).astype(BF16)
    inner_b = project(rows_b, w_enc_up)
    active_b = exact_gelu(inner_b).astype(BF16)
    encoded = hidden + project(active_b, w_enc_down)
    rows_m = layer_norm(encoded, enc_gain[2], enc_shift[2]).astype(BF16)
    pairs_m = lay.gather_keys(project(rows_m, w_cross_kv).astype(BF16))
    rows_e = layer_norm(after_self, dec_gain[1], dec_shift[1]).astype(BF16)
    query_e = project(rows_e, w_cross_q).astype(BF16)
    mixed_e, total_e = attend(
        query_e, pairs_m[:, :width], pairs_m[:, width:], target_query, source_key, first, False
    )
    after_cross = after_self + project(mixed_e, w_cross_proj)
    rows_f = layer_norm(after_cross, dec_gain[2], dec_shift[2]).astype(BF16)
    inner_f = project(rows_f, w_dec_up)
    active_f = exact_gelu(inner_f).astype(BF16)
    final_rows = after_cross + project(active_f, w_dec_down)
    decoded, final_back = jax.vjp(layer_norm, final_rows, dec_gain[3], dec_shift[3])

    d_final, dec_gain_three, dec_shift_three = final_back(cotangent)

    def ffn_back(d_out, rows_in, inner, active, weight_up, weight_down):
        d_low = d_out.astype(BF16)
        grad_down = lay.reduce_rows(weight_grad(active, d_low))
        d_active = back_project(d_low, weight_down)
        _, gelu_back = jax.vjp(exact_gelu, inner)
        d_inner = gelu_back(d_active)[0].astype(BF16)
        grad_up = lay.reduce_columns(weight_grad(rows_in, d_inner), 1)[:, 0]
        return back_project(d_inner, weight_up), grad_up, grad_down

    d_normed, grad_dec_up, grad_dec_down = ffn_back(
        d_final, rows_f, inner_f, active_f, w_dec_up, w_dec_down
    )
    d_input, dec_gain_two, dec_shift_two = norm_back(
        after_cross, dec_gain[2], dec_shift[2], d_normed
    )
    d_cross = d_final + d_input
    d_low = d_cross.astype(BF16)
    grad_cross_proj = lay.reduce_rows(weight_grad(mixed_e, d_low))
    d_mixed = back_project(d_low, w_cross_proj).astype(BF16)
    d_query, d_keys, d_values = attend_back(
        query_e,
        pairs_m[:, :width],
        pairs_m[:, width:],
        target_query,
        source_key,
        first,
        False,
        total_e,
        mixed_e,
        d_mixed,
    )
    d_pairs = lay.scatter_keys(jnp.concatenate([d_keys, d_values], 1))
    grad_cross_q = lay.reduce_columns(weight_grad(rows_e, d_query), 1)[:, 0]
    grad_cross_kv = lay.reduce_columns(weight_grad(rows_m, d_pairs), 2)
    d_normed = back_project(d_query, w_cross_q)
    d_memory = back_project(d_pairs, w_cross_kv)
    d_input, dec_gain_one, dec_shift_one = norm_back(
        after_self, dec_gain[1], dec_shift[1], d_normed
    )
    d_self = d_cross + d_input
    d_encoded, enc_gain_two, enc_shift_two = norm_back(encoded, enc_gain[2], enc_shift[2], d_memory)
    d_normed, grad_enc_up, grad_enc_down = ffn_back(
        d_encoded, rows_b, inner_b, active_b, w_enc_up, w_enc_down
    )
    d_input, enc_gain_one, enc_shift_one = norm_back(hidden, enc_gain[1], enc_shift[1], d_normed)
    d_hidden = d_encoded + d_input

    def self_back(d_out, rows_in, query, pairs, marks, causal, totals, mixed, w_qkv, w_proj):
        d_low = d_out.astype(BF16)
        grad_proj = lay.reduce_rows(weight_grad(mixed, d_low))
        d_mixed = back_project(d_low, w_proj).astype(BF16)
        d_query, d_keys, d_values = attend_back(
            query,
            pairs[:, :width],
            pairs[:, width:],
            marks[0],
            marks[1],
            first,
            causal,
            totals,
            mixed,
            d_mixed,
        )
        d_pairs = lay.scatter_keys(jnp.concatenate([d_keys, d_values], 1))
        d_qkv = jnp.concatenate([d_query, d_pairs], 1)
        grad_qkv = lay.reduce_columns(weight_grad(rows_in, d_qkv), 3)
        return back_project(d_qkv, w_qkv), grad_qkv, grad_proj

    d_normed, grad_self_qkv, grad_self_proj = self_back(
        d_self,
        rows_c,
        query_c,
        pairs_c,
        (target_query, target_key),
        True,
        total_c,
        mixed_c,
        w_self_qkv,
        w_self_proj,
    )
    d_input, dec_gain_zero, dec_shift_zero = norm_back(
        x_target, dec_gain[0], dec_shift[0], d_normed
    )
    target_grad = d_self + d_input
    d_normed, grad_enc_qkv, grad_enc_proj = self_back(
        d_hidden,
        rows_a,
        query_a,
        pairs_a,
        (source_query, source_key),
        False,
        total_a,
        mixed_a,
        w_enc_qkv,
        w_enc_proj,
    )
    d_input, enc_gain_zero, enc_shift_zero = norm_back(
        x_source, enc_gain[0], enc_shift[0], d_normed
    )
    source_grad = d_hidden + d_input
    norms = jnp.stack(
        [
            enc_gain_zero,
            enc_gain_one,
            enc_gain_two,
            enc_shift_zero,
            enc_shift_one,
            enc_shift_two,
            dec_gain_zero,
            dec_gain_one,
            dec_gain_two,
            dec_gain_three,
            dec_shift_zero,
            dec_shift_one,
            dec_shift_two,
            dec_shift_three,
        ]
    )
    part = width // lay.seq
    norms = lax.dynamic_slice_in_dim(
        lax.psum(norms, ("dp", "seq", "tensor")), lay.half * part, part, 1
    )
    return (
        lay.from_slots(decoded.astype(BF16)),
        lay.from_slots(source_grad.astype(BF16)).astype(F32),
        lay.from_slots(target_grad.astype(BF16)).astype(F32),
        norms[0:3],
        norms[3:6],
        grad_enc_qkv,
        grad_enc_proj,
        grad_enc_up,
        grad_enc_down,
        norms[6:10],
        norms[10:14],
        grad_self_qkv,
        grad_self_proj,
        grad_cross_q,
        grad_cross_kv,
        grad_cross_proj,
        grad_dec_up,
        grad_dec_down,
    )


def swap_pairs(count, bit):
    return [(i, i ^ bit) for i in range(count)]


def norm_parts(inputs):
    centred = inputs - jnp.mean(inputs, -1, keepdims=True)
    scale = lax.rsqrt(jnp.mean(centred * centred, -1, keepdims=True) + EPS)
    return centred * scale, scale


def norm_pull(hat, scale, gain, cotangent):
    tilted = cotangent * gain
    return scale * (
        tilted
        - jnp.mean(tilted, -1, keepdims=True)
        - hat * jnp.mean(tilted * hat, -1, keepdims=True)
    )


ROW_BLOCK = 256
VMEM = 56 << 20
LIGHT = pl.CostEstimate(flops=1 << 20, bytes_accessed=1 << 16, transcendentals=0)


def row_call(kernel, inputs, vectors, outs, sums, name):
    rows, width = inputs[0].shape
    block = pl.BlockSpec((ROW_BLOCK, width), lambda i: (i, 0))
    whole = pl.BlockSpec((1, width), lambda i: (0, 0))
    return pl.pallas_call(
        kernel,
        grid=(rows // ROW_BLOCK,),
        in_specs=[block] * len(inputs) + [whole] * len(vectors),
        out_specs=[block] * len(outs) + [whole] * sums,
        out_shape=[jax.ShapeDtypeStruct((rows, width), kind) for kind in outs]
        + [jax.ShapeDtypeStruct((1, width), F32)] * sums,
        compiler_params=pltpu.CompilerParams(vmem_limit_bytes=VMEM),
        cost_estimate=LIGHT,
        name=name,
    )(*inputs, *vectors)


def norm_kernel(x_ref, gain_ref, shift_ref, low_ref):
    hat, _ = norm_parts(x_ref[...].astype(F32))
    low_ref[...] = (hat * gain_ref[...] + shift_ref[...]).astype(BF16)


def norm_rows(inputs, gain, shift):
    return row_call(norm_kernel, [inputs], [gain, shift], [BF16], 0, "norm_rows")[0]


def add_norm_kernel(x_ref, own_ref, other_ref, gain_ref, shift_ref, sum_ref, low_ref):
    total = (
        x_ref[...].astype(F32) + own_ref[...].astype(F32) + other_ref[...].astype(F32)
    )
    sum_ref[...] = total
    hat, _ = norm_parts(total)
    low_ref[...] = (hat * gain_ref[...] + shift_ref[...]).astype(BF16)


def add_norm(inputs, own, other, gain, shift):
    return row_call(
        add_norm_kernel, [inputs, own, other], [gain, shift], [F32, BF16], 0, "add_norm"
    )


def add_sums(first, gain_out, shift_out, cotangent, hat):
    @pl.when(first)
    def _():
        gain_out[...] = jnp.zeros_like(gain_out)
        shift_out[...] = jnp.zeros_like(shift_out)

    gain_out[...] += jnp.sum(cotangent * hat, 0, keepdims=True)
    shift_out[...] += jnp.sum(cotangent, 0, keepdims=True)


def last_norm_kernel(
    x_ref, own_ref, other_ref, cot_ref, gain_ref, shift_ref, y_ref, d_ref, low_ref, dg_ref, ds_ref
):
    total = (
        x_ref[...].astype(F32) + own_ref[...].astype(F32) + other_ref[...].astype(F32)
    )
    hat, scale = norm_parts(total)
    y_ref[...] = (hat * gain_ref[...] + shift_ref[...]).astype(BF16)
    cotangent = cot_ref[...].astype(F32)
    d_total = norm_pull(hat, scale, gain_ref[...], cotangent)
    d_ref[...] = d_total
    low_ref[...] = d_total.astype(BF16)
    add_sums(pl.program_id(0) == 0, dg_ref, ds_ref, cotangent, hat)


def last_norm(inputs, own, other, cotangent, gain, shift):
    return row_call(
        last_norm_kernel,
        [inputs, own, other, cotangent],
        [gain, shift],
        [BF16, F32, BF16],
        2,
        "last_norm",
    )


def norm_back_kernel(residual, low, *refs):
    x_ref, own_ref, other_ref = refs[:3]
    refs = refs[3:]
    if residual:
        res_ref, refs = refs[0], refs[1:]
    gain_ref, refs = refs[0], refs[1:]
    hat, scale = norm_parts(x_ref[...].astype(F32))
    cotangent = own_ref[...].astype(F32) + other_ref[...].astype(F32)
    d_total = norm_pull(hat, scale, gain_ref[...], cotangent)
    if residual:
        d_total = d_total + res_ref[...]
    refs[0][...] = d_total.astype(refs[0].dtype)
    if low:
        refs[1][...] = d_total.astype(BF16)
    add_sums(pl.program_id(0) == 0, refs[-2], refs[-1], cotangent, hat)


def norm_back_rows(inputs, own, other, gain, residual, kinds):
    return row_call(
        functools.partial(norm_back_kernel, residual is not None, len(kinds) > 1),
        [inputs, own, other] + ([] if residual is None else [residual]),
        [gain],
        kinds,
        2,
        "norm_back",
    )


def chip_attend_kernel(causal, q_ref, k_ref, v_ref, qa_ref, ka_ref, o_ref, lse_ref):
    rows = q_ref.shape[0]
    block = 256
    low_half = lax.broadcasted_iota(jnp.int32, (1, LANES), 1) < HEAD_DIM
    for start in range(0, rows, block):
        keys = start + block if causal else k_ref.shape[0]
        query = q_ref[pl.ds(start, block), :] * BF16(SCALE)
        query_mark = qa_ref[pl.ds(start, block), :]
        key_block = k_ref[:keys, :]
        key_mark = ka_ref[:keys, :]
        values = v_ref[:keys, :]
        halves = []
        lses = []
        for head in range(2):
            keep = low_half if head == 0 else jnp.logical_not(low_half)
            scores = mxu(
                jnp.where(keep, query, query_mark), jnp.where(keep, key_block, key_mark), NT
            )
            if causal:
                scores = jnp.where(
                    lax.broadcasted_iota(jnp.int32, (block, keys), 1)
                    <= start + lax.broadcasted_iota(jnp.int32, (block, keys), 0),
                    scores,
                    NEG,
                )
            top = jnp.max(scores, -1, keepdims=True)
            weights = jnp.exp(scores - top)
            total = jnp.sum(weights, -1, keepdims=True)
            mixed = mxu(weights.astype(BF16), values, NN)
            halves.append(mixed / total)
            lses.append(top + jnp.log(total))
        o_ref[pl.ds(start, block), :] = jnp.where(low_half, halves[0], halves[1]).astype(BF16)
        turned = jnp.where(low_half, lses[0], lses[1]).T
        lse_ref[0, 0:1, pl.ds(start, block)] = turned[0:1]
        lse_ref[0, 1:2, pl.ds(start, block)] = turned[HEAD_DIM : HEAD_DIM + 1]


def pair_spec(rows, stride, offset):
    return pl.BlockSpec((rows, LANES), lambda p: (0, stride * p + offset))


def chip_attend(queries, q_at, pairs, k_at, v_at, query_mark, key_mark, causal):
    rows = queries.shape[0]
    keys = pairs.shape[0]
    count = queries.shape[1] // LANES // q_at[0]
    return pl.pallas_call(
        functools.partial(chip_attend_kernel, causal),
        grid=(count,),
        in_specs=[
            pair_spec(rows, *q_at),
            pair_spec(keys, *k_at),
            pair_spec(keys, *v_at),
            pl.BlockSpec((rows, LANES), lambda p: (0, 0)),
            pl.BlockSpec((keys, LANES), lambda p: (0, 0)),
        ],
        out_specs=[
            pair_spec(rows, 1, 0),
            pl.BlockSpec((1, 2, rows), lambda p: (p, 0, 0)),
        ],
        out_shape=[
            jax.ShapeDtypeStruct((rows, count * LANES), BF16),
            jax.ShapeDtypeStruct((count, 2, rows), F32),
        ],
        compiler_params=pltpu.CompilerParams(vmem_limit_bytes=VMEM),
        cost_estimate=LIGHT,
        name="attend",
    )(queries, pairs, pairs, query_mark, key_mark)


def chip_attend_back_kernel(causal, fused, *refs):
    q_ref, k_ref, v_ref, qa_ref, ka_ref, lse_ref, o_ref, do_ref = refs[:8]
    outs, (dk_acc, dv_acc) = refs[8:-2], refs[-2:]
    rows = q_ref.shape[0]
    block = 256
    low_half = lax.broadcasted_iota(jnp.int32, (1, LANES), 1) < HEAD_DIM
    zero = jnp.zeros((), BF16)
    dk_acc[...] = jnp.zeros_like(dk_acc)
    dv_acc[...] = jnp.zeros_like(dv_acc)
    for start in range(0, rows, block):
        keys = start + block if causal else k_ref.shape[0]
        span = pl.ds(start, block)
        query = q_ref[span, :] * BF16(SCALE)
        query_mark = qa_ref[span, :]
        key_block = k_ref[:keys, :]
        key_mark = ka_ref[:keys, :]
        values = v_ref[:keys, :]
        d_out = do_ref[span, :]
        inner = (d_out.astype(F32) * o_ref[span, :].astype(F32)).T
        d_query = None
        for head in range(2):
            keep = low_half if head == 0 else jnp.logical_not(low_half)
            delta = jnp.sum(
                inner[head * HEAD_DIM : (head + 1) * HEAD_DIM], axis=0, keepdims=True
            )
            scores = mxu(
                jnp.where(keep, key_block, key_mark), jnp.where(keep, query, query_mark), NT
            )
            if causal:
                scores = jnp.where(
                    lax.broadcasted_iota(jnp.int32, (keys, block), 0)
                    <= start + lax.broadcasted_iota(jnp.int32, (keys, block), 1),
                    scores,
                    NEG,
                )
            probs = jnp.exp(scores - lse_ref[0, head : head + 1, span])
            own_out = jnp.where(keep, d_out, zero)
            d_probs = mxu(values, own_out, NT)
            d_scores = (probs * (d_probs - delta)).astype(BF16)
            dv_acc[:keys, :] += mxu(probs.astype(BF16), own_out, NN)
            dk_acc[:keys, :] += mxu(d_scores, jnp.where(keep, query, zero), NN)
            term = mxu(jnp.where(keep, key_block, zero), d_scores, TN)
            d_query = term if d_query is None else d_query + term
        outs[0][span, :LANES] = (d_query * SCALE).T.astype(BF16)
    if fused:
        outs[0][:, LANES : 2 * LANES] = dk_acc[...].astype(BF16)
        outs[0][:, 2 * LANES :] = dv_acc[...].astype(BF16)
    else:
        outs[1][:, :LANES] = dk_acc[...].astype(BF16)
        outs[1][:, LANES:] = dv_acc[...].astype(BF16)


def chip_attend_back(
    queries, q_at, pairs, k_at, v_at, query_mark, key_mark, causal, log_total, mixed, d_mixed, fused
):
    rows = queries.shape[0]
    keys = pairs.shape[0]
    count = mixed.shape[1] // LANES

    def out(rows, blocks):
        return (
            pl.BlockSpec((rows, blocks * LANES), lambda p: (0, p)),
            jax.ShapeDtypeStruct((rows, count * blocks * LANES), BF16),
        )

    outs = [out(rows, 3)] if fused else [out(rows, 1), out(keys, 2)]
    return pl.pallas_call(
        functools.partial(chip_attend_back_kernel, causal, fused),
        grid=(count,),
        in_specs=[
            pair_spec(rows, *q_at),
            pair_spec(keys, *k_at),
            pair_spec(keys, *v_at),
            pl.BlockSpec((rows, LANES), lambda p: (0, 0)),
            pl.BlockSpec((keys, LANES), lambda p: (0, 0)),
            pl.BlockSpec((1, 2, rows), lambda p: (p, 0, 0)),
            pair_spec(rows, 1, 0),
            pair_spec(rows, 1, 0),
        ],
        out_specs=[spec for spec, _ in outs],
        out_shape=[shape for _, shape in outs],
        scratch_shapes=[pltpu.VMEM((keys, LANES), F32), pltpu.VMEM((keys, LANES), F32)],
        compiler_params=pltpu.CompilerParams(vmem_limit_bytes=VMEM),
        cost_estimate=LIGHT,
        name="attend_back",
    )(queries, pairs, pairs, query_mark, key_mark, log_total, mixed, d_mixed)


def piece_kernel(kind, low, high, count, x_ref, *refs):
    if count == 1:
        order_ref, stack_ref, rest = refs[0], refs[1], refs[2:]
        weights = [stack_ref.at[order_ref[i]] for i in range(stack_ref.shape[0])]
    else:
        weights, rest = refs[:count], refs[count:]
    own = high - low
    total = None
    for i, ref in enumerate(weights):
        span = pl.ds(i * own, own)
        if kind == "columns":
            rest[-1][:, span] = mxu(x_ref[...], ref[:, low:high], NN).astype(BF16)
        elif kind == "gelu":
            inner = mxu(x_ref[...], ref[:, low:high], NN)
            below = 0.5 + 0.5 * lax.erf(inner * (0.5**0.5))
            rest[0][:, span] = (inner * below).astype(BF16)
            bell = jnp.exp(inner * inner * (-0.5)) * (0.5 / jnp.pi) ** 0.5
            rest[1][:, span] = (below + inner * bell).astype(BF16)
        elif kind == "rows":
            term = mxu(x_ref[:, span], ref[low:high, :], NN)
            total = term if total is None else total + term
        elif kind == "columns_back":
            term = mxu(x_ref[:, span], ref[:, low:high], NT)
            total = term if total is None else total + term
        elif kind == "rows_back":
            rest[-1][:, span] = mxu(x_ref[...], ref[low:high, :], NT).astype(BF16)
        elif kind == "rows_back_slope":
            term = mxu(x_ref[...], ref[low:high, :], NT)
            rest[-1][:, span] = (term * rest[0][:, span].astype(F32)).astype(BF16)
    if total is not None:
        rest[-1][...] = total.astype(BF16)


def piece_product(kind, rows_in, pieces, low, high, slope=None, block=512):
    rows, depth = rows_in.shape
    stacked = len(pieces) == 2
    shape = pieces[1].shape[1:] if stacked else pieces[0].shape
    all_own = 4 * (high - low)
    width = {
        "columns": all_own,
        "gelu": all_own,
        "rows": shape[1],
        "columns_back": shape[0],
        "rows_back": all_own,
        "rows_back_slope": all_own,
    }[kind]
    outs = 2 if kind == "gelu" else 1
    out = pl.BlockSpec((block, width), lambda i: (i, 0))
    results = pl.pallas_call(
        functools.partial(piece_kernel, kind, low, high, 1 if stacked else len(pieces)),
        grid=(rows // block,),
        in_specs=[pl.BlockSpec((block, depth), lambda i: (i, 0))]
        + (
            [
                pl.BlockSpec(memory_space=pltpu.SMEM),
                pl.BlockSpec(pieces[1].shape, lambda i: (0, 0, 0)),
            ]
            if stacked
            else [pl.BlockSpec(piece.shape, lambda i: (0, 0)) for piece in pieces]
        )
        + ([] if slope is None else [out]),
        out_specs=[out] * outs,
        out_shape=[jax.ShapeDtypeStruct((rows, width), BF16)] * outs,
        compiler_params=pltpu.CompilerParams(vmem_limit_bytes=VMEM),
        cost_estimate=LIGHT,
        name="product_" + kind,
    )(rows_in, *pieces, *([] if slope is None else [slope]))
    return results if outs > 1 else results[0]


def weight_kernel(count, *refs):
    out_ref = refs[-1]
    at = 0
    for i in range(count):
        own = refs[i].shape[1]
        out_ref[pl.ds(at, own), :] = mxu(refs[i][...], refs[count + i][...], TN).astype(BF16)
        at += own


def weight_grads(pairs, part):
    rows, width = pairs[0][1].shape
    owns = [hidden.shape[1] // 4 for hidden, _ in pairs]
    return pl.pallas_call(
        functools.partial(weight_kernel, len(pairs)),
        grid=(2,),
        in_specs=[
            pl.BlockSpec((rows, own), lambda i: (0, 2 * part + i)) for own in owns
        ]
        + [pl.BlockSpec((rows, width), lambda i: (0, 0)) for _ in pairs],
        out_specs=pl.BlockSpec((sum(owns), width), lambda i: (i, 0)),
        out_shape=jax.ShapeDtypeStruct((2 * sum(owns), width), BF16),
        compiler_params=pltpu.CompilerParams(vmem_limit_bytes=VMEM),
        cost_estimate=LIGHT,
        name="weight_grads",
    )(*[hidden for hidden, _ in pairs], *[wide for _, wide in pairs])


CROSS = ("seq", "tensor")


class Chip:
    def __init__(self):
        self.core = lax.axis_index("seq")
        self.place = lax.axis_index("tensor")
        self.line = lax.axis_index("dp")
        self.first = [(i, i ^ 1) for i in range(4)] + [(4 + i, 4 + (i ^ 2)) for i in range(4)]
        self.second = [(i, i ^ 2) for i in range(4)] + [(4 + i, 4 + (i ^ 1)) for i in range(4)]

    def other(self, block):
        return lax.ppermute(block, "seq", swap_pairs(2, 1))

    def gather(self, block):
        near = lax.ppermute(block, CROSS, self.first)
        side = lax.ppermute(block, CROSS, self.second)
        far = lax.ppermute(side, CROSS, self.first)
        return [block, side, near, far]

    def ordered(self, own, other, index):
        first = index == 0
        return jnp.concatenate([jnp.where(first, own, other), jnp.where(first, other, own)], 0)

    def swap_start(self, blocks):
        near_bit = 1 + self.core

        def to(bits):
            return lax.dynamic_index_in_dim(blocks, jnp.bitwise_xor(self.place, bits), 0)

        cuts = lax.optimization_barrier((to(0), to(near_bit), to(3 - near_bit), to(3)))
        far = lax.ppermute(cuts[3], "tensor", swap_pairs(4, 3))
        return cuts[0], self.send_near(cuts[1]), self.send_side(cuts[2]), far

    def swap_end(self, parts):
        own, near, side, far = parts
        low, high = lax.rem(self.place, 2), self.place // 2
        first = self.core == 0
        beside, across = jnp.where(first, near, side), jnp.where(first, side, near)
        blocks = self.ordered(self.ordered(own, beside, low), self.ordered(across, far, low), high)
        return blocks.reshape(-1, own.shape[2]) if own.ndim == 3 else blocks

    def swap_rows(self, block):
        return self.swap_end(self.swap_start(block))

    def both_cores(self, rows):
        return self.ordered(rows, self.other(rows), self.core)

    def from_start(self, rows):
        half = rows.shape[0] // 2
        own = lax.dynamic_slice_in_dim(rows, self.core * half, half, 0)
        return self.swap_start(own.reshape(4, half // 4, -1))

    def from_end(self, parts):
        return self.swap_end(parts).reshape((4,) + parts[0].shape[1:])

    def from_slot(self, rows):
        return self.from_end(self.from_start(rows))

    def send_near(self, block):
        return lax.ppermute(block, CROSS, self.first)

    def send_side(self, block):
        return lax.ppermute(block, CROSS, self.second)

    def along(self, block, bit):
        return lax.ppermute(block, "dp", swap_pairs(4, bit))


def add_low(left, right):
    return (left.astype(F32) + right.astype(F32)).astype(BF16)


def chip_local(
    source,
    target,
    out_grad,
    source_segments,
    target_segments,
    enc_gain,
    enc_shift,
    enc_qkv,
    enc_proj,
    enc_up,
    enc_down,
    dec_gain,
    dec_shift,
    dec_self_qkv,
    dec_self_proj,
    dec_cross_q,
    dec_cross_kv,
    dec_cross_proj,
    dec_up,
    dec_down,
):
    chip = Chip()
    core = chip.core
    tie = lax.optimization_barrier

    def own_columns(weight):
        part = weight.shape[-1] // 2
        cut = lax.dynamic_slice_in_dim(weight, core * part, part, weight.ndim - 1)
        return cut.reshape(weight.shape[0], -1)

    def own_rows(weight):
        part = weight.shape[0] // 2
        return lax.dynamic_slice_in_dim(weight, core * part, part, 0)

    def pin(value, *others):
        return tie((value,) + others)[0]

    bundles = [
        own_columns(enc_qkv),
        own_columns(dec_self_qkv),
        jnp.concatenate([own_rows(enc_proj), own_rows(dec_self_proj), own_rows(dec_cross_proj)], 0),
        jnp.concatenate([own_columns(dec_cross_q), own_columns(dec_cross_kv)], 1),
        own_rows(dec_down),
    ]
    near_bit = 1 + core
    order = jnp.bitwise_xor(
        chip.place, jnp.stack([0 * core, 3 - near_bit, near_bit, 0 * core + 3])
    ).astype(jnp.int32)

    def all_groups(own):
        return [order, lax.all_gather(own, "tensor", axis=0)]

    inner = enc_up.shape[1] // 2
    pieces = [None] * len(bundles)

    def launch(index, *after):
        own = pin(bundles[index], *after)
        pieces[index] = [own, chip.send_side(own), chip.send_near(own)]
        return pieces[index][1]

    def relay(index, value):
        side, near, value = tie((pieces[index][1], pieces[index][2], value))
        pieces[index][1:] = [side, near]
        pieces[index].append(chip.send_near(side))
        return value

    def arrived(index, value):
        tied = tie(tuple(pieces[index]) + (value,))
        pieces[index] = list(tied[:-1])
        return tied[-1]

    def enc(index):
        return enc_gain[index : index + 1], enc_shift[index : index + 1]

    def dec(index):
        return dec_gain[index : index + 1], dec_shift[index : index + 1]

    def part_rows(rows_in, weight, low, high):
        own = piece_product("rows", rows_in, weight, low, high)
        return own, chip.other(own)

    def part_back(grad, weight, low, high):
        own = piece_product("columns_back", grad, weight, low, high)
        return own, chip.other(own)

    fused_at = ((3, 0), (3, 1), (3, 2))

    def attend_self(qkv, marks, causal):
        return chip_attend(
            qkv, fused_at[0], qkv, fused_at[1], fused_at[2], marks[0], marks[1], causal
        )

    launch(0)
    swapped = arrived(0, chip.swap_rows(relay(0, source)))
    launch(1, swapped)
    x_source = chip.both_cores(swapped)
    sent_target = chip.swap_start(pin(target, swapped))
    w_enc_up = all_groups(pin(own_columns(enc_up), swapped))
    source_ids = lax.dynamic_index_in_dim(source_segments, chip.place, 0, keepdims=False)
    target_ids = lax.dynamic_index_in_dim(target_segments, chip.place, 0, keepdims=False)
    ids = jnp.arange(LANES, dtype=jnp.int32)[None] % HEAD_DIM
    counted = ids < IDS
    source_query = jnp.where(source_ids[:, None] == ids, NEG, 0.0).astype(BF16)
    target_query = jnp.where(target_ids[:, None] == ids, NEG, 0.0).astype(BF16)
    source_key = ((source_ids[:, None] != ids) & counted).astype(BF16)
    target_key = ((target_ids[:, None] != ids) & counted).astype(BF16)
    rows_a = norm_rows(x_source, *enc(0))
    rows_a = pin(rows_a, source_query, source_key)
    qkv_a = piece_product("columns", rows_a, pieces[0], 0, bundles[0].shape[1])
    launch(2, qkv_a)
    mixed_a, total_a = attend_self(qkv_a, (source_query, source_key), False)
    mixed_a, sent_target = tie((relay(1, mixed_a), sent_target))
    x_target = chip.both_cores(chip.swap_end(sent_target))
    w_enc_down = all_groups(pin(own_rows(enc_down), mixed_a))
    rows_c = norm_rows(pin(x_target, target_query, target_key), *dec(0))
    rows_c = arrived(1, rows_c)
    qkv_c = piece_product("columns", rows_c, pieces[1], 0, bundles[1].shape[1])
    qkv_c = relay(2, qkv_c)
    w_dec_up = all_groups(pin(own_columns(dec_up), qkv_c))
    mixed_c, total_c = attend_self(qkv_c, (target_query, target_key), True)
    proj_rows = bundles[2].shape[0] // 3
    mixed_c, mixed_a = tie((arrived(2, mixed_c), mixed_a))
    launch(3, mixed_c)
    own_a, other_a = part_rows(mixed_a, pieces[2], 0, proj_rows)
    own_c, other_c = part_rows(mixed_c, pieces[2], proj_rows, 2 * proj_rows)
    other_a, other_c = tie((other_a, other_c, own_a, own_c))[:2]
    hidden, rows_b = add_norm(x_source, own_a, other_a, *enc(1))
    after_self, rows_e = add_norm(x_target, own_c, other_c, *dec(1))
    rows_b = pin(rows_b, rows_e)
    active_b, slope_b = piece_product("gelu", rows_b, w_enc_up, 0, inner, block=256)
    active_b = relay(3, active_b)
    encoded, rows_m = add_norm(hidden, *part_rows(active_b, w_enc_down, 0, inner), *enc(2))
    rows_m, rows_e = tie((arrived(3, rows_m), rows_e))
    launch(4, rows_m)
    head_width = dec_cross_q.shape[1] // 2
    pairs_m = piece_product("columns", rows_m, pieces[3], head_width, 3 * head_width)
    query_e = piece_product("columns", rows_e, pieces[3], 0, head_width)
    query_e = pin(query_e, pairs_m)
    mixed_e, total_e = chip_attend(
        query_e, (1, 0), pairs_m, (2, 0), (2, 1), target_query, source_key, False
    )
    mixed_e = relay(4, mixed_e)
    after_cross, rows_f = add_norm(
        after_self, *part_rows(mixed_e, pieces[2], 2 * proj_rows, 3 * proj_rows), *dec(2)
    )
    sent_grad = chip.swap_start(pin(out_grad, rows_f))
    active_f, slope_f = piece_product("gelu", rows_f, w_dec_up, 0, inner, block=256)
    active_f, sent_grad = tie((arrived(4, active_f), sent_grad))
    cotangent = chip.both_cores(chip.swap_end(sent_grad))
    w_dec_down = pieces[4]
    decoded, d_final, low_final, gain_d3, shift_d3 = last_norm(
        after_cross, *part_rows(active_f, w_dec_down, 0, inner), cotangent, *dec(3)
    )


    low_bit = lax.rem(chip.line, 2)
    high_bit = chip.line // 2

    def here(value, step, *args):
        args, value = tie((args, value))
        *result, sent = step(*args)
        return pin(value, result[1], *sent), result

    def to_side(came, kept):
        half = kept.shape[0] // 2
        sent = add_low(kept[half:], came[half:])
        return chip.send_side(sent), add_low(kept[:half], came[:half]), [sent]

    def to_line(*states):
        def cut(bits):
            parts = []
            for came, kept in states:
                quarter = kept.shape[0] // 4
                at = jnp.bitwise_xor(chip.line, bits) * quarter
                parts.append(
                    add_low(
                        lax.dynamic_slice_in_dim(kept, at, quarter, 0),
                        lax.dynamic_slice_in_dim(came, at, quarter, 0),
                    )
                )
            return jnp.concatenate(parts, 0)

        sent = [cut(bits) for bits in (3, 2, 1)]
        return [chip.along(part, bits) for part, bits in zip(sent, (3, 2, 1))], cut(0), sent

    def from_line(came, own):
        total = own.astype(F32)
        for block in came:
            total = total + block.astype(F32)
        own = total.astype(BF16)
        return [chip.along(own, bits) for bits in (3, 2, 1)], own, []

    def to_core(came, own):
        far, next_but_one, next_one = came
        first = chip.ordered(own, next_one, low_bit)
        second = chip.ordered(next_but_one, far, low_bit)
        return share(chip.ordered(first, second, high_bit))

    def share(whole):
        width = whole.shape[1] // 2
        sent = lax.dynamic_slice_in_dim(whole, (1 - core) * width, width, 1)
        own = lax.dynamic_slice_in_dim(whole, core * width, width, 1)
        return chip.other(sent), own

    def in_place(came, own):
        return chip.ordered(own[None], came[None], core)

    def sum_line(*states):
        total = jnp.concatenate([add_low(*state) for state in states], 0)
        return None, total, []

    def send_half(value, *pairs):
        sent = weight_grads(list(pairs), 1)
        return pin(value, sent), chip.send_near(sent)

    def keep_half(value, came, *pairs):
        first, value = tie((pairs[0], value))
        kept = weight_grads([first] + list(pairs[1:]), 0)
        return pin(value, kept), (came, kept)

    def ffn_back(low_out, slope, weight):
        return piece_product("rows_back_slope", low_out, weight, 0, inner, slope)

    low_send, near_fd = send_half(low_final, (active_f, low_final))
    d_inner_f = ffn_back(low_send, slope_f, w_dec_down)
    d_inner_f, near_fu = send_half(d_inner_f, (d_inner_f, rows_f))
    own = piece_product("columns_back", d_inner_f, w_dec_up, 0, inner)
    own, near_fd = tie((own, near_fd))
    other = chip.other(own)
    hold, keep_fd = keep_half(own, near_fd, (active_f, low_final))
    hold, side_fd = here(hold, to_side, *keep_fd)
    hold, keep_fu = keep_half(hold, near_fu, (d_inner_f, rows_f))
    d_cross, low_cross, gain_d2, shift_d2 = norm_back_rows(
        after_cross, own, pin(other, hold), dec(2)[0], d_final, [F32, BF16]
    )
    d_mixed = piece_product("rows_back", low_cross, pieces[2], 2 * proj_rows, 3 * proj_rows)
    d_mixed, side_fu = here(d_mixed, to_side, *keep_fu)
    d_query_e, d_pairs_m = chip_attend_back(
        query_e,
        (1, 0),
        pairs_m,
        (2, 0),
        (2, 1),
        target_query,
        source_key,
        False,
        total_e,
        mixed_e,
        d_mixed,
        False,
    )
    d_pairs_m, (_, total_f) = here(d_pairs_m, sum_line, side_fd, side_fu)
    sum_f = lax.psum(total_f, "dp")
    own_m, other_m = part_back(d_pairs_m, pieces[3], head_width, 3 * head_width)
    own_e, other_e = part_back(pin(d_query_e, own_m), pieces[3], 0, head_width)
    d_encoded, low_encoded, gain_e2, shift_e2 = norm_back_rows(
        encoded, own_m, pin(other_m, own_e), enc(2)[0], None, [F32, BF16]
    )
    low_send, near_bd = send_half(low_encoded, (active_b, low_encoded))
    d_inner_b = ffn_back(low_send, slope_b, w_enc_down)
    d_inner_b, near_bu = send_half(d_inner_b, (d_inner_b, rows_b))
    own = piece_product("columns_back", d_inner_b, w_enc_up, 0, inner)
    own, near_bd, other_e = tie((own, near_bd, other_e))
    other = chip.other(own)
    hold, keep_bd = keep_half(own, near_bd, (active_b, low_encoded))
    hold, side_bd = here(hold, to_side, *keep_bd)
    hold, keep_bu = keep_half(hold, near_bu, (d_inner_b, rows_b))
    d_hidden, low_hidden, gain_e1, shift_e1 = norm_back_rows(
        hidden, own, pin(other, hold), enc(1)[0], d_encoded, [F32, BF16]
    )
    pairs_x = ((mixed_e, low_cross), (d_query_e, rows_e), (d_pairs_m, rows_m))
    own_e, side_bu = here(pin(own_e, low_hidden), to_side, *keep_bu)
    pairs_x = tie((pairs_x, own_e))[0]
    own_e, near_x = send_half(own_e, *pairs_x)
    own_e, keep_x = keep_half(own_e, near_x, *pairs_x)
    d_self, low_self, gain_d1, shift_d1 = norm_back_rows(
        after_self, own_e, other_e, dec(1)[0], d_cross, [F32, BF16]
    )

    def self_back(d_mixed, qkv, marks, causal, totals, mixed):
        (d_qkv,) = chip_attend_back(
            qkv,
            fused_at[0],
            qkv,
            fused_at[1],
            fused_at[2],
            marks[0],
            marks[1],
            causal,
            totals,
            mixed,
            d_mixed,
            True,
        )
        return d_qkv

    d_mixed = piece_product("rows_back", low_self, pieces[2], proj_rows, 2 * proj_rows)
    d_mixed, (_, total_b) = here(d_mixed, sum_line, side_bd, side_bu)
    d_qkv_c = self_back(d_mixed, qkv_c, (target_query, target_key), True, total_c, mixed_c)
    d_qkv_c, sum_f, total_b = tie((d_qkv_c, sum_f, total_b))
    sum_b = lax.psum(total_b, "dp")
    d_qkv_c, side_x = here(d_qkv_c, to_side, *keep_x)
    pairs_c = ((mixed_c, low_self), (d_qkv_c, rows_c))
    d_qkv_c, near_c = send_half(d_qkv_c, *pairs_c)
    own_c = piece_product("columns_back", d_qkv_c, pieces[1], 0, 3 * head_width)
    own_c, keep_c = keep_half(own_c, near_c, *pairs_c)
    low_hidden, decoded = tie((low_hidden, decoded, own_c))[:2]
    sent_decoded = chip.from_start(decoded)
    d_mixed = piece_product("rows_back", low_hidden, pieces[2], 0, proj_rows)
    d_qkv_a = self_back(d_mixed, qkv_a, (source_query, source_key), False, total_a, mixed_a)
    pairs_a = ((mixed_a, low_hidden), (d_qkv_a, rows_a))
    d_qkv_a, near_a = send_half(d_qkv_a, *pairs_a)
    d_qkv_a, side_c = here(d_qkv_a, to_side, *keep_c)
    own_a = piece_product("columns_back", d_qkv_a, pieces[0], 0, 3 * head_width)
    own_a, (_, total_xc) = here(own_a, sum_line, side_x, side_c)
    own_a, sum_b, total_xc, sent_decoded, near_a = tie(
        (own_a, sum_b, total_xc, sent_decoded, near_a)
    )
    decoded = chip.from_end(sent_decoded)
    sum_xc = lax.psum(total_xc, "dp")
    other_a, other_c = chip.other(own_a), chip.other(pin(own_c, own_a))
    own_a, keep_a = keep_half(own_a, near_a, *pairs_a)
    own_a, side_a = here(own_a, to_side, *keep_a)
    sum_f, sum_b = tie((sum_f, sum_b, own_a))[:2]
    source_grad, gain_e0, shift_e0 = norm_back_rows(
        x_source, own_a, other_a, enc(0)[0], d_hidden, [BF16]
    )
    own_c = pin(own_c, source_grad)
    target_grad, gain_d0, shift_d0 = norm_back_rows(
        x_target, own_c, other_c, dec(0)[0], d_self, [BF16]
    )
    gain_d0, line_a = here(gain_d0, to_line, side_a)
    source_grad = chip.from_slot(pin(source_grad, gain_d0))
    target_grad = chip.from_slot(pin(target_grad, gain_d0))
    line_a, sum_xc = tie((line_a, sum_xc))

    norms = jnp.concatenate(
        [
            gain_e0,
            gain_e1,
            gain_e2,
            shift_e0,
            shift_e1,
            shift_e2,
            gain_d0,
            gain_d1,
            gain_d2,
            gain_d3,
            shift_d0,
            shift_d1,
            shift_d2,
            shift_d3,
        ],
        0,
    )
    part = norms.shape[1] // 2
    norms = lax.dynamic_slice_in_dim(norms, core * part, part, 1)
    norms = norms + chip.send_near(norms)
    norms = norms + chip.send_side(norms)
    norms = norms + chip.along(norms, 1)
    norms = norms + chip.along(norms, 2)
    line_a = from_line(*line_a)[:2]
    line_a = to_core(*line_a)

    def wide(block, blocks):
        cores, rows, width = block.shape
        block = block.reshape(cores, blocks, rows // blocks, width)
        return jnp.transpose(block, (3, 1, 0, 2)).reshape(width, blocks, -1).astype(F32)

    def tall(block):
        return block.reshape(-1, block.shape[2]).astype(F32)

    n = proj_rows
    done_f, done_b = in_place(*share(sum_f)), in_place(*share(sum_b))
    done_xc, done_a = in_place(*share(sum_xc)), in_place(*line_a)
    done_x, done_c = done_xc[:, : 4 * n], done_xc[:, 4 * n :]
    source_grad, target_grad = source_grad.astype(F32), target_grad.astype(F32)
    hid = done_f.shape[1] // 2
    return (
        decoded,
        source_grad,
        target_grad,
        norms[0:3],
        norms[3:6],
        wide(done_a[:, n:], 3),
        tall(done_a[:, :n]),
        wide(done_b[:, inner:], 1)[:, 0],
        tall(done_b[:, :inner]),
        norms[6:10],
        norms[10:14],
        wide(done_c[:, n:], 3),
        tall(done_c[:, :n]),
        wide(done_x[:, n : n + head_width], 1)[:, 0],
        wide(done_x[:, n + head_width :], 2),
        tall(done_x[:, :n]),
        wide(done_f[:, hid:], 1)[:, 0],
        tall(done_f[:, :hid]),
    )


def solution(mesh):
    rows = P("dp", ("seq", "tensor"), None)
    segments = P("dp", None)
    shape = dict(mesh.shape)
    chips = shape["dp"] == 4 and shape["seq"] == 2 and shape["tensor"] == 4
    return jax.shard_map(
        chip_local if chips else local,
        mesh=mesh,
        in_specs=(
            rows,
            rows,
            rows,
            segments,
            segments,
            P(),
            P(),
            P(None, None, "tensor"),
            P("tensor", None),
            P(None, "tensor"),
            P("tensor", None),
            P(),
            P(),
            P(None, None, "tensor"),
            P("tensor", None),
            P(None, "tensor"),
            P(None, None, "tensor"),
            P("tensor", None),
            P(None, "tensor"),
            P("tensor", None),
        ),
        out_specs=(
            rows,
            rows,
            rows,
            P(None, "seq"),
            P(None, "seq"),
            P("seq", None, "tensor"),
            P("tensor", "seq"),
            P("seq", "tensor"),
            P("tensor", "seq"),
            P(None, "seq"),
            P(None, "seq"),
            P("seq", None, "tensor"),
            P("tensor", "seq"),
            P("seq", "tensor"),
            P("seq", None, "tensor"),
            P("tensor", "seq"),
            P("seq", "tensor"),
            P("tensor", "seq"),
        ),
        check_vma=False,
    )
```
